32 devices in a mesh: grp: 2 (over x), lon: 16 (over z, y, core).
Axes of the slice: x: 2, y: 2, z: 4, core: 2. Of those that a mesh axis runs over, the one named last changes fastest.
Arguments:
- control: float32 [32, 512, 512], P('grp', 'lon'), parts along dimension 0, may hold values from -6 to 6
- std_field: float32 [16, 512, 512], P(None, 'lon'), may hold values from 0.5 to 2
- kappa_lon: float32 [512, 512], P('lon'), may hold values from 0.18 to 0.245
- kappa_lat: float32 [512, 512], P('lon'), may hold values from 0.18 to 0.245
- sea_mask: int32 [512, 512], P('lon'), may hold values 0 or 1
- vertical: float32 [16, 16], replicated, may hold values from -1.5 to 1.5
- block_index: int32 [32, 16, 8], P(('grp', 'lon')), parts along dimension 0, may hold values from 0 to 2047, as said below
- weights: float32 [32, 16, 8, 128], P(('grp', 'lon')), parts along dimension 0, may hold values from -1 to 1
- obs_value: float32 [32, 16, 8], P(('grp', 'lon')), parts along dimension 0, may hold values from -6 to 6
- obs_rinv: float32 [32, 16, 8], P(('grp', 'lon')), parts along dimension 0, may hold values from 0.5 to 4
- obs_count: int32 [32, 16], P(('grp', 'lon')), parts along dimension 0, may hold values from 0 to 8, as said below
Outputs:
- gradient: float32 [32, 512, 512], P('grp', 'lon'), parts along dimension 0
- departure: float32 [32, 16, 8], P(('grp', 'lon')), parts along dimension 0
The draws below stay inside these ranges and needn't reach their ends.
There are 2 independent parts, one for each index of `grp`. The reference program is written for one: setup_inputs(seed, part) draws one part's arguments, and reference() takes and returns one part's arrays. A program takes and returns all parts, laid end to end along the dimension named above; an argument that names none is the same for every part. Nothing has to cross between parts.
Inputs may be any that keep to these rules, and one draw needn't show every extreme that they name: Slot c of owner p for tile t holds an observation exactly when c < obs_count[p, t]; in every draw one tile has 8 observations from every owner. `block_index`: each slot names one stencil block of its tile.
All inputs are finite; a program needn't handle non-finite values. No bound on the sum of `sea_mask` on one device may be relied on, other than what follows from the above.
Results may differ from the reference program's by a relative error of at most 0.000067.
Values sent between devices are 32-bit elements; how exact they have to be, the bound alone decides.
No kernel may reach another device: no remote copies, remote signals or barrier semaphores. Data moves between devices by JAX's collectives and lax.ppermute only.
A program may use at most 64 MiB of HBM per device.

```python
import math
import jax
import jax.numpy as jnp
from jax import lax

VL = 16
CLON = 32
LAT = 512
STEN = 128
CAP = 8
PASSES = 10
NLON = 512
OWNERS = 16
NSEG = 4
NBLK = 2048


def draw_obs_count(key, part):
    key = jax.random.fold_in(key, 7)
    first, second, third = jax.random.split(key, 3)
    level = jax.random.randint(first, (OWNERS,), 0, 4)
    base = jax.random.randint(second, (OWNERS, OWNERS), 0, CAP + 1)
    counts = jnp.minimum(CAP, base * (1 + level)[None, :] // 2)
    full_tile = jax.random.randint(third, (), 0, OWNERS)
    columns = jnp.arange(OWNERS)[None, :] + jnp.zeros((OWNERS, OWNERS), jnp.int32)
    counts = jnp.where(columns == full_tile, CAP, counts)
    return counts.astype(jnp.int32)


def draw_block_index(key, part):
    key = jax.random.fold_in(key, 11)
    first, second, third, fourth, fifth = jax.random.split(key, 5)
    shape = (OWNERS, OWNERS, CAP)
    level = jax.random.randint(first, shape, 0, VL)
    segment = jax.random.randint(second, shape, 0, NSEG)
    side = jax.random.randint(third, shape, 0, 2)
    inner = jax.random.randint(fourth, shape, 0, CLON)
    edge_pick = jax.random.randint(fifth, shape, 0, 2)
    column = jnp.where(edge_pick == 0, side * (CLON - 1), inner)
    index = (level * CLON + column) * NSEG + segment
    position = jnp.arange(OWNERS * OWNERS * CAP, dtype=jnp.int32).reshape(shape)
    index = jnp.where(position == 0, NBLK - 1, index)
    index = jnp.where(position == 1, 0, index)
    return index.astype(jnp.int32)


def with_ends(result, own_key, least, largest):
    longest = result.shape.index(max(result.shape))
    spots = []
    for shift in (0, 1):
        where = [jax.random.randint(jax.random.fold_in(own_key, axis), (), 0, length) for axis, length in enumerate(result.shape)]
        where[longest] = (where[longest] + shift) % result.shape[longest]
        spots.append(tuple(where))
    return result.at[spots[0]].set(least).at[spots[1]].set(largest)


def block_levels(rng, shape, cuts, smallest, largest):
    def one(dim, shards_of):
        heights = jax.random.uniform(jax.random.fold_in(jax.random.fold_in(rng, 6), dim), (shards_of,), jnp.float32, smallest / len(cuts), largest / len(cuts))
        return jnp.repeat(jnp.exp(heights), shape[dim] // shards_of).reshape((-1,) + (1,) * (len(shape) - dim - 1))

    level = one(*cuts[0])
    for cut in cuts[1:]:
        level = level * one(*cut)
    return level


def scatter_about(own_key, shape, deviation, limit, cuts=(), kind=jnp.bfloat16):
    gain = block_levels(own_key, shape, cuts, -0.22, 0.18) if cuts else 1.0
    entries = jax.random.normal(own_key, shape, jnp.float32) * deviation * gain
    return jnp.minimum(jnp.maximum(entries, -limit), limit).astype(kind)


def setup_inputs(seed: int = 0, part: int = 0) -> dict:
    splits = jax.random.split(jax.random.key(seed), 12)
    own_keys = jax.random.split(jax.random.fold_in(splits[11], part), 12)
    control = scatter_about(own_keys[0], (VL, NLON, LAT), 1.0, 6.0, ((1, 16),), jnp.float32)
    std_field = jnp.clip(jnp.exp(math.log(2.0) - 1.3862944 * jax.random.uniform(splits[1], (VL, NLON, LAT), jnp.float32) ** block_levels(splits[1], (VL, NLON, LAT), ((1, 16),), -0.2, 0.2)), 0.5, 2.0)
    kappa_lon = jnp.clip(0.18 + 0.065 * jax.random.uniform(splits[2], (NLON, LAT), jnp.float32) ** block_levels(splits[2], (NLON, LAT), ((0, 16),), -0.2, 0.2), 0.18, 0.245)
    kappa_lat = jnp.clip(0.18 + 0.065 * jax.random.uniform(splits[3], (NLON, LAT), jnp.float32) ** block_levels(splits[3], (NLON, LAT), ((0, 16),), -0.2, 0.2), 0.18, 0.245)
    sea_mask = with_ends((jax.random.randint(splits[4], (NLON, LAT), 0, 100) < 99).astype(jnp.int32), jax.random.fold_in(splits[4], 1), 0, 1)
    vertical = scatter_about(splits[5], (VL, VL), VL ** -0.5, 1.5, (), jnp.float32)
    block_index = draw_block_index(jax.random.fold_in(jax.random.fold_in(splits[11], part), 71), part)
    weights = scatter_about(own_keys[7], (OWNERS, OWNERS, CAP, STEN), 32 ** -0.5, 1.0, ((0, 16),), jnp.float32)
    obs_value = scatter_about(own_keys[8], (OWNERS, OWNERS, CAP), 1.0, 6.0, ((0, 16),), jnp.float32)
    obs_rinv = jnp.clip(jnp.exp(math.log(4.0) - 2.0794415 * jax.random.uniform(own_keys[9], (OWNERS, OWNERS, CAP), jnp.float32) ** block_levels(own_keys[9], (OWNERS, OWNERS, CAP), ((0, 16),), -0.2, 0.2)), 0.5, 4.0)
    obs_count = draw_obs_count(jax.random.fold_in(jax.random.fold_in(splits[11], part), 71), part)
    return {"control": control, "std_field": std_field, "kappa_lon": kappa_lon, "kappa_lat": kappa_lat, "sea_mask": sea_mask, "vertical": vertical, "block_index": block_index, "weights": weights, "obs_value": obs_value, "obs_rinv": obs_rinv, "obs_count": obs_count}


def mix_levels(matrix, field):
    return jnp.einsum("ab,bxy->axy", matrix, field, precision=lax.Precision.HIGHEST)


def smooth_step(field, face_lon, face_lat):
    flux_lon = face_lon[None] * (jnp.roll(field, -1, 1) - field)
    flux_lat = face_lat[None] * (field[:, :, 1:] - field[:, :, :-1])
    padded = jnp.pad(flux_lat, ((0, 0), (0, 0), (1, 1)))
    return field + (flux_lon - jnp.roll(flux_lon, 1, 1)) + (padded[:, :, 1:] - padded[:, :, :-1])


def diffuse(field, face_lon, face_lat):
    for turn in range(PASSES):
        field = smooth_step(field, face_lon, face_lat)
    return field


def reference(control, std_field, kappa_lon, kappa_lat, sea_mask, vertical, block_index, weights, obs_value, obs_rinv, obs_count):
    wet = sea_mask.astype(jnp.float32)
    face_lon = kappa_lon * wet * jnp.roll(wet, -1, 0)
    face_lat = kappa_lat[:, :-1] * wet[:, :-1] * wet[:, 1:]
    mixed = mix_levels(vertical, control)
    state = wet[None] * std_field * diffuse(mixed, face_lon, face_lat)
    blocks_all = state.reshape(VL, OWNERS, CLON, NSEG, STEN).transpose(1, 0, 2, 3, 4).reshape(OWNERS, NBLK, STEN)
    tile_ids = jnp.arange(OWNERS, dtype=jnp.int32)[None, :, None] + jnp.zeros_like(block_index)
    values = blocks_all[tile_ids, block_index]
    evolved = jnp.sum(values * weights, axis=-1)
    valid = jnp.arange(CAP, dtype=jnp.int32)[None, None, :] < obs_count[:, :, None]
    departure = jnp.where(valid, evolved - obs_value, jnp.float32(0.0))
    scaled = obs_rinv * departure
    spread = scaled[..., None] * weights
    adjoint_blocks = jnp.zeros((OWNERS, NBLK, STEN), jnp.float32).at[tile_ids, block_index].add(spread)
    adjoint_state = adjoint_blocks.reshape(OWNERS, VL, CLON, NSEG, STEN).transpose(1, 0, 2, 3, 4).reshape(VL, NLON, LAT)
    weighted = wet[None] * std_field * adjoint_state
    gradient = control + mix_levels(vertical.T, diffuse(weighted, face_lon, face_lat))
    return gradient, departure
```

```python
import jax
import jax.numpy as jnp
from jax import lax
from jax.experimental import pallas as pl
from jax.experimental.pallas import tpu as pltpu
from jax.sharding import PartitionSpec as P

STEN = 128
PASSES = 10
WIDE = 256
F32 = jnp.float32
BF16 = jnp.bfloat16
VMEM_LIMIT = 40 * 1024 * 1024

VMEM_SPEC = pl.BlockSpec(memory_space=pltpu.VMEM)
SMEM_SPEC = pl.BlockSpec(memory_space=pltpu.SMEM)


def split(x):
    high = x.astype(BF16)
    return high, (x - high.astype(F32)).astype(BF16)


def dot(a, b):
    return jnp.dot(a, b, preferred_element_type=F32)


def iota(shape, dim):
    return lax.broadcasted_iota(jnp.int32, shape, dim)


def onehot(condition):
    return jnp.where(condition, F32(1.0), F32(0.0)).astype(BF16)


def product(left, right):
    (lh, ll), (rh, rl) = left, right
    return dot(lh, rh) + (dot(lh, rl) + dot(ll, rh))


def mixing_matrix(vertical):
    levels = vertical.shape[0]
    group = WIDE // levels
    expand = onehot(iota((levels, WIDE), 1) // group == iota((levels, WIDE), 0))
    keep = iota((WIDE, WIDE), 0) // levels == iota((WIDE, WIDE), 1) % group
    out = []
    for part in split(vertical):
        rows = dot(part, expand)
        tiled = jnp.concatenate([rows] * group, axis=0)
        out.append(jnp.where(keep, tiled, F32(0.0)).astype(BF16))
    return tuple(out)


def mixing_matrix_back(vertical_t):
    levels = vertical_t.shape[0]
    group = WIDE // levels
    spread = onehot(iota((levels, WIDE), 1) % levels == iota((levels, WIDE), 0))
    repeat = onehot(iota((WIDE, levels), 0) // group == iota((WIDE, levels), 1))
    keep = iota((WIDE, WIDE), 0) % group == iota((WIDE, WIDE), 1) // levels
    out = []
    for part in split(vertical_t):
        rows = dot(part, spread).astype(BF16)
        out.append(jnp.where(keep, dot(repeat, rows), F32(0.0)).astype(BF16))
    return tuple(out)


def head_kernel(v_ref, control_ref, klon_ref, klat_ref, mask_ref, mixed_ref, faces_ref, left_ref, right_ref):
    levels, cols, lat = control_ref.shape
    group = WIDE // levels
    wet = mask_ref[...].astype(F32)
    east = jnp.where(iota((cols, lat), 0) == cols - 1, F32(1.0), pltpu.roll(wet, cols - 1, 0))
    north = jnp.where(iota((cols, lat), 1) == lat - 1, F32(0.0), pltpu.roll(wet, lat - 1, 1))
    faces_ref[0] = klon_ref[...] * wet * east
    faces_ref[1] = klat_ref[...] * wet * north
    matrix = mixing_matrix(v_ref[...])
    for g in range(cols // group):
        x = control_ref[:, g * group : (g + 1) * group, :].reshape(WIDE, lat)
        y = product(matrix, split(x))
        mixed_ref[g * group : (g + 1) * group] = y.reshape(group, levels, lat)
    halo = PASSES
    for out, start in ((left_ref, 0), (right_ref, cols - halo)):
        out[0:halo] = mixed_ref[start : start + halo]
        for k in range(2):
            out[halo + k, 0:halo, :] = faces_ref[k, start : start + halo, :]
            out[halo + k, halo:levels, :] = jnp.zeros((levels - halo, lat), F32)
        out[halo, halo : halo + 1, :] = wet[0:1]


def build_faces(faces_ref, mask_ref, from_left, from_right, lon_ref, lat_ref):
    halo = PASSES
    cols = faces_ref.shape[1]
    shape = lon_ref.shape[1:]
    for c in range(cols + 2 * halo):
        if c < halo:
            lon_row = from_left[halo, c : c + 1, :]
            lat_row = from_left[halo + 1, c : c + 1, :]
            if c == halo - 1:
                lon_row = lon_row * mask_ref[0:1, :].astype(F32)
        elif c < halo + cols:
            own = c - halo
            lon_row = faces_ref[0, own : own + 1, :]
            lat_row = faces_ref[1, own : own + 1, :]
            if own == cols - 1:
                lon_row = lon_row * from_right[halo, halo : halo + 1, :]
        else:
            far = c - halo - cols
            lon_row = from_right[halo, far : far + 1, :]
            lat_row = from_right[halo + 1, far : far + 1, :]
        lon_ref[c] = jnp.broadcast_to(lon_row, shape)
        lat_ref[c] = jnp.broadcast_to(lat_row, shape)


def one_pass(src, dst, lon_ref, lat_ref, low, high):
    levels, lat = src.shape[1:]
    half = lon_ref.shape[1]
    for h in range(levels // half):
        rows = slice(h * half, (h + 1) * half)
        here = src[low, rows, :]
        flux_west = lon_ref[low - 1] * (here - src[low - 1, rows, :])
        for c in range(low, high):
            east = src[c + 1, rows, :]
            flux_east = lon_ref[c] * (east - here)
            flux_north = lat_ref[c] * (pltpu.roll(here, lat - 1, 1) - here)
            flux_south = pltpu.roll(flux_north, 1, 1)
            dst[c, rows, :] = here + (flux_east - flux_west) + (flux_north - flux_south)
            here, flux_west = east, flux_east


def diffuse(a_ref, b_ref, lon_ref, lat_ref):
    width = a_ref.shape[0]

    def pair(turn, carry):
        one_pass(a_ref, b_ref, lon_ref, lat_ref, 1, width - 1)
        one_pass(b_ref, a_ref, lon_ref, lat_ref, 2, width - 2)
        return carry

    lax.fori_loop(0, PASSES // 2, pair, 0)


def block_place(index, cols, segs):
    return index // (cols * segs), (index // segs) % cols, index % segs


def weights_kernel(index_ref, recv_ref, std_ref, mask_ref, out_ref, pick_ref, std_rows, wet_rows):
    owners, rows, _ = recv_ref.shape
    slots = rows // 2
    levels, cols, lat = std_ref.shape
    segs = lat // STEN
    for s in range(segs):
        part = slice(s * STEN, (s + 1) * STEN)
        wet_rows[s * cols : (s + 1) * cols, :] = mask_ref[:, part].astype(F32)
        for a in range(levels):
            first = (a * segs + s) * cols
            std_rows[first : first + cols, :] = std_ref[a, :, part]

    def pick(o, carry):
        for k in range(slots):
            slot = o * slots + k
            level, column, seg = block_place(index_ref[slot], cols, segs)
            value = std_rows[pl.ds((level * segs + seg) * cols + column, 1), :]
            wet = wet_rows[pl.ds(seg * cols + column, 1), :]
            pick_ref[pl.ds(slot, 1), :] = value * wet
        return carry

    lax.fori_loop(0, owners, pick, 0)
    out_ref[...] = recv_ref[:, 0:slots, :].reshape(owners * slots, STEN) * pick_ref[...]


def to_row(column):
    eye = iota((STEN, STEN), 0) == iota((STEN, STEN), 1)
    return jnp.sum(jnp.where(eye, column, F32(0.0)), axis=0, keepdims=True)


def first_kernel(
    index_ref, mixed_ref, from_left, from_right, faces_ref, mask_ref, recv_ref, ws_ref,
    spread_ref, departure_ref, a_ref, b_ref, lon_ref, lat_ref, rows_ref, pick_ref,
):
    halo = PASSES
    cols, levels, lat = mixed_ref.shape
    segs = lat // STEN
    owners, rows, _ = recv_ref.shape
    slots = rows // 2
    total = owners * slots
    build_faces(faces_ref, mask_ref, from_left, from_right, lon_ref, lat_ref)
    a_ref[0:halo] = from_left[0:halo]
    a_ref[halo : halo + cols] = mixed_ref[...]
    a_ref[halo + cols : 2 * halo + cols] = from_right[0:halo]
    diffuse(a_ref, b_ref, lon_ref, lat_ref)
    for c in range(cols):
        for s in range(segs):
            first = (c * segs + s) * levels
            rows_ref[first : first + levels, :] = a_ref[halo + c, :, s * STEN : (s + 1) * STEN]

    def pick(o, carry):
        for k in range(slots):
            slot = o * slots + k
            level, column, seg = block_place(index_ref[slot], cols, segs)
            pick_ref[pl.ds(slot, 1), :] = rows_ref[pl.ds((column * segs + seg) * levels + level, 1), :]
        return carry

    lax.fori_loop(0, owners, pick, 0)
    ws = ws_ref[...]
    meta = recv_ref[:, slots:, :].reshape(total, STEN)
    evolved = jnp.sum(pick_ref[...] * ws, axis=1, keepdims=True)
    departure = jnp.where(meta[:, 3:4] > 0.5, evolved - meta[:, 0:1], F32(0.0))
    scaled = meta[:, 1:2] * departure
    spread_ref[0:total, :] = scaled * ws
    spread_ref[total:, :] = jnp.zeros((spread_ref.shape[0] - total, STEN), F32)
    for j in range(total // STEN):
        part = slice(j * STEN, (j + 1) * STEN)
        departure_ref[j : j + 1, :] = to_row(departure[part])
        spread_ref[total + j : total + j + 1, :] = to_row(meta[part, 2:3])


def second_kernel(
    vt_ref, control_ref, own_ref, left_ref, right_ref, faces_ref, mask_ref, from_left, from_right,
    out_ref, a_ref, b_ref, lon_ref, lat_ref,
):
    halo = PASSES
    levels, cols, lat = control_ref.shape
    segs = lat // STEN
    rows = segs * levels
    total = own_ref.shape[0] // STEN * STEN
    build_faces(faces_ref, mask_ref, from_left, from_right, lon_ref, lat_ref)

    def scatter(source, first, count, place):
        keys = source[total : total + total // STEN, :].astype(jnp.int32)
        keys = (keys % (cols * segs)) * levels + keys // (cols * segs) - first * rows
        pieces = [jnp.concatenate(split(source[j * STEN : (j + 1) * STEN, :]), axis=1) for j in range(total // STEN)]
        for c in range(count):
            sums = jnp.zeros((rows, 2 * STEN), F32)
            for j, piece in enumerate(pieces):
                hit = iota((rows, STEN), 0) + c * rows == keys[j : j + 1, :]
                sums = sums + dot(onehot(hit), piece)
            sums = sums[:, :STEN] + sums[:, STEN:]
            for s in range(segs):
                a_ref[place + c, :, s * STEN : (s + 1) * STEN] = sums[s * levels : (s + 1) * levels]

    scatter(own_ref, 0, cols, halo)
    scatter(left_ref, cols - halo, halo, 0)
    scatter(right_ref, 0, halo, halo + cols)
    diffuse(a_ref, b_ref, lon_ref, lat_ref)
    matrix = mixing_matrix_back(vt_ref[...])
    group = WIDE // levels
    for g in range(cols // group):
        part = slice(g * group, (g + 1) * group)
        x = a_ref[halo + g * group : halo + (g + 1) * group].reshape(WIDE, lat)
        y = product(matrix, split(x)).reshape(levels, group, lat)
        out_ref[:, part, :] = control_ref[:, part, :] + y


def call(kernel, out_shape, specs, scratch=()):
    return pl.pallas_call(
        kernel,
        out_shape=out_shape,
        in_specs=specs,
        out_specs=jax.tree.map(lambda _: VMEM_SPEC, out_shape),
        scratch_shapes=list(scratch),
        compiler_params=pltpu.CompilerParams(vmem_limit_bytes=VMEM_LIMIT),
    )


def shape(*dims):
    return jax.ShapeDtypeStruct(dims, F32)


def local(
    control, std_field, kappa_lon, kappa_lat, sea_mask, vertical,
    block_index, weights, obs_value, obs_rinv, obs_count,
):
    levels, cols, lat = control.shape
    owners, slots = block_index.shape[1:]
    total = owners * slots
    halo = PASSES
    width = cols + 2 * halo
    count = lax.axis_size("lon")
    to_right = [(i, (i + 1) % count) for i in range(count)]
    to_left = [((i + 1) % count, i) for i in range(count)]

    valid = jnp.arange(slots, dtype=jnp.int32)[None, :] < obs_count[0][:, None]
    meta = jnp.stack(
        [obs_value[0], obs_rinv[0], block_index[0].astype(F32), valid.astype(F32)], axis=-1
    )
    meta = jnp.pad(meta, ((0, 0), (0, 0), (0, STEN - 4)))
    sent = jnp.concatenate([weights[0], meta], axis=1)

    mixed, faces, edge_left, edge_right = call(
        head_kernel,
        (shape(cols, levels, lat), shape(2, cols, lat), shape(halo + 2, levels, lat), shape(halo + 2, levels, lat)),
        [VMEM_SPEC] * 5,
    )(vertical, control, kappa_lon, kappa_lat, sea_mask)
    from_left = lax.ppermute(edge_right, "lon", to_right)
    from_right = lax.ppermute(edge_left, "lon", to_left)

    recv = lax.all_to_all(sent, "lon", split_axis=0, concat_axis=0, tiled=True)
    index = recv[:, slots:, 2].reshape(total).astype(jnp.int32)
    picked = pltpu.VMEM((total, STEN), F32)
    blocks = pltpu.VMEM((levels * cols * lat // STEN, STEN), F32)
    ws = call(
        weights_kernel, shape(total, STEN), [SMEM_SPEC] + [VMEM_SPEC] * 3, [picked, blocks, pltpu.VMEM((cols * lat // STEN, STEN), F32)]
    )(index, recv, std_field, sea_mask)

    field = pltpu.VMEM((width, levels, lat), F32)
    face = pltpu.VMEM((width, 8, lat), F32)
    extra = -(-total // (8 * STEN)) * 8
    spread, departure = call(
        first_kernel,
        (shape(total + extra, STEN), shape(total // STEN, STEN)),
        [SMEM_SPEC] + [VMEM_SPEC] * 7,
        [field, field, face, face, blocks, picked],
    )(index, mixed, from_left, from_right, faces, sea_mask, recv, ws)

    spread_left = lax.ppermute(spread, "lon", to_right)
    spread_right = lax.ppermute(spread, "lon", to_left)
    everyone = lax.all_gather(departure, "lon").reshape(count, owners, slots)
    mine = lax.dynamic_index_in_dim(everyone, lax.axis_index("lon"), axis=1, keepdims=False)

    gradient = call(
        second_kernel, shape(levels, cols, lat), [VMEM_SPEC] * 9, [field, field, face, face]
    )(vertical.T, control, spread, spread_left, spread_right, faces, sea_mask, from_left, from_right)
    return gradient, mine[None]


def solution(mesh):
    in_specs = (
        P("grp", "lon", None),
        P(None, "lon", None),
        P("lon", None),
        P("lon", None),
        P("lon", None),
        P(),
        P(("grp", "lon"), None, None),
        P(("grp", "lon"), None, None, None),
        P(("grp", "lon"), None, None),
        P(("grp", "lon"), None, None),
        P(("grp", "lon"), None),
    )
    out_specs = (P("grp", "lon", None), P(("grp", "lon"), None, None))
    return jax.shard_map(local, mesh=mesh, in_specs=in_specs, out_specs=out_specs, check_vma=False)
```

```python
import jax
import jax.numpy as jnp
from jax import lax
from jax.experimental import pallas as pl
from jax.experimental.pallas import tpu as pltpu
from jax.sharding import PartitionSpec as P

STEN = 128
PASSES = 10
WIDE = 256
F32 = jnp.float32
BF16 = jnp.bfloat16
VMEM_LIMIT = 40 * 1024 * 1024

VMEM_SPEC = pl.BlockSpec(memory_space=pltpu.VMEM)
SMEM_SPEC = pl.BlockSpec(memory_space=pltpu.SMEM)


def split(x):
    high = x.astype(BF16)
    return high, (x - high.astype(F32)).astype(BF16)


def split3(x):
    high = x.astype(BF16)
    rest = x - high.astype(F32)
    middle = rest.astype(BF16)
    return high, middle, (rest - middle.astype(F32)).astype(BF16)


def dot(a, b):
    return jnp.dot(a, b, preferred_element_type=F32)


def log2(n):
    assert n & (n - 1) == 0
    return n.bit_length() - 1


def iota(shape, dim):
    return lax.broadcasted_iota(jnp.int32, shape, dim)


def onehot(condition):
    return jnp.where(condition, F32(1.0), F32(0.0)).astype(BF16)


def product(left, right):
    (lh, ll), (rh, rl) = left, right
    return dot(lh, rh) + (dot(lh, rl) + dot(ll, rh))


def mixing_matrix(vertical):
    levels = vertical.shape[0]
    group = WIDE // levels
    expand = onehot(iota((levels, WIDE), 1) // group == iota((levels, WIDE), 0))
    keep = iota((WIDE, WIDE), 0) // levels == iota((WIDE, WIDE), 1) % group
    out = []
    for part in split(vertical):
        rows = dot(part, expand)
        tiled = jnp.concatenate([rows] * group, axis=0)
        out.append(jnp.where(keep, tiled, F32(0.0)).astype(BF16))
    return tuple(out)


def mixing_matrix_back(vertical_t):
    levels = vertical_t.shape[0]
    group = WIDE // levels
    spread = onehot(iota((levels, WIDE), 1) % levels == iota((levels, WIDE), 0))
    repeat = onehot(iota((WIDE, levels), 0) // group == iota((WIDE, levels), 1))
    keep = iota((WIDE, WIDE), 0) % group == iota((WIDE, WIDE), 1) // levels
    out = []
    for part in split(vertical_t):
        rows = dot(part, spread).astype(BF16)
        out.append(jnp.where(keep, dot(repeat, rows), F32(0.0)).astype(BF16))
    return tuple(out)


def deinterleave(lat):
    parts = lat // STEN
    target = iota((lat, lat), 1)
    return onehot(iota((lat, lat), 0) == (target % STEN) * parts + target // STEN)


def interleave(lat):
    parts = lat // STEN
    source = iota((lat, lat), 0)
    return onehot(iota((lat, lat), 1) == (source % STEN) * parts + source // STEN)


def spread_block(lat):
    parts = lat // STEN
    target = iota((STEN, lat), 1)
    return onehot(iota((STEN, lat), 0) == (target % (STEN // parts)) * parts + target // STEN)


def lane_segment(rows, lat):
    parts = lat // STEN
    return (iota((rows, lat), 1) % STEN) // (STEN // parts)


def move(x, matrix):
    return tuple(dot(part, matrix).astype(BF16) for part in x)


def head_kernel(
    v_ref, control_hbm, klon_hbm, klat_hbm, mask_hbm, mixed_ref, faces_ref, left_ref, right_ref,
    control_ref, klon_ref, klat_ref, mask_ref, sems,
):
    copies = [
        pltpu.make_async_copy(source, target, sems.at[k])
        for k, (source, target) in enumerate(
            ((mask_hbm, mask_ref), (klon_hbm, klon_ref), (klat_hbm, klat_ref), (control_hbm, control_ref))
        )
    ]
    for copy in copies:
        copy.start()
    levels, cols, lat = control_ref.shape
    parts = lat // STEN
    group = WIDE // levels
    halo = PASSES
    edge = halo * levels
    place = deinterleave(lat)
    matrix = mixing_matrix(v_ref[...])
    for copy in copies[:3]:
        copy.wait()
    wet = mask_ref[...].astype(F32)
    east = jnp.where(iota((cols, lat), 0) == cols - 1, F32(1.0), pltpu.roll(wet, cols - 1, 0))
    north = jnp.where(iota((cols, lat), 1) == lat - 1, F32(0.0), pltpu.roll(wet, lat - 1, 1))
    for k, face in enumerate((klon_ref[...] * wet * east, klat_ref[...] * wet * north, wet)):
        held = sum(dot(piece, place) for piece in (split3(face) if k < 2 else (face.astype(BF16),)))
        for q in range(parts):
            faces_ref[k * parts + q] = held[:, q * STEN : (q + 1) * STEN]
    copies[3].wait()
    for g in range(cols // group):
        x = control_ref[:, g * group : (g + 1) * group, :].reshape(WIDE, lat)
        y = product(matrix, move(split(x), place))
        for q in range(parts):
            mixed_ref[q, g * WIDE : (g + 1) * WIDE, :] = y[:, q * STEN : (q + 1) * STEN]
    for out, start in ((left_ref, 0), (right_ref, cols - halo)):
        for q in range(parts):
            out[q * edge : (q + 1) * edge, :] = mixed_ref[q, start * levels : start * levels + edge, :]
        for k in range(2 * parts):
            first = parts * edge + k * halo
            out[first : first + halo, :] = faces_ref[k, start : start + halo, :]
        first = parts * edge + 2 * parts * halo
        for q in range(parts):
            out[first + q : first + q + 1, :] = faces_ref[2 * parts + q, 0:1, :]
        out[first + parts :, :] = jnp.zeros((out.shape[0] - first - parts, STEN), F32)


def build_faces(faces_ref, from_left, from_right, lon_ref, lat_ref, levels):
    halo = PASSES
    cols = faces_ref.shape[1]
    parts = faces_ref.shape[0] // 3
    first = parts * halo * levels
    shape = (8, STEN)

    def far(source, k, c):
        at = first + k * halo + c
        return source[at : at + 1, :]

    for c in range(cols + 2 * halo):
        rows = slice(8 * c, 8 * c + 8)
        for q in range(parts):
            if c < halo:
                lon_row, lat_row = far(from_left, q, c), far(from_left, parts + q, c)
                if c == halo - 1:
                    lon_row = lon_row * faces_ref[2 * parts + q, 0:1, :]
            elif c < halo + cols:
                own = c - halo
                lon_row = faces_ref[q, own : own + 1, :]
                lat_row = faces_ref[parts + q, own : own + 1, :]
                if own == cols - 1:
                    at = first + 2 * parts * halo + q
                    lon_row = lon_row * from_right[at : at + 1, :]
            else:
                own = c - halo - cols
                lon_row, lat_row = far(from_right, q, own), far(from_right, parts + q, own)
            lon_ref[q, rows, :] = jnp.broadcast_to(lon_row, shape)
            lat_ref[q, rows, :] = jnp.broadcast_to(lat_row, shape)
            if q == parts - 1:
                lat_ref[parts, rows, :] = jnp.broadcast_to(pltpu.roll(lat_row, 1, 1), shape)


def add_ghosts(ref, first, values):
    count = values[0].shape[0]
    parts = len(values)
    ref[parts, first : first + count, :] = pltpu.roll(values[0], STEN - 1, 1)
    ref[parts + 1, first : first + count, :] = pltpu.roll(values[-1], 1, 1)


def fill(ref, first, values):
    for q, value in enumerate(values):
        ref[q, first : first + value.shape[0], :] = value
    add_ghosts(ref, first, values)


def one_pass(src, dst, lon_ref, lat_ref, levels, low, high):
    parts = lon_ref.shape[0]
    halves = range(levels // 8)

    def load(k, c, h):
        return src[k, c * levels + 8 * h : c * levels + 8 * h + 8, :]

    def face(ref, k, c):
        return ref[k, 8 * c : 8 * c + 8, :]

    here = [[load(q, low, h) for q in range(parts)] for h in halves]
    west = [[face(lon_ref, q, low - 1) * (here[h][q] - load(q, low - 1, h)) for q in range(parts)] for h in halves]
    for c in range(low, high):
        lon = [face(lon_ref, q, c) for q in range(parts)]
        lat = [face(lat_ref, q, c) for q in range(parts + 1)]
        for h in halves:
            line = here[h]
            east = [load(q, c + 1, h) for q in range(parts)]
            flux_east = [lon[q] * (east[q] - line[q]) for q in range(parts)]
            ahead = line[1:] + [load(parts, c, h)]
            flux_north = [lat[parts] * (line[0] - load(parts + 1, c, h))]
            flux_north += [lat[q] * (ahead[q] - line[q]) for q in range(parts)]
            out = [
                line[q] + (flux_east[q] - west[h][q]) + (flux_north[q + 1] - flux_north[q])
                for q in range(parts)
            ]
            first = c * levels + 8 * h
            for q in range(parts):
                dst[q, first : first + 8, :] = out[q]
            add_ghosts(dst, first, out)
            here[h], west[h] = east, flux_east


def diffuse(a_ref, b_ref, lon_ref, lat_ref, levels):
    width = a_ref.shape[1] // levels

    def pair(turn, carry):
        one_pass(a_ref, b_ref, lon_ref, lat_ref, levels, 1, width - 1)
        one_pass(b_ref, a_ref, lon_ref, lat_ref, levels, 2, width - 2)
        return carry

    lax.fori_loop(0, PASSES // 2, pair, 0)


def block_place(index, cols, parts):
    return (
        lax.shift_right_logical(index, log2(cols * parts)),
        lax.shift_right_logical(index, log2(parts)) & (cols - 1),
        index & (parts - 1),
    )


def weights_kernel(index_ref, recv_ref, std_ref, mask_ref, out_ref, held_ref, pick_ref, std_rows, wet_rows):
    owners, rows, _ = recv_ref.shape
    slots = rows // 2
    total = owners * slots
    levels, cols, lat = std_ref.shape
    parts = lat // STEN
    for s in range(parts):
        part = slice(s * STEN, (s + 1) * STEN)
        wet_rows[s * cols : (s + 1) * cols, :] = mask_ref[:, part].astype(F32)
        for a in range(levels):
            first = (a * parts + s) * cols
            std_rows[first : first + cols, :] = std_ref[a, :, part]

    def pick(o, carry):
        for k in range(slots):
            slot = o * slots + k
            level, column, seg = block_place(index_ref[slot], cols, parts)
            value = std_rows[pl.ds((level * parts + seg) * cols + column, 1), :]
            wet = wet_rows[pl.ds(seg * cols + column, 1), :]
            pick_ref[pl.ds(slot, 1), :] = value * wet
        return carry

    lax.fori_loop(0, owners, pick, 0)
    ws = recv_ref[:, 0:slots, :].reshape(total, STEN) * pick_ref[...]
    out_ref[...] = ws
    place = spread_block(lat)
    for j in range(total // STEN):
        part = slice(j * STEN, (j + 1) * STEN)
        index = recv_ref[j * (STEN // slots) : (j + 1) * (STEN // slots), slots:, :].reshape(STEN, STEN)
        seg = index[:, 2:3].astype(jnp.int32) & (parts - 1)
        held = sum(dot(piece, place) for piece in split3(ws[part]))
        held = jnp.where(lane_segment(STEN, lat) == seg, held, F32(0.0))
        for q in range(parts):
            held_ref[q, part, :] = held[:, q * STEN : (q + 1) * STEN]


def to_row(column):
    eye = iota((STEN, STEN), 0) == iota((STEN, STEN), 1)
    return jnp.sum(jnp.where(eye, column, F32(0.0)), axis=0, keepdims=True)


def to_column(row):
    eye = iota((STEN, STEN), 0) == iota((STEN, STEN), 1)
    return jnp.sum(jnp.where(eye, row, F32(0.0)), axis=1, keepdims=True)


def first_kernel(
    index_ref, mixed_ref, from_left, from_right, faces_ref, recv_ref, ws_ref, held_ref,
    spread_ref, departure_ref, a_ref, b_ref, lon_ref, lat_ref, pick_ref,
):
    halo = PASSES
    parts, own_rows, _ = mixed_ref.shape
    owners, rows, _ = recv_ref.shape
    cols = faces_ref.shape[1]
    levels = own_rows // cols
    slots = rows // 2
    total = owners * slots
    edge = halo * levels
    build_faces(faces_ref, from_left, from_right, lon_ref, lat_ref, levels)
    fill(a_ref, 0, [from_left[q * edge : (q + 1) * edge, :] for q in range(parts)])
    fill(a_ref, edge, [mixed_ref[q] for q in range(parts)])
    fill(a_ref, edge + own_rows, [from_right[q * edge : (q + 1) * edge, :] for q in range(parts)])
    diffuse(a_ref, b_ref, lon_ref, lat_ref, levels)

    def pick(o, carry):
        for k in range(slots):
            slot = o * slots + k
            level, column, _ = block_place(index_ref[slot], cols, parts)
            row = edge + column * levels + level
            for q in range(parts):
                pick_ref[q, pl.ds(slot, 1), :] = a_ref[q, pl.ds(row, 1), :]
        return carry

    lax.fori_loop(0, owners, pick, 0)
    meta = recv_ref[:, slots:, :].reshape(total, STEN)
    evolved = sum(pick_ref[q] * held_ref[q] for q in range(parts))
    evolved = jnp.sum(evolved, axis=1, keepdims=True)
    departure = jnp.where(meta[:, 3:4] > 0.5, evolved - meta[:, 0:1], F32(0.0))
    scaled = meta[:, 1:2] * departure
    spread_ref[0:total, :] = scaled * ws_ref[...]
    spread_ref[total:, :] = jnp.zeros((spread_ref.shape[0] - total, STEN), F32)
    for j in range(total // STEN):
        part = slice(j * STEN, (j + 1) * STEN)
        spread_ref[total + j : total + j + 1, :] = to_row(meta[part, 2:3])
    lanes = jnp.where(iota((total, STEN), 1) == (iota((total, STEN), 0) & (slots - 1)), departure, F32(0.0))
    departure_ref[...] = jnp.sum(lanes.reshape(owners, slots, STEN), axis=1)


def second_kernel(
    vt_ref, control_ref, own_ref, left_ref, right_ref, faces_ref, from_left, from_right,
    out_ref, a_ref, b_ref, lon_ref, lat_ref,
):
    halo = PASSES
    levels, cols, lat = control_ref.shape
    parts = lat // STEN
    edge = halo * levels
    total = own_ref.shape[0] // STEN * STEN
    build_faces(faces_ref, from_left, from_right, lon_ref, lat_ref, levels)
    place = spread_block(lat)

    def scatter(source, first, count, step, target):
        pieces = []
        keys = []
        for j in range(total // STEN):
            index = source[total + j : total + j + 1, :].astype(jnp.int32)
            level, column, seg = block_place(index, cols, parts)
            keys.append((column - first) * levels + level)
            keep = lane_segment(STEN, lat) == to_column(seg.astype(F32)).astype(jnp.int32)
            held = [dot(piece, place) for piece in split(source[j * STEN : (j + 1) * STEN, :])]
            held = [jnp.where(keep, piece, F32(0.0)).astype(BF16) for piece in held]
            pieces.append(jnp.concatenate(held, axis=1))
        for c in range(0, count, step):
            rows = step * levels
            sums = jnp.zeros((rows, 2 * lat), F32)
            for key, piece in zip(keys, pieces):
                sums = sums + dot(onehot(iota((rows, STEN), 0) + c * levels == key), piece)
            sums = sums[:, :lat] + sums[:, lat:]
            fill(a_ref, (target + c) * levels, [sums[:, q * STEN : (q + 1) * STEN] for q in range(parts)])

    scatter(own_ref, 0, cols, 8, halo)
    scatter(left_ref, cols - halo, halo, halo // 2, 0)
    scatter(right_ref, 0, halo, halo // 2, halo + cols)
    diffuse(a_ref, b_ref, lon_ref, lat_ref, levels)
    matrix = mixing_matrix_back(vt_ref[...])
    back = interleave(lat)
    group = WIDE // levels
    for g in range(cols // group):
        part = slice(g * group, (g + 1) * group)
        rows = slice(edge + g * WIDE, edge + (g + 1) * WIDE)
        x = jnp.concatenate([a_ref[q, rows, :] for q in range(parts)], axis=1)
        y = product(matrix, move(split(x), back)).reshape(levels, group, lat)
        out_ref[:, part, :] = control_ref[:, part, :] + y


def call(kernel, out_shape, specs, scratch=()):
    return pl.pallas_call(
        kernel,
        out_shape=out_shape,
        in_specs=specs,
        out_specs=jax.tree.map(lambda _: VMEM_SPEC, out_shape),
        scratch_shapes=list(scratch),
        compiler_params=pltpu.CompilerParams(vmem_limit_bytes=VMEM_LIMIT),
    )


def shape(*dims):
    return jax.ShapeDtypeStruct(dims, F32)


def local(
    control, std_field, kappa_lon, kappa_lat, sea_mask, vertical,
    block_index, weights, obs_value, obs_rinv, obs_count,
):
    levels, cols, lat = control.shape
    parts = lat // STEN
    owners, slots = block_index.shape[1:]
    total = owners * slots
    halo = PASSES
    width = cols + 2 * halo
    count = lax.axis_size("lon")
    to_right = [(i, (i + 1) % count) for i in range(count)]
    to_left = [((i + 1) % count, i) for i in range(count)]

    valid = jnp.arange(slots, dtype=jnp.int32)[None, :] < obs_count[0][:, None]
    meta = jnp.stack(
        [obs_value[0], obs_rinv[0], block_index[0].astype(F32), valid.astype(F32)], axis=-1
    )
    meta = jnp.pad(meta, ((0, 0), (0, 0), (0, STEN - 4)))
    sent = jnp.concatenate([weights[0], meta], axis=1)

    message = parts * halo * (levels + 2) + parts
    message = -(-message // 8) * 8
    mixed, faces, edge_left, edge_right = call(
        head_kernel,
        (
            shape(parts, cols * levels, STEN), shape(3 * parts, cols, STEN),
            shape(message, STEN), shape(message, STEN),
        ),
        [VMEM_SPEC] + [pl.BlockSpec(memory_space=pl.ANY)] * 4,
        [
            pltpu.VMEM((levels, cols, lat), F32), pltpu.VMEM((cols, lat), F32), pltpu.VMEM((cols, lat), F32),
            pltpu.VMEM((cols, lat), jnp.int32), pltpu.SemaphoreType.DMA((4,)),
        ],
    )(vertical, control, kappa_lon, kappa_lat, sea_mask)
    from_left = lax.ppermute(edge_right, "lon", to_right)
    from_right = lax.ppermute(edge_left, "lon", to_left)

    recv = lax.all_to_all(sent, "lon", split_axis=0, concat_axis=0, tiled=True)
    index = recv[:, slots:, 2].reshape(total).astype(jnp.int32)
    ws, held = call(
        weights_kernel,
        (shape(total, STEN), shape(parts, total, STEN)),
        [SMEM_SPEC] + [VMEM_SPEC] * 3,
        [
            pltpu.VMEM((total, STEN), F32), pltpu.VMEM((levels * cols * parts, STEN), F32),
            pltpu.VMEM((cols * parts, STEN), F32),
        ],
    )(index, recv, std_field, sea_mask)

    field = pltpu.VMEM((parts + 2, width * levels, STEN), F32)
    faces_held = [pltpu.VMEM((parts, width * 8, STEN), F32), pltpu.VMEM((parts + 1, width * 8, STEN), F32)]
    extra = -(-total // (8 * STEN)) * 8
    spread, departure = call(
        first_kernel,
        (shape(total + extra, STEN), shape(owners, STEN)),
        [SMEM_SPEC] + [VMEM_SPEC] * 7,
        [field, field, *faces_held, pltpu.VMEM((parts, total, STEN), F32)],
    )(index, mixed, from_left, from_right, faces, recv, ws, held)

    spread_left = lax.ppermute(spread, "lon", to_right)
    spread_right = lax.ppermute(spread, "lon", to_left)
    mine = lax.all_to_all(departure[:, None, :], "lon", split_axis=0, concat_axis=0, tiled=True)

    gradient = call(
        second_kernel, shape(levels, cols, lat), [VMEM_SPEC] * 8, [field, field, *faces_held]
    )(vertical.T, control, spread, spread_left, spread_right, faces, from_left, from_right)
    return gradient, mine[:, 0, :slots][None]


def solution(mesh):
    in_specs = (
        P("grp", "lon", None),
        P(None, "lon", None),
        P("lon", None),
        P("lon", None),
        P("lon", None),
        P(),
        P(("grp", "lon"), None, None),
        P(("grp", "lon"), None, None, None),
        P(("grp", "lon"), None, None),
        P(("grp", "lon"), None, None),
        P(("grp", "lon"), None),
    )
    out_specs = (P("grp", "lon", None), P(("grp", "lon"), None, None))
    return jax.shard_map(local, mesh=mesh, in_specs=in_specs, out_specs=out_specs, check_vma=False)
```

```python
import jax
import jax.numpy as jnp
from jax import lax
from jax.experimental import pallas as pl
from jax.experimental.pallas import tpu as pltpu
from jax.sharding import PartitionSpec as P

STEN = 128
PASSES = 10
WIDE = 256
F32 = jnp.float32
BF16 = jnp.bfloat16
TIERS = ((0, 4), (4, PASSES))
VMEM_LIMIT = 24 * 1024 * 1024

VMEM_SPEC = pl.BlockSpec(memory_space=pltpu.VMEM)
SMEM_SPEC = pl.BlockSpec(memory_space=pltpu.SMEM)


def split(x):
    high = x.astype(BF16)
    return high, (x - high.astype(F32)).astype(BF16)


def split3(x):
    high = x.astype(BF16)
    rest = x - high.astype(F32)
    middle = rest.astype(BF16)
    return high, middle, (rest - middle.astype(F32)).astype(BF16)


def dot(a, b):
    return jnp.dot(a, b, preferred_element_type=F32)


def log2(n):
    assert n & (n - 1) == 0
    return n.bit_length() - 1


def iota(shape, dim):
    return lax.broadcasted_iota(jnp.int32, shape, dim)


def onehot(condition):
    return jnp.where(condition, F32(1.0), F32(0.0)).astype(BF16)


def product(left, right):
    (lh, ll), (rh, rl) = left, right
    return dot(lh, rh) + (dot(lh, rl) + dot(ll, rh))


def mixing_matrix(vertical):
    levels = vertical.shape[0]
    group = WIDE // levels
    expand = onehot(iota((levels, WIDE), 1) // group == iota((levels, WIDE), 0))
    keep = iota((WIDE, WIDE), 0) // levels == iota((WIDE, WIDE), 1) % group
    out = []
    for part in split(vertical):
        rows = dot(part, expand)
        tiled = jnp.concatenate([rows] * group, axis=0)
        out.append(jnp.where(keep, tiled, F32(0.0)).astype(BF16))
    return tuple(out)


def mixing_matrix_back(vertical):
    levels = vertical.shape[0]
    group = WIDE // levels
    spread = onehot(iota((levels, WIDE), 1) % levels == iota((levels, WIDE), 0))
    repeat = onehot(iota((WIDE, levels), 0) // group == iota((WIDE, levels), 1))
    keep = iota((WIDE, WIDE), 0) % group == iota((WIDE, WIDE), 1) // levels
    out = []
    for part in split(vertical):
        rows = lax.dot_general(part, spread, (((0,), (0,)), ((), ())), preferred_element_type=F32)
        rows = rows.astype(BF16)
        out.append(jnp.where(keep, dot(repeat, rows), F32(0.0)).astype(BF16))
    return tuple(out)


def deinterleave(lat):
    parts = lat // STEN
    target = iota((lat, lat), 1)
    return onehot(iota((lat, lat), 0) == (target % STEN) * parts + target // STEN)


def interleave(lat):
    parts = lat // STEN
    source = iota((lat, lat), 0)
    return onehot(iota((lat, lat), 1) == (source % STEN) * parts + source // STEN)


def spread_block(lat):
    parts = lat // STEN
    target = iota((STEN, lat), 1)
    return onehot(iota((STEN, lat), 0) == (target % (STEN // parts)) * parts + target // STEN)


def lane_segment(rows, lat):
    parts = lat // STEN
    return (iota((rows, lat), 1) % STEN) // (STEN // parts)


def move(x, matrix):
    return tuple(dot(part, matrix).astype(BF16) for part in x)


def head_kernel(v_ref, control_ref, klon_ref, klat_ref, mask_ref, mixed_ref, faces_ref, left_ref, right_ref):
    levels, cols, lat = control_ref.shape
    parts = lat // STEN
    group = WIDE // levels
    halo = PASSES
    edge = halo * levels
    place = deinterleave(lat)
    matrix = mixing_matrix(v_ref[...])
    wet = mask_ref[...].astype(F32)
    east = jnp.where(iota((cols, lat), 0) == cols - 1, F32(1.0), pltpu.roll(wet, cols - 1, 0))
    north = jnp.where(iota((cols, lat), 1) == lat - 1, F32(0.0), pltpu.roll(wet, lat - 1, 1))
    for k, face in enumerate((klon_ref[...] * wet * east, klat_ref[...] * wet * north, wet)):
        held = sum(dot(piece, place) for piece in (split3(face) if k < 2 else (face.astype(BF16),)))
        for q in range(parts):
            faces_ref[k * parts + q] = held[:, q * STEN : (q + 1) * STEN]
    for g in range(cols // group):
        x = control_ref[:, g * group : (g + 1) * group, :].reshape(WIDE, lat)
        y = product(matrix, move(split(x), place))
        for q in range(parts):
            mixed_ref[q, g * WIDE : (g + 1) * WIDE, :] = y[:, q * STEN : (q + 1) * STEN]
    for out, start in ((left_ref, 0), (right_ref, cols - halo)):
        for q in range(parts):
            out[q * edge : (q + 1) * edge, :] = mixed_ref[q, start * levels : start * levels + edge, :]
        for k in range(2 * parts):
            first = parts * edge + k * halo
            out[first : first + halo, :] = faces_ref[k, start : start + halo, :]
        first = parts * edge + 2 * parts * halo
        for q in range(parts):
            out[first + q : first + q + 1, :] = faces_ref[2 * parts + q, 0:1, :]
        out[first + parts :, :] = jnp.zeros((out.shape[0] - first - parts, STEN), F32)


def build_faces(faces_ref, from_left, from_right, lon_ref, lat_ref, levels):
    halo = PASSES
    cols = faces_ref.shape[1]
    parts = faces_ref.shape[0] // 3
    first = parts * halo * levels
    shape = (8, STEN)

    def far(source, k, c):
        at = first + k * halo + c
        return source[at : at + 1, :]

    for c in range(cols + 2 * halo):
        rows = slice(8 * c, 8 * c + 8)
        for q in range(parts):
            if c < halo:
                lon_row, lat_row = far(from_left, q, c), far(from_left, parts + q, c)
                if c == halo - 1:
                    lon_row = lon_row * faces_ref[2 * parts + q, 0:1, :]
            elif c < halo + cols:
                own = c - halo
                lon_row = faces_ref[q, own : own + 1, :]
                lat_row = faces_ref[parts + q, own : own + 1, :]
                if own == cols - 1:
                    at = first + 2 * parts * halo + q
                    lon_row = lon_row * from_right[at : at + 1, :]
            else:
                own = c - halo - cols
                lon_row, lat_row = far(from_right, q, own), far(from_right, parts + q, own)
            lon_ref[q, rows, :] = jnp.broadcast_to(lon_row, shape)
            lat_ref[q, rows, :] = jnp.broadcast_to(lat_row, shape)
            if q == parts - 1:
                lat_ref[parts, rows, :] = jnp.broadcast_to(pltpu.roll(lat_row, 1, 1), shape)


def add_ghosts(ref, first, values):
    count = values[0].shape[0]
    parts = len(values)
    ref[parts, first : first + count, :] = pltpu.roll(values[0], STEN - 1, 1)
    ref[parts + 1, first : first + count, :] = pltpu.roll(values[-1], 1, 1)


def fill(ref, first, values):
    for q, value in enumerate(values):
        ref[q, first : first + value.shape[0], :] = value
    add_ghosts(ref, first, values)


def one_pass(src, dst, lon_ref, lat_ref, levels, low, high):
    parts = lon_ref.shape[0]
    halves = range(levels // 8)

    def load(k, c, h):
        return src[k, c * levels + 8 * h : c * levels + 8 * h + 8, :]

    def face(ref, k, c):
        return ref[k, 8 * c : 8 * c + 8, :]

    here = [[load(q, low, h) for q in range(parts)] for h in halves]
    west = [[face(lon_ref, q, low - 1) * (here[h][q] - load(q, low - 1, h)) for q in range(parts)] for h in halves]
    for c in range(low, high):
        lon = [face(lon_ref, q, c) for q in range(parts)]
        lat = [face(lat_ref, q, c) for q in range(parts + 1)]
        for h in halves:
            line = here[h]
            east = [load(q, c + 1, h) for q in range(parts)]
            flux_east = [lon[q] * (east[q] - line[q]) for q in range(parts)]
            ahead = line[1:] + [load(parts, c, h)]
            flux_north = [lat[parts] * (line[0] - load(parts + 1, c, h))]
            flux_north += [lat[q] * (ahead[q] - line[q]) for q in range(parts)]
            out = [
                line[q] + (flux_east[q] - west[h][q]) + (flux_north[q + 1] - flux_north[q])
                for q in range(parts)
            ]
            first = c * levels + 8 * h
            for q in range(parts):
                dst[q, first : first + 8, :] = out[q]
            add_ghosts(dst, first, out)
            here[h], west[h] = east, flux_east


def diffuse(a_ref, b_ref, lon_ref, lat_ref, levels):
    width = a_ref.shape[1] // levels

    for first, last in TIERS:

        def pair(turn, carry):
            one_pass(a_ref, b_ref, lon_ref, lat_ref, levels, first + 1, width - first - 1)
            one_pass(b_ref, a_ref, lon_ref, lat_ref, levels, first + 2, width - first - 2)
            return carry

        lax.fori_loop(first // 2, last // 2, pair, 0)


def block_place(index, cols, parts):
    return (
        lax.shift_right_logical(index, log2(cols * parts)),
        lax.shift_right_logical(index, log2(parts)) & (cols - 1),
        index & (parts - 1),
    )


def weights_kernel(place_ref, recv_ref, std_ref, mask_ref, out_ref, held_ref, pick_ref, std_rows, wet_rows):
    owners, rows, _ = recv_ref.shape
    slots = rows // 2
    total = owners * slots
    levels, cols, lat = std_ref.shape
    parts = lat // STEN
    for s in range(parts):
        part = slice(s * STEN, (s + 1) * STEN)
        wet_rows[s * cols : (s + 1) * cols, :] = mask_ref[:, part].astype(F32)
        for a in range(levels):
            first = (a * parts + s) * cols
            std_rows[first : first + cols, :] = std_ref[a, :, part]

    def pick(o, carry):
        for k in range(slots):
            slot = o * slots + k
            level, column, seg = block_place(place_ref[0, slot], cols, parts)
            value = std_rows[pl.ds((level * parts + seg) * cols + column, 1), :]
            wet = wet_rows[pl.ds(seg * cols + column, 1), :]
            pick_ref[pl.ds(slot, 1), :] = value * wet
        return carry

    lax.fori_loop(0, owners, pick, 0)
    ws = recv_ref[:, 0:slots, :].reshape(total, STEN) * pick_ref[...]
    out_ref[...] = ws
    place = spread_block(lat)
    for j in range(total // STEN):
        part = slice(j * STEN, (j + 1) * STEN)
        index = recv_ref[j * (STEN // slots) : (j + 1) * (STEN // slots), slots:, :].reshape(STEN, STEN)
        seg = index[:, 2:3].astype(jnp.int32) & (parts - 1)
        held = sum(dot(piece, place) for piece in split3(ws[part]))
        held = jnp.where(lane_segment(STEN, lat) == seg, held, F32(0.0))
        for q in range(parts):
            held_ref[q, part, :] = held[:, q * STEN : (q + 1) * STEN]


def to_row(column):
    eye = iota((STEN, STEN), 0) == iota((STEN, STEN), 1)
    return jnp.sum(jnp.where(eye, column, F32(0.0)), axis=0, keepdims=True)


def to_column(row):
    eye = iota((STEN, STEN), 0) == iota((STEN, STEN), 1)
    return jnp.sum(jnp.where(eye, row, F32(0.0)), axis=1, keepdims=True)


def first_kernel(
    place_ref, mixed_ref, from_left, from_right, faces_ref, recv_ref, ws_ref, held_ref,
    spread_ref, departure_ref, a_ref, b_ref, lon_ref, lat_ref, pick_ref,
):
    halo = PASSES
    parts, own_rows, _ = mixed_ref.shape
    owners, rows, _ = recv_ref.shape
    cols = faces_ref.shape[1]
    levels = own_rows // cols
    slots = rows // 2
    total = owners * slots
    edge = halo * levels
    build_faces(faces_ref, from_left, from_right, lon_ref, lat_ref, levels)
    fill(a_ref, 0, [from_left[q * edge : (q + 1) * edge, :] for q in range(parts)])
    fill(a_ref, edge, [mixed_ref[q] for q in range(parts)])
    fill(a_ref, edge + own_rows, [from_right[q * edge : (q + 1) * edge, :] for q in range(parts)])
    diffuse(a_ref, b_ref, lon_ref, lat_ref, levels)

    def pick(o, carry):
        for k in range(slots):
            slot = o * slots + k
            row = place_ref[1, slot]
            for q in range(parts):
                pick_ref[q, pl.ds(slot, 1), :] = a_ref[q, pl.ds(row, 1), :]
        return carry

    lax.fori_loop(0, owners, pick, 0)
    meta = recv_ref[:, slots:, :].reshape(total, STEN)
    evolved = sum(pick_ref[q] * held_ref[q] for q in range(parts))
    evolved = jnp.sum(evolved, axis=1, keepdims=True)
    departure = jnp.where(meta[:, 3:4] > 0.5, evolved - meta[:, 0:1], F32(0.0))
    scaled = meta[:, 1:2] * departure
    spread_ref[0:total, :] = scaled * ws_ref[...]
    spread_ref[total:, :] = jnp.zeros((spread_ref.shape[0] - total, STEN), F32)
    for j in range(total // STEN):
        part = slice(j * STEN, (j + 1) * STEN)
        spread_ref[total + j : total + j + 1, :] = to_row(meta[part, 2:3])
    lanes = jnp.where(iota((total, STEN), 1) == (iota((total, STEN), 0) & (slots - 1)), departure, F32(0.0))
    departure_ref[...] = jnp.sum(lanes.reshape(owners, slots, STEN), axis=1)


def second_kernel(
    v_ref, control_ref, own_ref, left_ref, right_ref, faces_ref, from_left, from_right,
    out_ref, a_ref, b_ref, lon_ref, lat_ref,
):
    halo = PASSES
    levels, cols, lat = control_ref.shape
    parts = lat // STEN
    edge = halo * levels
    total = own_ref.shape[0] // STEN * STEN
    build_faces(faces_ref, from_left, from_right, lon_ref, lat_ref, levels)
    place = spread_block(lat)

    def scatter(source, first, count, step, target):
        pieces = []
        keys = []
        for j in range(total // STEN):
            index = source[total + j : total + j + 1, :].astype(jnp.int32)
            level, column, seg = block_place(index, cols, parts)
            keys.append((column - first) * levels + level)
            keep = lane_segment(STEN, lat) == to_column(seg.astype(F32)).astype(jnp.int32)
            held = [dot(piece, place) for piece in split(source[j * STEN : (j + 1) * STEN, :])]
            held = [jnp.where(keep, piece, F32(0.0)).astype(BF16) for piece in held]
            pieces.append(jnp.concatenate(held, axis=1))
        for c in range(0, count, step):
            rows = step * levels
            sums = jnp.zeros((rows, 2 * lat), F32)
            for key, piece in zip(keys, pieces):
                sums = sums + dot(onehot(iota((rows, STEN), 0) + c * levels == key), piece)
            sums = sums[:, :lat] + sums[:, lat:]
            fill(a_ref, (target + c) * levels, [sums[:, q * STEN : (q + 1) * STEN] for q in range(parts)])

    scatter(own_ref, 0, cols, 8, halo)
    scatter(left_ref, cols - halo, halo, halo // 2, 0)
    scatter(right_ref, 0, halo, halo // 2, halo + cols)
    diffuse(a_ref, b_ref, lon_ref, lat_ref, levels)
    matrix = mixing_matrix_back(v_ref[...])
    back = interleave(lat)
    group = WIDE // levels
    for g in range(cols // group):
        part = slice(g * group, (g + 1) * group)
        rows = slice(edge + g * WIDE, edge + (g + 1) * WIDE)
        x = jnp.concatenate([a_ref[q, rows, :] for q in range(parts)], axis=1)
        y = product(matrix, move(split(x), back)).reshape(levels, group, lat)
        out_ref[:, part, :] = control_ref[:, part, :] + y


def call(kernel, out_shape, specs, scratch, flops, moved):
    return pl.pallas_call(
        kernel,
        out_shape=out_shape,
        in_specs=specs,
        out_specs=jax.tree.map(lambda _: VMEM_SPEC, out_shape),
        scratch_shapes=list(scratch),
        cost_estimate=pl.CostEstimate(flops=flops, bytes_accessed=moved, transcendentals=0),
        compiler_params=pltpu.CompilerParams(vmem_limit_bytes=VMEM_LIMIT),
    )


def shape(*dims):
    return jax.ShapeDtypeStruct(dims, F32)


def local(
    control, std_field, kappa_lon, kappa_lat, sea_mask, vertical,
    block_index, weights, obs_value, obs_rinv, obs_count,
):
    levels, cols, lat = control.shape
    parts = lat // STEN
    owners, slots = block_index.shape[1:]
    total = owners * slots
    halo = PASSES
    width = cols + 2 * halo
    cells = width * levels * lat
    count = lax.axis_size("lon")
    to_right = [(i, (i + 1) % count) for i in range(count)]
    to_left = [((i + 1) % count, i) for i in range(count)]

    valid = jnp.arange(slots, dtype=jnp.int32)[None, :] < obs_count[0][:, None]
    meta = jnp.stack(
        [obs_value[0], obs_rinv[0], block_index[0].astype(F32), valid.astype(F32)], axis=-1
    )
    meta = jnp.pad(meta, ((0, 0), (0, 0), (0, STEN - 4)))
    sent = jnp.concatenate([weights[0], meta], axis=1)
    sent, matrix = lax.optimization_barrier((sent, vertical))

    message = parts * halo * (levels + 2) + parts
    message = -(-message // 8) * 8
    mixed, faces, edge_left, edge_right = call(
        head_kernel,
        (
            shape(parts, cols * levels, STEN), shape(3 * parts, cols, STEN),
            shape(message, STEN), shape(message, STEN),
        ),
        [VMEM_SPEC] * 5, [],
        12 * cells * lat, 8 * 4 * cells,
    )(matrix, control, kappa_lon, kappa_lat, sea_mask)
    from_left = lax.ppermute(edge_right, "lon", to_right)
    from_right = lax.ppermute(edge_left, "lon", to_left)

    recv = lax.all_to_all(sent, "lon", split_axis=0, concat_axis=0, tiled=True)
    index = recv[:, slots:, 2].reshape(total).astype(jnp.int32)
    level, column, _ = block_place(index, cols, parts)
    places = jnp.stack([index, (halo + column) * levels + level])
    ws, held = call(
        weights_kernel,
        (shape(total, STEN), shape(parts, total, STEN)),
        [SMEM_SPEC] + [VMEM_SPEC] * 3,
        [
            pltpu.VMEM((total, STEN), F32), pltpu.VMEM((levels * cols * parts, STEN), F32),
            pltpu.VMEM((cols * parts, STEN), F32),
        ],
        6 * total * STEN * lat, 4 * 4 * cells,
    )(places, recv, std_field, sea_mask)

    field = pltpu.VMEM((parts + 2, width * levels, STEN), F32)
    faces_held = [pltpu.VMEM((parts, width * 8, STEN), F32), pltpu.VMEM((parts + 1, width * 8, STEN), F32)]
    extra = -(-total // (8 * STEN)) * 8
    spread, departure = call(
        first_kernel,
        (shape(total + extra, STEN), shape(owners, STEN)),
        [SMEM_SPEC] + [VMEM_SPEC] * 7,
        [field, field, *faces_held, pltpu.VMEM((parts, total, STEN), F32)],
        10 * PASSES * cells, 2 * PASSES * 4 * cells,
    )(places, mixed, from_left, from_right, faces, recv, ws, held)

    spread_left = lax.ppermute(spread, "lon", to_right)
    spread_right = lax.ppermute(spread, "lon", to_left)
    mine = lax.all_to_all(departure[:, None, :], "lon", split_axis=0, concat_axis=0, tiled=True)

    gradient = call(
        second_kernel, shape(levels, cols, lat), [VMEM_SPEC] * 8, [field, field, *faces_held],
        10 * PASSES * cells, 2 * PASSES * 4 * cells,
    )(vertical, control, spread, spread_left, spread_right, faces, from_left, from_right)
    gradient, mine = lax.optimization_barrier((gradient, mine))
    return gradient, mine[:, 0, :slots][None]


def solution(mesh):
    in_specs = (
        P("grp", "lon", None),
        P(None, "lon", None),
        P("lon", None),
        P("lon", None),
        P("lon", None),
        P(),
        P(("grp", "lon"), None, None),
        P(("grp", "lon"), None, None, None),
        P(("grp", "lon"), None, None),
        P(("grp", "lon"), None, None),
        P(("grp", "lon"), None),
    )
    out_specs = (P("grp", "lon", None), P(("grp", "lon"), None, None))
    return jax.shard_map(local, mesh=mesh, in_specs=in_specs, out_specs=out_specs, check_vma=False)
```

```python
import jax
import jax.numpy as jnp
from jax import lax
from jax.experimental import pallas as pl
from jax.experimental.pallas import tpu as pltpu
from jax.sharding import PartitionSpec as P

STEN = 128
PASSES = 10
WIDE = 256
F32 = jnp.float32
BF16 = jnp.bfloat16
WHOLE_VMEM = 60 * 1024 * 1024
TIERS = ((0, 4), (4, PASSES))
VMEM_LIMIT = 24 * 1024 * 1024

VMEM_SPEC = pl.BlockSpec(memory_space=pltpu.VMEM)
SMEM_SPEC = pl.BlockSpec(memory_space=pltpu.SMEM)


def split(x):
    high = x.astype(BF16)
    return high, (x - high.astype(F32)).astype(BF16)


def split3(x):
    high = x.astype(BF16)
    rest = x - high.astype(F32)
    middle = rest.astype(BF16)
    return high, middle, (rest - middle.astype(F32)).astype(BF16)


def dot(a, b):
    return jnp.dot(a, b, preferred_element_type=F32)


def log2(n):
    assert n & (n - 1) == 0
    return n.bit_length() - 1


def iota(shape, dim):
    return lax.broadcasted_iota(jnp.int32, shape, dim)


def onehot(condition):
    return jnp.where(condition, F32(1.0), F32(0.0)).astype(BF16)


def product(left, right):
    (lh, ll), (rh, rl) = left, right
    return dot(lh, rh) + (dot(lh, rl) + dot(ll, rh))


def mixing_matrix(vertical):
    levels = vertical.shape[0]
    group = WIDE // levels
    expand = onehot(iota((levels, WIDE), 1) // group == iota((levels, WIDE), 0))
    keep = iota((WIDE, WIDE), 0) // levels == iota((WIDE, WIDE), 1) % group
    out = []
    for part in split(vertical):
        rows = dot(part, expand)
        tiled = jnp.concatenate([rows] * group, axis=0)
        out.append(jnp.where(keep, tiled, F32(0.0)).astype(BF16))
    return tuple(out)


def mixing_matrix_back(vertical):
    levels = vertical.shape[0]
    group = WIDE // levels
    spread = onehot(iota((levels, WIDE), 1) % levels == iota((levels, WIDE), 0))
    repeat = onehot(iota((WIDE, levels), 0) // group == iota((WIDE, levels), 1))
    keep = iota((WIDE, WIDE), 0) % group == iota((WIDE, WIDE), 1) // levels
    out = []
    for part in split(vertical):
        rows = lax.dot_general(part, spread, (((0,), (0,)), ((), ())), preferred_element_type=F32)
        rows = rows.astype(BF16)
        out.append(jnp.where(keep, dot(repeat, rows), F32(0.0)).astype(BF16))
    return tuple(out)


def deinterleave(lat):
    parts = lat // STEN
    target = iota((lat, lat), 1)
    return onehot(iota((lat, lat), 0) == (target % STEN) * parts + target // STEN)


def interleave(lat):
    parts = lat // STEN
    source = iota((lat, lat), 0)
    return onehot(iota((lat, lat), 1) == (source % STEN) * parts + source // STEN)


def spread_block(lat):
    parts = lat // STEN
    target = iota((STEN, lat), 1)
    return onehot(iota((STEN, lat), 0) == (target % (STEN // parts)) * parts + target // STEN)


def lane_segment(rows, lat):
    parts = lat // STEN
    return (iota((rows, lat), 1) % STEN) // (STEN // parts)


def move(x, matrix):
    return tuple(dot(part, matrix).astype(BF16) for part in x)


def pack_meta(slots, values):
    stacked = jnp.concatenate(values, axis=0)
    eye = onehot(iota((stacked.shape[0], STEN), 0) == iota((stacked.shape[0], STEN), 1))
    return sum(
        lax.dot_general(part, eye, (((0,), (0,)), ((), ())), preferred_element_type=F32)
        for part in split3(stacked)
    )


def unpack_meta(recv_ref, slots, field):
    owners = recv_ref.shape[0]
    total = owners * slots
    rows = jnp.broadcast_to(recv_ref[:, slots : slots + 1, :], (owners, slots, STEN)).reshape(total, STEN)
    wanted = (iota((total, STEN), 0) & (slots - 1)) + field * slots
    return jnp.sum(jnp.where(iota((total, STEN), 1) == wanted, rows, F32(0.0)), axis=1, keepdims=True)


def head_kernel(
    mask_hbm, klon_hbm, klat_hbm, v_hbm, control_hbm, mixed_ref, faces_ref, left_ref, right_ref,
    mask_ref, klon_ref, klat_ref, v_ref, control_ref, sems,
):
    pairs = (
        (mask_hbm, mask_ref), (klon_hbm, klon_ref), (klat_hbm, klat_ref), (v_hbm, v_ref), (control_hbm, control_ref),
    )
    copies = [pltpu.make_async_copy(source, target, sems.at[k]) for k, (source, target) in enumerate(pairs)]
    for copy in copies:
        copy.start()
    levels, cols, lat = control_ref.shape
    parts = lat // STEN
    group = WIDE // levels
    halo = PASSES
    edge = halo * levels
    place = deinterleave(lat)
    for copy in copies[:4]:
        copy.wait()
    matrix = mixing_matrix(v_ref[...])
    wet = mask_ref[...].astype(F32)
    east = jnp.where(iota((cols, lat), 0) == cols - 1, F32(1.0), pltpu.roll(wet, cols - 1, 0))
    north = jnp.where(iota((cols, lat), 1) == lat - 1, F32(0.0), pltpu.roll(wet, lat - 1, 1))
    for k, face in enumerate((klon_ref[...] * wet * east, klat_ref[...] * wet * north, wet)):
        held = sum(dot(piece, place) for piece in (split3(face) if k < 2 else (face.astype(BF16),)))
        for q in range(parts):
            faces_ref[k * parts + q] = held[:, q * STEN : (q + 1) * STEN]
    copies[4].wait()
    for g in range(cols // group):
        x = control_ref[:, g * group : (g + 1) * group, :].reshape(WIDE, lat)
        y = product(matrix, move(split(x), place))
        for q in range(parts):
            mixed_ref[q, g * WIDE : (g + 1) * WIDE, :] = y[:, q * STEN : (q + 1) * STEN]
    for out, start in ((left_ref, 0), (right_ref, cols - halo)):
        for q in range(parts):
            out[q * edge : (q + 1) * edge, :] = mixed_ref[q, start * levels : start * levels + edge, :]
        for k in range(2 * parts):
            first = parts * edge + k * halo
            out[first : first + halo, :] = faces_ref[k, start : start + halo, :]
        first = parts * edge + 2 * parts * halo
        for q in range(parts):
            out[first + q : first + q + 1, :] = faces_ref[2 * parts + q, 0:1, :]
        out[first + parts :, :] = jnp.zeros((out.shape[0] - first - parts, STEN), F32)


def pack_kernel(faces_hbm, index_ref, value_ref, rinv_ref, count_ref, weights_ref, sent_ref):
    owners, slots, _ = weights_ref.shape
    sent_ref[:, 0:slots, :] = weights_ref[...]
    valid = jnp.where(iota((slots, owners), 0) < count_ref[...], F32(1.0), F32(0.0))
    meta = pack_meta(slots, [value_ref[...], rinv_ref[...], index_ref[...].astype(F32), valid])
    sent_ref[:, slots:, :] = jnp.broadcast_to(meta[:, None, :], (owners, slots, STEN))


def build_faces(faces_ref, from_left, from_right, lon_ref, lat_ref, levels):
    halo = PASSES
    cols = faces_ref.shape[1]
    parts = faces_ref.shape[0] // 3
    first = parts * halo * levels
    shape = (8, STEN)

    def far(source, k, c):
        at = first + k * halo + c
        return source[at : at + 1, :]

    for c in range(cols + 2 * halo):
        rows = slice(8 * c, 8 * c + 8)
        for q in range(parts):
            if c < halo:
                lon_row, lat_row = far(from_left, q, c), far(from_left, parts + q, c)
                if c == halo - 1:
                    lon_row = lon_row * faces_ref[2 * parts + q, 0:1, :]
            elif c < halo + cols:
                own = c - halo
                lon_row = faces_ref[q, own : own + 1, :]
                lat_row = faces_ref[parts + q, own : own + 1, :]
                if own == cols - 1:
                    at = first + 2 * parts * halo + q
                    lon_row = lon_row * from_right[at : at + 1, :]
            else:
                own = c - halo - cols
                lon_row, lat_row = far(from_right, q, own), far(from_right, parts + q, own)
            lon_ref[q, rows, :] = jnp.broadcast_to(lon_row, shape)
            lat_ref[q, rows, :] = jnp.broadcast_to(lat_row, shape)
            if q == parts - 1:
                lat_ref[parts, rows, :] = jnp.broadcast_to(pltpu.roll(lat_row, 1, 1), shape)


def add_ghosts(ref, first, values):
    count = values[0].shape[0]
    parts = len(values)
    ref[parts, first : first + count, :] = pltpu.roll(values[0], STEN - 1, 1)
    ref[parts + 1, first : first + count, :] = pltpu.roll(values[-1], 1, 1)


def fill(ref, first, values):
    for q, value in enumerate(values):
        ref[q, first : first + value.shape[0], :] = value
    add_ghosts(ref, first, values)


def one_pass(src, dst, lon_ref, lat_ref, levels, low, high):
    parts = lon_ref.shape[0]
    halves = range(levels // 8)

    def load(k, c, h):
        return src[k, c * levels + 8 * h : c * levels + 8 * h + 8, :]

    def face(ref, k, c):
        return ref[k, 8 * c : 8 * c + 8, :]

    here = [[load(q, low, h) for q in range(parts)] for h in halves]
    west = [[face(lon_ref, q, low - 1) * (here[h][q] - load(q, low - 1, h)) for q in range(parts)] for h in halves]
    for c in range(low, high):
        lon = [face(lon_ref, q, c) for q in range(parts)]
        lat = [face(lat_ref, q, c) for q in range(parts + 1)]
        for h in halves:
            line = here[h]
            east = [load(q, c + 1, h) for q in range(parts)]
            flux_east = [lon[q] * (east[q] - line[q]) for q in range(parts)]
            ahead = line[1:] + [load(parts, c, h)]
            flux_north = [lat[parts] * (line[0] - load(parts + 1, c, h))]
            flux_north += [lat[q] * (ahead[q] - line[q]) for q in range(parts)]
            out = [
                line[q] + (flux_east[q] - west[h][q]) + (flux_north[q + 1] - flux_north[q])
                for q in range(parts)
            ]
            first = c * levels + 8 * h
            for q in range(parts):
                dst[q, first : first + 8, :] = out[q]
            add_ghosts(dst, first, out)
            here[h], west[h] = east, flux_east


def diffuse(a_ref, b_ref, lon_ref, lat_ref, levels):
    width = a_ref.shape[1] // levels

    for first, last in TIERS:

        def pair(turn, carry):
            one_pass(a_ref, b_ref, lon_ref, lat_ref, levels, first + 1, width - first - 1)
            one_pass(b_ref, a_ref, lon_ref, lat_ref, levels, first + 2, width - first - 2)
            return carry

        lax.fori_loop(first // 2, last // 2, pair, 0)


def block_place(index, cols, parts):
    return (
        lax.shift_right_logical(index, log2(cols * parts)),
        lax.shift_right_logical(index, log2(parts)) & (cols - 1),
        index & (parts - 1),
    )


def weights_kernel(place_ref, recv_ref, std_ref, mask_ref, out_ref, held_ref, pick_ref, std_rows, wet_rows):
    owners, rows, _ = recv_ref.shape
    slots = rows // 2
    total = owners * slots
    levels, cols, lat = std_ref.shape
    parts = lat // STEN
    for s in range(parts):
        part = slice(s * STEN, (s + 1) * STEN)
        wet_rows[s * cols : (s + 1) * cols, :] = mask_ref[:, part].astype(F32)
        for a in range(levels):
            first = (a * parts + s) * cols
            std_rows[first : first + cols, :] = std_ref[a, :, part]

    def pick(o, carry):
        for k in range(slots):
            slot = o * slots + k
            level, column, seg = block_place(place_ref[0, slot], cols, parts)
            value = std_rows[pl.ds((level * parts + seg) * cols + column, 1), :]
            wet = wet_rows[pl.ds(seg * cols + column, 1), :]
            pick_ref[pl.ds(slot, 1), :] = value * wet
        return carry

    lax.fori_loop(0, owners, pick, 0)
    ws = recv_ref[:, 0:slots, :].reshape(total, STEN) * pick_ref[...]
    out_ref[...] = ws
    place = spread_block(lat)
    segs = unpack_meta(recv_ref, slots, 2).astype(jnp.int32) & (parts - 1)
    for j in range(total // STEN):
        part = slice(j * STEN, (j + 1) * STEN)
        seg = segs[part]
        held = sum(dot(piece, place) for piece in split3(ws[part]))
        held = jnp.where(lane_segment(STEN, lat) == seg, held, F32(0.0))
        for q in range(parts):
            held_ref[q, part, :] = held[:, q * STEN : (q + 1) * STEN]


def to_row(column):
    eye = iota((STEN, STEN), 0) == iota((STEN, STEN), 1)
    return jnp.sum(jnp.where(eye, column, F32(0.0)), axis=0, keepdims=True)


def to_column(row):
    eye = iota((STEN, STEN), 0) == iota((STEN, STEN), 1)
    return jnp.sum(jnp.where(eye, row, F32(0.0)), axis=1, keepdims=True)


def first_kernel(
    place_ref, mixed_ref, from_left, from_right, faces_ref, recv_ref, ws_ref, held_ref,
    spread_ref, departure_ref, a_ref, b_ref, lon_ref, lat_ref, pick_ref,
):
    halo = PASSES
    parts, own_rows, _ = mixed_ref.shape
    owners, rows, _ = recv_ref.shape
    cols = faces_ref.shape[1]
    levels = own_rows // cols
    slots = rows // 2
    total = owners * slots
    edge = halo * levels
    build_faces(faces_ref, from_left, from_right, lon_ref, lat_ref, levels)
    fill(a_ref, 0, [from_left[q * edge : (q + 1) * edge, :] for q in range(parts)])
    fill(a_ref, edge, [mixed_ref[q] for q in range(parts)])
    fill(a_ref, edge + own_rows, [from_right[q * edge : (q + 1) * edge, :] for q in range(parts)])
    diffuse(a_ref, b_ref, lon_ref, lat_ref, levels)

    def pick(o, carry):
        for k in range(slots):
            slot = o * slots + k
            row = place_ref[1, slot]
            for q in range(parts):
                pick_ref[q, pl.ds(slot, 1), :] = a_ref[q, pl.ds(row, 1), :]
        return carry

    lax.fori_loop(0, owners, pick, 0)
    value, rinv, index, valid = (unpack_meta(recv_ref, slots, field) for field in range(4))
    evolved = sum(pick_ref[q] * held_ref[q] for q in range(parts))
    evolved = jnp.sum(evolved, axis=1, keepdims=True)
    departure = jnp.where(valid > 0.5, evolved - value, F32(0.0))
    scaled = rinv * departure
    spread_ref[0:total, :] = scaled * ws_ref[...]
    spread_ref[total:, :] = jnp.zeros((spread_ref.shape[0] - total, STEN), F32)
    for j in range(total // STEN):
        part = slice(j * STEN, (j + 1) * STEN)
        spread_ref[total + j : total + j + 1, :] = to_row(index[part])
    room = departure_ref.shape
    place = jnp.zeros(room, F32)
    for j in range(room[1]):
        wanted = (iota((total, STEN), 0) & (slots - 1)) + place_ref[2, 0] * slots - j * STEN
        lanes = jnp.where(iota((total, STEN), 1) == wanted, departure, F32(0.0))
        lanes = jnp.sum(lanes.reshape(owners, slots, STEN), axis=1)
        place = jnp.where(iota(room, 1) == j, lanes[:, None, :], place)
        if (j + 1) * STEN >= owners * slots:
            break
    departure_ref[...] = place


def second_kernel(
    v_ref, control_ref, own_ref, left_ref, right_ref, faces_ref, from_left, from_right,
    out_ref, a_ref, b_ref, lon_ref, lat_ref,
):
    halo = PASSES
    levels, cols, lat = control_ref.shape
    parts = lat // STEN
    edge = halo * levels
    total = own_ref.shape[0] // STEN * STEN
    build_faces(faces_ref, from_left, from_right, lon_ref, lat_ref, levels)
    place = spread_block(lat)

    def scatter(source, first, count, step, target):
        pieces = []
        keys = []
        for j in range(total // STEN):
            index = source[total + j : total + j + 1, :].astype(jnp.int32)
            level, column, seg = block_place(index, cols, parts)
            keys.append((column - first) * levels + level)
            keep = lane_segment(STEN, lat) == to_column(seg.astype(F32)).astype(jnp.int32)
            held = [dot(piece, place) for piece in split(source[j * STEN : (j + 1) * STEN, :])]
            held = [jnp.where(keep, piece, F32(0.0)).astype(BF16) for piece in held]
            pieces.append(jnp.concatenate(held, axis=1))
        for c in range(0, count, step):
            rows = step * levels
            sums = jnp.zeros((rows, 2 * lat), F32)
            for key, piece in zip(keys, pieces):
                sums = sums + dot(onehot(iota((rows, STEN), 0) + c * levels == key), piece)
            sums = sums[:, :lat] + sums[:, lat:]
            fill(a_ref, (target + c) * levels, [sums[:, q * STEN : (q + 1) * STEN] for q in range(parts)])

    scatter(own_ref, 0, cols, 8, halo)
    scatter(left_ref, cols - halo, halo, halo // 2, 0)
    scatter(right_ref, 0, halo, halo // 2, halo + cols)
    diffuse(a_ref, b_ref, lon_ref, lat_ref, levels)
    matrix = mixing_matrix_back(v_ref[...])
    back = interleave(lat)
    group = WIDE // levels
    for g in range(cols // group):
        part = slice(g * group, (g + 1) * group)
        rows = slice(edge + g * WIDE, edge + (g + 1) * WIDE)
        x = jnp.concatenate([a_ref[q, rows, :] for q in range(parts)], axis=1)
        y = product(matrix, move(split(x), back)).reshape(levels, group, lat)
        out_ref[:, part, :] = control_ref[:, part, :] + y


def call(kernel, out_shape, specs, scratch, flops, moved, limit=VMEM_LIMIT):
    return pl.pallas_call(
        kernel,
        out_shape=out_shape,
        in_specs=specs,
        out_specs=jax.tree.map(lambda _: VMEM_SPEC, out_shape),
        scratch_shapes=list(scratch),
        cost_estimate=pl.CostEstimate(flops=flops, bytes_accessed=moved, transcendentals=0),
        compiler_params=pltpu.CompilerParams(vmem_limit_bytes=limit),
    )


def shape(*dims):
    return jax.ShapeDtypeStruct(dims, F32)


def local(
    control, std_field, kappa_lon, kappa_lat, sea_mask, vertical,
    block_index, weights, obs_value, obs_rinv, obs_count,
):
    levels, cols, lat = control.shape
    parts = lat // STEN
    owners, slots = block_index.shape[1:]
    total = owners * slots
    halo = PASSES
    width = cols + 2 * halo
    cells = width * levels * lat
    count = lax.axis_size("lon")
    to_right = [(i, (i + 1) % count) for i in range(count)]
    to_left = [((i + 1) % count, i) for i in range(count)]

    message = parts * halo * (levels + 2) + parts
    message = -(-message // 8) * 8
    plane = pltpu.VMEM((cols, lat), F32)
    hbm = pl.BlockSpec(memory_space=pltpu.HBM)
    mixed, faces, edge_left, edge_right = call(
        head_kernel,
        (
            shape(parts, cols * levels, STEN), shape(3 * parts, cols, STEN),
            shape(message, STEN), shape(message, STEN),
        ),
        [hbm] * 5,
        [
            pltpu.VMEM((cols, lat), jnp.int32), plane, plane, pltpu.VMEM((levels, levels), F32),
            pltpu.VMEM((levels, cols, lat), F32), pltpu.SemaphoreType.DMA((5,)),
        ],
        12 * cells * lat, 8 * 4 * cells, WHOLE_VMEM,
    )(sea_mask, kappa_lon, kappa_lat, vertical, control)
    from_left = lax.ppermute(edge_right, "lon", to_right)
    from_right = lax.ppermute(edge_left, "lon", to_left)

    sent = call(
        pack_kernel, shape(owners, 2 * slots, STEN), [hbm] + [VMEM_SPEC] * 5, [],
        6 * STEN * owners * STEN, 4 * 4 * total * STEN, WHOLE_VMEM,
    )(faces, block_index[0].T, obs_value[0].T, obs_rinv[0].T, obs_count, weights[0])
    recv = lax.all_to_all(sent, "lon", split_axis=0, concat_axis=0, tiled=True)
    index = recv[:, slots, 2 * slots : 3 * slots].reshape(total).astype(jnp.int32)
    level, column, _ = block_place(index, cols, parts)
    here = jnp.full((total,), lax.axis_index("lon"), jnp.int32)
    places = jnp.stack([index, (halo + column) * levels + level, here])
    ws, held = call(
        weights_kernel,
        (shape(total, STEN), shape(parts, total, STEN)),
        [SMEM_SPEC] + [VMEM_SPEC] * 3,
        [
            pltpu.VMEM((total, STEN), F32), pltpu.VMEM((levels * cols * parts, STEN), F32),
            pltpu.VMEM((cols * parts, STEN), F32),
        ],
        6 * total * STEN * lat, 4 * 4 * cells,
    )(places, recv, std_field, sea_mask)

    field = pltpu.VMEM((parts + 2, width * levels, STEN), F32)
    faces_held = [pltpu.VMEM((parts, width * 8, STEN), F32), pltpu.VMEM((parts + 1, width * 8, STEN), F32)]
    extra = -(-total // (8 * STEN)) * 8
    back = -(-total // (16 * STEN)) * 16
    spread, departure = call(
        first_kernel,
        (shape(total + extra, STEN), shape(owners, back, STEN)),
        [SMEM_SPEC] + [VMEM_SPEC] * 7,
        [field, field, *faces_held, pltpu.VMEM((parts, total, STEN), F32)],
        10 * PASSES * cells, 2 * PASSES * 4 * cells,
    )(places, mixed, from_left, from_right, faces, recv, ws, held)

    spread_left = lax.ppermute(spread, "lon", to_right)
    spread_right = lax.ppermute(spread, "lon", to_left)
    mine = lax.psum_scatter(departure, "lon", scatter_dimension=0, tiled=True)

    gradient = call(
        second_kernel, shape(levels, cols, lat), [VMEM_SPEC] * 8, [field, field, *faces_held],
        10 * PASSES * cells, 2 * PASSES * 4 * cells,
    )(vertical, control, spread, spread_left, spread_right, faces, from_left, from_right)
    gradient, mine = lax.optimization_barrier((gradient, mine))
    return gradient, mine.reshape(1, back * STEN // slots, slots)[:, :count]


def solution(mesh):
    in_specs = (
        P("grp", "lon", None),
        P(None, "lon", None),
        P("lon", None),
        P("lon", None),
        P("lon", None),
        P(),
        P(("grp", "lon"), None, None),
        P(("grp", "lon"), None, None, None),
        P(("grp", "lon"), None, None),
        P(("grp", "lon"), None, None),
        P(("grp", "lon"), None),
    )
    out_specs = (P("grp", "lon", None), P(("grp", "lon"), None, None))
    return jax.shard_map(local, mesh=mesh, in_specs=in_specs, out_specs=out_specs, check_vma=False)
```

```python
import jax
import jax.numpy as jnp
from jax import lax
from jax.experimental import pallas as pl
from jax.experimental.pallas import tpu as pltpu
from jax.sharding import PartitionSpec as P

STEN = 128
PASSES = 10
WIDE = 256
F32 = jnp.float32
BF16 = jnp.bfloat16
WHOLE_VMEM = 60 * 1024 * 1024
TIERS = ((0, 4), (4, PASSES))
VMEM_LIMIT = 24 * 1024 * 1024

VMEM_SPEC = pl.BlockSpec(memory_space=pltpu.VMEM)
SMEM_SPEC = pl.BlockSpec(memory_space=pltpu.SMEM)


def split(x):
    high = x.astype(BF16)
    return high, (x - high.astype(F32)).astype(BF16)


def split3(x):
    high = x.astype(BF16)
    rest = x - high.astype(F32)
    middle = rest.astype(BF16)
    return high, middle, (rest - middle.astype(F32)).astype(BF16)


def dot(a, b):
    return jnp.dot(a, b, preferred_element_type=F32)


def log2(n):
    assert n & (n - 1) == 0
    return n.bit_length() - 1


def iota(shape, dim):
    return lax.broadcasted_iota(jnp.int32, shape, dim)


def onehot(condition):
    return jnp.where(condition, F32(1.0), F32(0.0)).astype(BF16)


def product(left, right):
    (lh, ll), (rh, rl) = left, right
    return dot(lh, rh) + (dot(lh, rl) + dot(ll, rh))


def mixing_matrix(vertical):
    levels = vertical.shape[0]
    group = WIDE // levels
    expand = onehot(iota((levels, WIDE), 1) // group == iota((levels, WIDE), 0))
    keep = iota((WIDE, WIDE), 0) // levels == iota((WIDE, WIDE), 1) % group
    out = []
    for part in split(vertical):
        rows = dot(part, expand)
        tiled = jnp.concatenate([rows] * group, axis=0)
        out.append(jnp.where(keep, tiled, F32(0.0)).astype(BF16))
    return tuple(out)


def mixing_matrix_back(vertical):
    levels = vertical.shape[0]
    group = WIDE // levels
    spread = onehot(iota((levels, WIDE), 1) % levels == iota((levels, WIDE), 0))
    repeat = onehot(iota((WIDE, levels), 0) // group == iota((WIDE, levels), 1))
    keep = iota((WIDE, WIDE), 0) % group == iota((WIDE, WIDE), 1) // levels
    out = []
    for part in split(vertical):
        rows = lax.dot_general(part, spread, (((0,), (0,)), ((), ())), preferred_element_type=F32)
        rows = rows.astype(BF16)
        out.append(jnp.where(keep, dot(repeat, rows), F32(0.0)).astype(BF16))
    return tuple(out)


def deinterleave(lat):
    parts = lat // STEN
    target = iota((lat, lat), 1)
    return onehot(iota((lat, lat), 0) == (target % STEN) * parts + target // STEN)


def interleave(lat):
    parts = lat // STEN
    source = iota((lat, lat), 0)
    return onehot(iota((lat, lat), 1) == (source % STEN) * parts + source // STEN)


def spread_block(lat):
    parts = lat // STEN
    target = iota((STEN, lat), 1)
    return onehot(iota((STEN, lat), 0) == (target % (STEN // parts)) * parts + target // STEN)


def lane_segment(rows, lat):
    parts = lat // STEN
    return (iota((rows, lat), 1) % STEN) // (STEN // parts)


def move(x, matrix):
    return tuple(dot(part, matrix).astype(BF16) for part in x)


def pack_meta(slots, values):
    stacked = jnp.concatenate(values, axis=0)
    eye = onehot(iota((stacked.shape[0], STEN), 0) == iota((stacked.shape[0], STEN), 1))
    return sum(
        lax.dot_general(part, eye, (((0,), (0,)), ((), ())), preferred_element_type=F32)
        for part in split3(stacked)
    )


def unpack_meta(recv_ref, slots, field):
    owners = recv_ref.shape[0]
    total = owners * slots
    rows = jnp.broadcast_to(recv_ref[:, slots : slots + 1, :], (owners, slots, STEN)).reshape(total, STEN)
    wanted = (iota((total, STEN), 0) & (slots - 1)) + field * slots
    return jnp.sum(jnp.where(iota((total, STEN), 1) == wanted, rows, F32(0.0)), axis=1, keepdims=True)


def head_kernel(
    mask_hbm, klon_hbm, klat_hbm, v_hbm, control_hbm, mixed_ref, faces_ref, left_ref, right_ref,
    mask_ref, klon_ref, klat_ref, v_ref, control_ref, sems,
):
    pairs = (
        (mask_hbm, mask_ref), (klon_hbm, klon_ref), (klat_hbm, klat_ref), (v_hbm, v_ref), (control_hbm, control_ref),
    )
    copies = [pltpu.make_async_copy(source, target, sems.at[k]) for k, (source, target) in enumerate(pairs)]
    for copy in copies:
        copy.start()
    levels, cols, lat = control_ref.shape
    parts = lat // STEN
    group = WIDE // levels
    halo = PASSES
    edge = halo * levels
    place = deinterleave(lat)
    for copy in copies[:4]:
        copy.wait()
    matrix = mixing_matrix(v_ref[...])
    wet = mask_ref[...].astype(F32)
    east = jnp.where(iota((cols, lat), 0) == cols - 1, F32(1.0), pltpu.roll(wet, cols - 1, 0))
    north = jnp.where(iota((cols, lat), 1) == lat - 1, F32(0.0), pltpu.roll(wet, lat - 1, 1))
    for k, face in enumerate((klon_ref[...] * wet * east, klat_ref[...] * wet * north, wet)):
        held = sum(dot(piece, place) for piece in (split3(face) if k < 2 else (face.astype(BF16),)))
        for q in range(parts):
            faces_ref[k * parts + q] = held[:, q * STEN : (q + 1) * STEN]
    copies[4].wait()
    for g in range(cols // group):
        x = control_ref[:, g * group : (g + 1) * group, :].reshape(WIDE, lat)
        y = product(matrix, move(split(x), place))
        for q in range(parts):
            mixed_ref[q, g * WIDE : (g + 1) * WIDE, :] = y[:, q * STEN : (q + 1) * STEN]
    for out, start in ((left_ref, 0), (right_ref, cols - halo)):
        for q in range(parts):
            out[q * edge : (q + 1) * edge, :] = mixed_ref[q, start * levels : start * levels + edge, :]
        for k in range(2 * parts):
            first = parts * edge + k * halo
            out[first : first + halo, :] = faces_ref[k, start : start + halo, :]
        first = parts * edge + 2 * parts * halo
        for q in range(parts):
            out[first + q : first + q + 1, :] = faces_ref[2 * parts + q, 0:1, :]
        out[first + parts :, :] = jnp.zeros((out.shape[0] - first - parts, STEN), F32)


def pack(index_ref, value_ref, rinv_ref, count_ref, weights_ref, sent_ref):
    owners, slots, _ = weights_ref.shape
    sent_ref[:, 0:slots, :] = weights_ref[...]
    valid = jnp.where(iota((slots, owners), 0) < count_ref[...], F32(1.0), F32(0.0))
    meta = pack_meta(slots, [value_ref[...], rinv_ref[...], index_ref[...].astype(F32), valid])
    sent_ref[:, slots:, :] = jnp.broadcast_to(meta[:, None, :], (owners, slots, STEN))


def hold_faces(ref, lon_ref, lat_ref, count):
    parts = lon_ref.shape[0]
    shape = (8, STEN)
    for c in range(count):
        rows = slice(8 * c, 8 * c + 8)
        for q in range(parts):
            lat_row = ref[parts + q, c : c + 1, :]
            lon_ref[q, rows, :] = jnp.broadcast_to(ref[q, c : c + 1, :], shape)
            lat_ref[q, rows, :] = jnp.broadcast_to(lat_row, shape)
            if q == parts - 1:
                lat_ref[parts, rows, :] = jnp.broadcast_to(pltpu.roll(lat_row, 1, 1), shape)


def join_faces(faces_ref, from_left, from_right, all_ref, levels):
    halo = PASSES
    cols = faces_ref.shape[1]
    parts = faces_ref.shape[0] // 3
    first = parts * halo * levels

    def far(source, k, c):
        at = first + k * halo + c
        return source[at : at + 1, :]

    for q in range(parts):
        at = first + 2 * parts * halo + q
        for k in (q, parts + q):
            all_ref[k, 0:halo, :] = from_left[first + k * halo : first + (k + 1) * halo, :]
            all_ref[k, halo : halo + cols, :] = faces_ref[k]
            all_ref[k, halo + cols : 2 * halo + cols, :] = from_right[first + k * halo : first + (k + 1) * halo, :]
        all_ref[q, halo - 1 : halo, :] = far(from_left, q, halo - 1) * faces_ref[2 * parts + q, 0:1, :]
        all_ref[q, halo + cols - 1 : halo + cols, :] = faces_ref[q, cols - 1 : cols, :] * from_right[at : at + 1, :]


def add_ghosts(ref, first, values):
    count = values[0].shape[0]
    parts = len(values)
    ref[parts, first : first + count, :] = pltpu.roll(values[0], STEN - 1, 1)
    ref[parts + 1, first : first + count, :] = pltpu.roll(values[-1], 1, 1)


def fill(ref, first, values):
    for q, value in enumerate(values):
        ref[q, first : first + value.shape[0], :] = value
    add_ghosts(ref, first, values)


def column_steps(src, dst, lon_ref, lat_ref, levels, low, high, step=0, face=0):
    parts = lon_ref.shape[0]
    halves = range(levels // 8)

    def load(k, c, h):
        return src[k, c * levels + 8 * h : c * levels + 8 * h + 8, :]

    def rate(ref, k, c):
        return ref[k, pl.ds(pl.multiple_of(8 * (c + face), 8), 8), :]

    here = [[load(q, low, h) for q in range(parts)] for h in halves]
    west = [[rate(lon_ref, q, low - 1) * (here[h][q] - load(q, low - 1, h)) for q in range(parts)] for h in halves]
    for c in range(low, high):
        lon = [rate(lon_ref, q, c) for q in range(parts)]
        lat = [rate(lat_ref, q, c) for q in range(parts + 1)]
        for h in halves:
            line = here[h]
            east = [load(q, c + 1, h) for q in range(parts)]
            flux_east = [lon[q] * (east[q] - line[q]) for q in range(parts)]
            ahead = line[1:] + [load(parts, c, h)]
            flux_north = [lat[parts] * (line[0] - load(parts + 1, c, h))]
            flux_north += [lat[q] * (ahead[q] - line[q]) for q in range(parts)]
            out = [
                line[q] + (flux_east[q] - west[h][q]) + (flux_north[q + 1] - flux_north[q])
                for q in range(parts)
            ]
            first = (c + step) * levels + 8 * h
            for q in range(parts):
                dst[q, first : first + 8, :] = out[q]
            add_ghosts(dst, first, out)
            here[h], west[h] = east, flux_east


def diffuse(a_ref, b_ref, lon_ref, lat_ref, levels, before_pass=None):
    width = a_ref.shape[1] // levels

    for first, last in TIERS:

        def pair(turn, carry):
            for k, (src, dst) in enumerate(((a_ref, b_ref), (b_ref, a_ref))):
                if before_pass is not None:
                    before_pass(2 * turn + k, src)
                column_steps(src, dst, lon_ref, lat_ref, levels, first + 1 + k, width - first - 1 - k)
            return carry

        lax.fori_loop(first // 2, last // 2, pair, 0)


def inner_kernel(
    mixed_ref, faces_ref, index_ref, value_ref, rinv_ref, count_ref, weights_ref,
    inner_ref, strips_ref, sent_ref, a_ref, b_ref, lon_ref, lat_ref,
):
    parts, own_rows, _ = mixed_ref.shape
    cols = faces_ref.shape[1]
    levels = own_rows // cols
    pack(index_ref, value_ref, rinv_ref, count_ref, weights_ref, sent_ref)
    hold_faces(faces_ref, lon_ref, lat_ref, cols)
    fill(a_ref, 0, [mixed_ref[q] for q in range(parts)])

    def save(turn, src):
        for side, (line, other) in enumerate(((turn, turn + 1), (cols - 1 - turn, cols - 2 - turn))):
            line = pl.ds(pl.multiple_of(line * levels, levels), levels)
            other = pl.ds(pl.multiple_of(other * levels, levels), levels)
            for q in range(parts):
                strips_ref[turn, side, q] = src[q, line, :]
                strips_ref[turn, side, parts + q] = src[q, other, :]

    diffuse(a_ref, b_ref, lon_ref, lat_ref, levels, save)
    for q in range(parts):
        inner_ref[q] = a_ref[q, PASSES * levels : (cols - PASSES) * levels, :]


def block_place(index, cols, parts):
    return (
        lax.shift_right_logical(index, log2(cols * parts)),
        lax.shift_right_logical(index, log2(parts)) & (cols - 1),
        index & (parts - 1),
    )


def weights_kernel(place_ref, recv_ref, std_ref, mask_ref, out_ref, held_ref, pick_ref, std_rows, wet_rows):
    owners, rows, _ = recv_ref.shape
    slots = rows // 2
    total = owners * slots
    levels, cols, lat = std_ref.shape
    parts = lat // STEN
    for s in range(parts):
        part = slice(s * STEN, (s + 1) * STEN)
        wet_rows[s * cols : (s + 1) * cols, :] = mask_ref[:, part].astype(F32)
        for a in range(levels):
            first = (a * parts + s) * cols
            std_rows[first : first + cols, :] = std_ref[a, :, part]

    def pick(o, carry):
        for k in range(slots):
            slot = o * slots + k
            level, column, seg = block_place(place_ref[0, slot], cols, parts)
            value = std_rows[pl.ds((level * parts + seg) * cols + column, 1), :]
            wet = wet_rows[pl.ds(seg * cols + column, 1), :]
            pick_ref[pl.ds(slot, 1), :] = value * wet
        return carry

    lax.fori_loop(0, owners, pick, 0)
    ws = recv_ref[:, 0:slots, :].reshape(total, STEN) * pick_ref[...]
    out_ref[...] = ws
    place = spread_block(lat)
    segs = unpack_meta(recv_ref, slots, 2).astype(jnp.int32) & (parts - 1)
    for j in range(total // STEN):
        part = slice(j * STEN, (j + 1) * STEN)
        seg = segs[part]
        held = sum(dot(piece, place) for piece in split3(ws[part]))
        held = jnp.where(lane_segment(STEN, lat) == seg, held, F32(0.0))
        for q in range(parts):
            held_ref[q, part, :] = held[:, q * STEN : (q + 1) * STEN]


def to_row(column):
    eye = iota((STEN, STEN), 0) == iota((STEN, STEN), 1)
    return jnp.sum(jnp.where(eye, column, F32(0.0)), axis=0, keepdims=True)


def to_column(row):
    eye = iota((STEN, STEN), 0) == iota((STEN, STEN), 1)
    return jnp.sum(jnp.where(eye, row, F32(0.0)), axis=1, keepdims=True)


def edge_kernel(
    inner_ref, strips_ref, from_left, from_right, faces_ref,
    rows_ref, all_ref, left_a, left_b, right_a, right_b, lon_ref, lat_ref,
):
    halo = PASSES
    levels = strips_ref.shape[3]
    parts = inner_ref.shape[0]
    cols = faces_ref.shape[1]
    edge = halo * levels
    join_faces(faces_ref, from_left, from_right, all_ref, levels)
    hold_faces(all_ref, lon_ref, lat_ref, cols + 2 * halo)
    fill(left_a, 0, [from_left[q * edge : (q + 1) * edge, :] for q in range(parts)])
    fill(right_a, 2 * levels, [from_right[q * edge : (q + 1) * edge, :] for q in range(parts)])

    def pair(turn, carry):
        for k, (left, left_to, right, right_to) in enumerate(
            ((left_a, left_b, right_a, right_b), (left_b, left_a, right_b, right_a))
        ):
            now = 2 * turn + k
            for side, ref, line, other in ((0, left, halo, halo + 1), (1, right, 1, 0)):
                fill(ref, line * levels, [strips_ref[now, side, q] for q in range(parts)])
                for q in range(parts):
                    ref[q, other * levels : (other + 1) * levels, :] = strips_ref[now, side, parts + q]
            column_steps(left, left_to, lon_ref, lat_ref, levels, 1, halo + 1, -1, now)
            column_steps(right, right_to, lon_ref, lat_ref, levels, 1, halo + 1, 1, halo + cols - 2 - now)
        return carry

    lax.fori_loop(0, PASSES // 2, pair, 0)
    for q in range(parts):
        rows_ref[q, 0:edge, :] = left_a[q, 0:edge, :]
        rows_ref[q, edge : cols * levels - edge, :] = inner_ref[q]
        rows_ref[q, cols * levels - edge :, :] = right_a[q, 2 * levels : 2 * levels + edge, :]


def departure_kernel(place_ref, rows_ref, recv_ref, ws_ref, held_ref, spread_ref, departure_ref, pick_ref):
    parts = rows_ref.shape[0]
    owners, rows, _ = recv_ref.shape
    slots = rows // 2
    total = owners * slots

    def pick(o, carry):
        for k in range(slots):
            slot = o * slots + k
            row = place_ref[1, slot]
            for q in range(parts):
                pick_ref[q, pl.ds(slot, 1), :] = rows_ref[q, pl.ds(row, 1), :]
        return carry

    lax.fori_loop(0, owners, pick, 0)
    value, rinv, index, valid = (unpack_meta(recv_ref, slots, field) for field in range(4))
    evolved = sum(pick_ref[q] * held_ref[q] for q in range(parts))
    evolved = jnp.sum(evolved, axis=1, keepdims=True)
    departure = jnp.where(valid > 0.5, evolved - value, F32(0.0))
    scaled = rinv * departure
    spread_ref[0:total, :] = scaled * ws_ref[...]
    spread_ref[total:, :] = jnp.zeros((spread_ref.shape[0] - total, STEN), F32)
    for j in range(total // STEN):
        part = slice(j * STEN, (j + 1) * STEN)
        spread_ref[total + j : total + j + 1, :] = to_row(index[part])
    lanes = jnp.where(iota((total, STEN), 1) == (iota((total, STEN), 0) & (slots - 1)), departure, F32(0.0))
    departure_ref[...] = jnp.sum(lanes.reshape(owners, slots, STEN), axis=1)


def second_kernel(
    v_ref, control_ref, own_ref, left_ref, right_ref, all_ref,
    out_ref, a_ref, b_ref, lon_ref, lat_ref,
):
    halo = PASSES
    levels, cols, lat = control_ref.shape
    parts = lat // STEN
    edge = halo * levels
    total = own_ref.shape[0] // STEN * STEN
    hold_faces(all_ref, lon_ref, lat_ref, cols + 2 * halo)
    place = spread_block(lat)

    def scatter(source, first, count, step, target):
        pieces = []
        keys = []
        for j in range(total // STEN):
            index = source[total + j : total + j + 1, :].astype(jnp.int32)
            level, column, seg = block_place(index, cols, parts)
            keys.append((column - first) * levels + level)
            keep = lane_segment(STEN, lat) == to_column(seg.astype(F32)).astype(jnp.int32)
            held = [dot(piece, place) for piece in split(source[j * STEN : (j + 1) * STEN, :])]
            held = [jnp.where(keep, piece, F32(0.0)).astype(BF16) for piece in held]
            pieces.append(jnp.concatenate(held, axis=1))
        for c in range(0, count, step):
            rows = step * levels
            sums = jnp.zeros((rows, 2 * lat), F32)
            for key, piece in zip(keys, pieces):
                sums = sums + dot(onehot(iota((rows, STEN), 0) + c * levels == key), piece)
            sums = sums[:, :lat] + sums[:, lat:]
            fill(a_ref, (target + c) * levels, [sums[:, q * STEN : (q + 1) * STEN] for q in range(parts)])

    scatter(own_ref, 0, cols, 8, halo)
    scatter(left_ref, cols - halo, halo, halo // 2, 0)
    scatter(right_ref, 0, halo, halo // 2, halo + cols)
    diffuse(a_ref, b_ref, lon_ref, lat_ref, levels)
    matrix = mixing_matrix_back(v_ref[...])
    back = interleave(lat)
    group = WIDE // levels
    for g in range(cols // group):
        part = slice(g * group, (g + 1) * group)
        rows = slice(edge + g * WIDE, edge + (g + 1) * WIDE)
        x = jnp.concatenate([a_ref[q, rows, :] for q in range(parts)], axis=1)
        y = product(matrix, move(split(x), back)).reshape(levels, group, lat)
        out_ref[:, part, :] = control_ref[:, part, :] + y


def call(kernel, out_shape, specs, scratch, flops, moved, limit=VMEM_LIMIT):
    return pl.pallas_call(
        kernel,
        out_shape=out_shape,
        in_specs=specs,
        out_specs=jax.tree.map(lambda _: VMEM_SPEC, out_shape),
        scratch_shapes=list(scratch),
        cost_estimate=pl.CostEstimate(flops=flops, bytes_accessed=moved, transcendentals=0),
        compiler_params=pltpu.CompilerParams(vmem_limit_bytes=limit),
    )


def shape(*dims):
    return jax.ShapeDtypeStruct(dims, F32)


def local(
    control, std_field, kappa_lon, kappa_lat, sea_mask, vertical,
    block_index, weights, obs_value, obs_rinv, obs_count,
):
    levels, cols, lat = control.shape
    parts = lat // STEN
    owners, slots = block_index.shape[1:]
    total = owners * slots
    halo = PASSES
    width = cols + 2 * halo
    cells = width * levels * lat
    count = lax.axis_size("lon")
    to_right = [(i, (i + 1) % count) for i in range(count)]
    to_left = [((i + 1) % count, i) for i in range(count)]

    message = parts * halo * (levels + 2) + parts
    message = -(-message // 8) * 8
    plane = pltpu.VMEM((cols, lat), F32)
    hbm = pl.BlockSpec(memory_space=pltpu.HBM)
    mixed, faces, edge_left, edge_right = call(
        head_kernel,
        (
            shape(parts, cols * levels, STEN), shape(3 * parts, cols, STEN),
            shape(message, STEN), shape(message, STEN),
        ),
        [hbm] * 5,
        [
            pltpu.VMEM((cols, lat), jnp.int32), plane, plane, pltpu.VMEM((levels, levels), F32),
            pltpu.VMEM((levels, cols, lat), F32), pltpu.SemaphoreType.DMA((5,)),
        ],
        12 * cells * lat, 8 * 4 * cells, WHOLE_VMEM,
    )(sea_mask, kappa_lon, kappa_lat, vertical, control)
    from_left = lax.ppermute(edge_right, "lon", to_right)
    from_right = lax.ppermute(edge_left, "lon", to_left)

    inside = pltpu.VMEM((parts + 2, cols * levels, STEN), F32)
    wedge = pltpu.VMEM((parts + 2, (halo + 2) * levels, STEN), F32)
    inner, strips, sent = call(
        inner_kernel,
        (
            shape(parts, (cols - 2 * halo) * levels, STEN), shape(PASSES, 2, 2 * parts, levels, STEN),
            shape(owners, 2 * slots, STEN),
        ),
        [VMEM_SPEC] * 7,
        [
            inside, inside,
            pltpu.VMEM((parts, cols * 8, STEN), F32), pltpu.VMEM((parts + 1, cols * 8, STEN), F32),
        ],
        5 * PASSES * cells, PASSES * 4 * cells,
    )(
        mixed, faces, block_index[0].T, obs_value[0].T, obs_rinv[0].T, obs_count, weights[0]
    )
    recv = lax.all_to_all(sent, "lon", split_axis=0, concat_axis=0, tiled=True)
    field = pltpu.VMEM((parts + 2, width * levels, STEN), F32)
    faces_held = [pltpu.VMEM((parts, width * 8, STEN), F32), pltpu.VMEM((parts + 1, width * 8, STEN), F32)]
    rows, all_faces = call(
        edge_kernel,
        (shape(parts, cols * levels, STEN), shape(2 * parts, -(-width // 8) * 8, STEN)),
        [VMEM_SPEC] * 5,
        [wedge, wedge, wedge, wedge, *faces_held],
        5 * PASSES * cells, PASSES * 4 * cells,
    )(inner, strips, from_left, from_right, faces)
    recv, rows = lax.optimization_barrier((recv, rows))
    index = recv[:, slots, 2 * slots : 3 * slots].reshape(total).astype(jnp.int32)
    level, column, _ = block_place(index, cols, parts)
    places = jnp.stack([index, column * levels + level])
    ws, held = call(
        weights_kernel,
        (shape(total, STEN), shape(parts, total, STEN)),
        [SMEM_SPEC] + [VMEM_SPEC] * 3,
        [
            pltpu.VMEM((total, STEN), F32), pltpu.VMEM((levels * cols * parts, STEN), F32),
            pltpu.VMEM((cols * parts, STEN), F32),
        ],
        6 * total * STEN * lat, 4 * 4 * cells,
    )(places, recv, std_field, sea_mask)

    extra = -(-total // (8 * STEN)) * 8
    spread, departure = call(
        departure_kernel,
        (shape(total + extra, STEN), shape(owners, STEN)),
        [SMEM_SPEC] + [VMEM_SPEC] * 4,
        [pltpu.VMEM((parts, total, STEN), F32)],
        8 * total * lat, 4 * 4 * total * lat,
    )(places, rows, recv, ws, held)

    spread_left = lax.ppermute(spread, "lon", to_right)
    spread_right = lax.ppermute(spread, "lon", to_left)
    mine = lax.all_to_all(departure[:, None, :], "lon", split_axis=0, concat_axis=0, tiled=True)

    gradient = call(
        second_kernel, shape(levels, cols, lat), [VMEM_SPEC] * 6, [field, field, *faces_held],
        10 * PASSES * cells, 2 * PASSES * 4 * cells,
    )(vertical, control, spread, spread_left, spread_right, all_faces)
    gradient, mine = lax.optimization_barrier((gradient, mine))
    return gradient, mine[:, 0, :slots][None]


def solution(mesh):
    in_specs = (
        P("grp", "lon", None),
        P(None, "lon", None),
        P("lon", None),
        P("lon", None),
        P("lon", None),
        P(),
        P(("grp", "lon"), None, None),
        P(("grp", "lon"), None, None, None),
        P(("grp", "lon"), None, None),
        P(("grp", "lon"), None, None),
        P(("grp", "lon"), None),
    )
    out_specs = (P("grp", "lon", None), P(("grp", "lon"), None, None))
    return jax.shard_map(local, mesh=mesh, in_specs=in_specs, out_specs=out_specs, check_vma=False)
```

```python
import jax
import jax.numpy as jnp
from jax import lax
from jax.experimental import pallas as pl
from jax.experimental.pallas import tpu as pltpu
from jax.sharding import PartitionSpec as P

STEN = 128
PASSES = 10
WIDE = 256
F32 = jnp.float32
BF16 = jnp.bfloat16
WHOLE_VMEM = 60 * 1024 * 1024
TIERS = ((0, 4), (4, PASSES))
VMEM_LIMIT = 24 * 1024 * 1024

VMEM_SPEC = pl.BlockSpec(memory_space=pltpu.VMEM)
SMEM_SPEC = pl.BlockSpec(memory_space=pltpu.SMEM)


def split(x):
    high = x.astype(BF16)
    return high, (x - high.astype(F32)).astype(BF16)


def split3(x):
    high = x.astype(BF16)
    rest = x - high.astype(F32)
    middle = rest.astype(BF16)
    return high, middle, (rest - middle.astype(F32)).astype(BF16)


def dot(a, b):
    return jnp.dot(a, b, preferred_element_type=F32)


def log2(n):
    assert n & (n - 1) == 0
    return n.bit_length() - 1


def iota(shape, dim):
    return lax.broadcasted_iota(jnp.int32, shape, dim)


def onehot(condition):
    return jnp.where(condition, F32(1.0), F32(0.0)).astype(BF16)


def product(left, right):
    (lh, ll), (rh, rl) = left, right
    return dot(lh, rh) + (dot(lh, rl) + dot(ll, rh))


def mixing_matrix(vertical):
    levels = vertical.shape[0]
    group = WIDE // levels
    expand = onehot(iota((levels, WIDE), 1) // group == iota((levels, WIDE), 0))
    keep = iota((WIDE, WIDE), 0) // levels == iota((WIDE, WIDE), 1) % group
    out = []
    for part in split(vertical):
        rows = dot(part, expand)
        tiled = jnp.concatenate([rows] * group, axis=0)
        out.append(jnp.where(keep, tiled, F32(0.0)).astype(BF16))
    return tuple(out)


def mixing_matrix_back(vertical):
    levels = vertical.shape[0]
    group = WIDE // levels
    spread = onehot(iota((levels, WIDE), 1) % levels == iota((levels, WIDE), 0))
    repeat = onehot(iota((WIDE, levels), 0) // group == iota((WIDE, levels), 1))
    keep = iota((WIDE, WIDE), 0) % group == iota((WIDE, WIDE), 1) // levels
    out = []
    for part in split(vertical):
        rows = lax.dot_general(part, spread, (((0,), (0,)), ((), ())), preferred_element_type=F32)
        rows = rows.astype(BF16)
        out.append(jnp.where(keep, dot(repeat, rows), F32(0.0)).astype(BF16))
    return tuple(out)


def deinterleave(lat):
    parts = lat // STEN
    target = iota((lat, lat), 1)
    return onehot(iota((lat, lat), 0) == (target % STEN) * parts + target // STEN)


def interleave(lat):
    parts = lat // STEN
    source = iota((lat, lat), 0)
    return onehot(iota((lat, lat), 1) == (source % STEN) * parts + source // STEN)


def spread_block(lat):
    parts = lat // STEN
    target = iota((STEN, lat), 1)
    return onehot(iota((STEN, lat), 0) == (target % (STEN // parts)) * parts + target // STEN)


def lane_segment(rows, lat):
    parts = lat // STEN
    return (iota((rows, lat), 1) % STEN) // (STEN // parts)


def move(x, matrix):
    return tuple(dot(part, matrix).astype(BF16) for part in x)


def pack_meta(slots, values):
    stacked = jnp.concatenate(values, axis=0)
    eye = onehot(iota((stacked.shape[0], STEN), 0) == iota((stacked.shape[0], STEN), 1))
    return sum(
        lax.dot_general(part, eye, (((0,), (0,)), ((), ())), preferred_element_type=F32)
        for part in split3(stacked)
    )


def unpack_meta(recv_ref, slots, field):
    owners = recv_ref.shape[0]
    total = owners * slots
    rows = jnp.broadcast_to(recv_ref[:, slots : slots + 1, :], (owners, slots, STEN)).reshape(total, STEN)
    wanted = (iota((total, STEN), 0) & (slots - 1)) + field * slots
    return jnp.sum(jnp.where(iota((total, STEN), 1) == wanted, rows, F32(0.0)), axis=1, keepdims=True)


def head_kernel(
    mask_hbm, klon_hbm, klat_hbm, v_hbm, control_hbm, mixed_ref, faces_ref, left_ref, right_ref,
    mask_ref, klon_ref, klat_ref, v_ref, control_ref, sems,
):
    pairs = (
        (mask_hbm, mask_ref), (klon_hbm, klon_ref), (klat_hbm, klat_ref), (v_hbm, v_ref), (control_hbm, control_ref),
    )
    copies = [pltpu.make_async_copy(source, target, sems.at[k]) for k, (source, target) in enumerate(pairs)]
    for copy in copies:
        copy.start()
    levels, cols, lat = control_ref.shape
    parts = lat // STEN
    group = WIDE // levels
    halo = PASSES
    edge = halo * levels
    place = deinterleave(lat)
    for copy in copies[:4]:
        copy.wait()
    matrix = mixing_matrix(v_ref[...])
    wet = mask_ref[...].astype(F32)
    east = jnp.where(iota((cols, lat), 0) == cols - 1, F32(1.0), pltpu.roll(wet, cols - 1, 0))
    north = jnp.where(iota((cols, lat), 1) == lat - 1, F32(0.0), pltpu.roll(wet, lat - 1, 1))
    for k, face in enumerate((klon_ref[...] * wet * east, klat_ref[...] * wet * north, wet)):
        held = sum(dot(piece, place) for piece in (split3(face) if k < 2 else (face.astype(BF16),)))
        for q in range(parts):
            faces_ref[k * parts + q] = held[:, q * STEN : (q + 1) * STEN]
    copies[4].wait()
    for g in range(cols // group):
        x = control_ref[:, g * group : (g + 1) * group, :].reshape(WIDE, lat)
        y = product(matrix, move(split(x), place))
        for q in range(parts):
            mixed_ref[q, g * WIDE : (g + 1) * WIDE, :] = y[:, q * STEN : (q + 1) * STEN]
    for out, start in ((left_ref, 0), (right_ref, cols - halo)):
        for q in range(parts):
            out[q * edge : (q + 1) * edge, :] = mixed_ref[q, start * levels : start * levels + edge, :]
        for k in range(2 * parts):
            first = parts * edge + k * halo
            out[first : first + halo, :] = faces_ref[k, start : start + halo, :]
        first = parts * edge + 2 * parts * halo
        for q in range(parts):
            out[first + q : first + q + 1, :] = faces_ref[2 * parts + q, 0:1, :]
        out[first + parts :, :] = jnp.zeros((out.shape[0] - first - parts, STEN), F32)


def pack(index_ref, value_ref, rinv_ref, count_ref, weights_ref, sent_ref):
    owners, slots, _ = weights_ref.shape
    sent_ref[:, 0:slots, :] = weights_ref[...]
    valid = jnp.where(iota((slots, owners), 0) < count_ref[...], F32(1.0), F32(0.0))
    meta = pack_meta(slots, [value_ref[...], rinv_ref[...], index_ref[...].astype(F32), valid])
    sent_ref[:, slots:, :] = jnp.broadcast_to(meta[:, None, :], (owners, slots, STEN))


def hold_faces(ref, lon_ref, lat_ref, count):
    parts = lon_ref.shape[0]
    shape = (8, STEN)
    for c in range(count):
        rows = slice(8 * c, 8 * c + 8)
        for q in range(parts):
            lat_row = ref[parts + q, c : c + 1, :]
            lon_ref[q, rows, :] = jnp.broadcast_to(ref[q, c : c + 1, :], shape)
            lat_ref[q, rows, :] = jnp.broadcast_to(lat_row, shape)
            if q == parts - 1:
                lat_ref[parts, rows, :] = jnp.broadcast_to(pltpu.roll(lat_row, 1, 1), shape)


def join_faces(faces_ref, from_left, from_right, all_ref, levels):
    halo = PASSES
    cols = faces_ref.shape[1]
    parts = faces_ref.shape[0] // 3
    first = parts * halo * levels

    def far(source, k, c):
        at = first + k * halo + c
        return source[at : at + 1, :]

    for q in range(parts):
        at = first + 2 * parts * halo + q
        for k in (q, parts + q):
            all_ref[k, 0:halo, :] = from_left[first + k * halo : first + (k + 1) * halo, :]
            all_ref[k, halo : halo + cols, :] = faces_ref[k]
            all_ref[k, halo + cols : 2 * halo + cols, :] = from_right[first + k * halo : first + (k + 1) * halo, :]
        all_ref[q, halo - 1 : halo, :] = far(from_left, q, halo - 1) * faces_ref[2 * parts + q, 0:1, :]
        all_ref[q, halo + cols - 1 : halo + cols, :] = faces_ref[q, cols - 1 : cols, :] * from_right[at : at + 1, :]


def add_ghosts(ref, first, values):
    count = values[0].shape[0]
    parts = len(values)
    ref[parts, first : first + count, :] = pltpu.roll(values[0], STEN - 1, 1)
    ref[parts + 1, first : first + count, :] = pltpu.roll(values[-1], 1, 1)


def fill(ref, first, values):
    for q, value in enumerate(values):
        ref[q, first : first + value.shape[0], :] = value
    add_ghosts(ref, first, values)


def column_steps(src, dst, lon_ref, lat_ref, levels, low, high, step=0, face=0):
    parts = lon_ref.shape[0]
    halves = range(levels // 8)

    def load(k, c, h):
        return src[k, c * levels + 8 * h : c * levels + 8 * h + 8, :]

    def rate(ref, k, c):
        return ref[k, pl.ds(pl.multiple_of(8 * (c + face), 8), 8), :]

    here = [[load(q, low, h) for q in range(parts)] for h in halves]
    west = [[rate(lon_ref, q, low - 1) * (here[h][q] - load(q, low - 1, h)) for q in range(parts)] for h in halves]
    for c in range(low, high):
        lon = [rate(lon_ref, q, c) for q in range(parts)]
        lat = [rate(lat_ref, q, c) for q in range(parts + 1)]
        for h in halves:
            line = here[h]
            east = [load(q, c + 1, h) for q in range(parts)]
            flux_east = [lon[q] * (east[q] - line[q]) for q in range(parts)]
            ahead = line[1:] + [load(parts, c, h)]
            flux_north = [lat[parts] * (line[0] - load(parts + 1, c, h))]
            flux_north += [lat[q] * (ahead[q] - line[q]) for q in range(parts)]
            out = [
                line[q] + (flux_east[q] - west[h][q]) + (flux_north[q + 1] - flux_north[q])
                for q in range(parts)
            ]
            first = (c + step) * levels + 8 * h
            for q in range(parts):
                dst[q, first : first + 8, :] = out[q]
            add_ghosts(dst, first, out)
            here[h], west[h] = east, flux_east


def diffuse(a_ref, b_ref, lon_ref, lat_ref, levels, before_pass=None):
    width = a_ref.shape[1] // levels

    for first, last in TIERS:

        def pair(turn, carry):
            for k, (src, dst) in enumerate(((a_ref, b_ref), (b_ref, a_ref))):
                if before_pass is not None:
                    before_pass(2 * turn + k, src)
                column_steps(src, dst, lon_ref, lat_ref, levels, first + 1 + k, width - first - 1 - k)
            return carry

        lax.fori_loop(first // 2, last // 2, pair, 0)


def inner_kernel(
    ready, faces_ref, mixed_ref, index_ref, value_ref, rinv_ref, count_ref, weights_ref,
    inner_ref, strips_ref, sent_ref, a_ref, b_ref, lon_ref, lat_ref,
):
    parts, own_rows, _ = mixed_ref.shape
    cols = faces_ref.shape[1]
    levels = own_rows // cols
    ready(1)
    hold_faces(faces_ref, lon_ref, lat_ref, cols)
    ready()
    pack(index_ref, value_ref, rinv_ref, count_ref, weights_ref, sent_ref)
    fill(a_ref, 0, [mixed_ref[q] for q in range(parts)])

    def save(turn, src):
        for side, (line, other) in enumerate(((turn, turn + 1), (cols - 1 - turn, cols - 2 - turn))):
            line = pl.ds(pl.multiple_of(line * levels, levels), levels)
            other = pl.ds(pl.multiple_of(other * levels, levels), levels)
            for q in range(parts):
                strips_ref[turn, side, q] = src[q, line, :]
                strips_ref[turn, side, parts + q] = src[q, other, :]

    diffuse(a_ref, b_ref, lon_ref, lat_ref, levels, save)
    for q in range(parts):
        inner_ref[q] = a_ref[q, PASSES * levels : (cols - PASSES) * levels, :]


def block_place(index, cols, parts):
    return (
        lax.shift_right_logical(index, log2(cols * parts)),
        lax.shift_right_logical(index, log2(parts)) & (cols - 1),
        index & (parts - 1),
    )


def to_row(column):
    eye = iota((STEN, STEN), 0) == iota((STEN, STEN), 1)
    return jnp.sum(jnp.where(eye, column, F32(0.0)), axis=0, keepdims=True)


def to_column(row):
    eye = iota((STEN, STEN), 0) == iota((STEN, STEN), 1)
    return jnp.sum(jnp.where(eye, row, F32(0.0)), axis=1, keepdims=True)


def departure_kernel(
    ready, place_ref, mask_ref, std_ref, recv_ref, rows_ref,
    spread_ref, departure_ref, ws_ref, held_ref, pick_ref, line_ref, std_rows, wet_rows,
):
    owners, rows, _ = recv_ref.shape
    slots = rows // 2
    total = owners * slots
    levels, cols, lat = std_ref.shape
    parts = lat // STEN
    ready(2)
    for s in range(parts):
        part = slice(s * STEN, (s + 1) * STEN)
        wet_rows[s * cols : (s + 1) * cols, :] = mask_ref[:, part].astype(F32)
        for a in range(levels):
            first = (a * parts + s) * cols
            std_rows[first : first + cols, :] = std_ref[a, :, part]

    def pick(o, carry):
        for k in range(slots):
            slot = o * slots + k
            level, column, seg = block_place(place_ref[0, slot], cols, parts)
            value = std_rows[pl.ds((level * parts + seg) * cols + column, 1), :]
            wet = wet_rows[pl.ds(seg * cols + column, 1), :]
            pick_ref[pl.ds(slot, 1), :] = value * wet
        return carry

    ready()
    lax.fori_loop(0, owners, pick, 0)
    ws = recv_ref[:, 0:slots, :].reshape(total, STEN) * pick_ref[...]
    ws_ref[...] = ws
    place = spread_block(lat)
    segs = unpack_meta(recv_ref, slots, 2).astype(jnp.int32) & (parts - 1)
    for j in range(total // STEN):
        part = slice(j * STEN, (j + 1) * STEN)
        seg = segs[part]
        held = sum(dot(piece, place) for piece in split3(ws[part]))
        held = jnp.where(lane_segment(STEN, lat) == seg, held, F32(0.0))
        for q in range(parts):
            held_ref[q, part, :] = held[:, q * STEN : (q + 1) * STEN]

    def pick_line(o, carry):
        for k in range(slots):
            slot = o * slots + k
            row = place_ref[1, slot]
            for q in range(parts):
                line_ref[q, pl.ds(slot, 1), :] = rows_ref[q, pl.ds(row, 1), :]
        return carry

    lax.fori_loop(0, owners, pick_line, 0)
    value, rinv, index, valid = (unpack_meta(recv_ref, slots, field) for field in range(4))
    evolved = sum(line_ref[q] * held_ref[q] for q in range(parts))
    evolved = jnp.sum(evolved, axis=1, keepdims=True)
    departure = jnp.where(valid > 0.5, evolved - value, F32(0.0))
    scaled = rinv * departure
    spread_ref[0:total, :] = scaled * ws_ref[...]
    spread_ref[total:, :] = jnp.zeros((spread_ref.shape[0] - total, STEN), F32)
    for j in range(total // STEN):
        part = slice(j * STEN, (j + 1) * STEN)
        spread_ref[total + j : total + j + 1, :] = to_row(index[part])
    lanes = jnp.where(iota((total, STEN), 1) == (iota((total, STEN), 0) & (slots - 1)), departure, F32(0.0))
    departure_ref[...] = jnp.sum(lanes.reshape(owners, slots, STEN), axis=1)


def edge_kernel(
    ready, faces_ref, from_left, from_right, strips_ref, inner_ref,
    rows_ref, all_ref, left_a, left_b, right_a, right_b, lon_ref, lat_ref,
):
    halo = PASSES
    levels = strips_ref.shape[3]
    parts = inner_ref.shape[0]
    cols = faces_ref.shape[1]
    edge = halo * levels
    ready(3)
    join_faces(faces_ref, from_left, from_right, all_ref, levels)
    hold_faces(all_ref, lon_ref, lat_ref, cols + 2 * halo)
    fill(left_a, 0, [from_left[q * edge : (q + 1) * edge, :] for q in range(parts)])
    fill(right_a, 2 * levels, [from_right[q * edge : (q + 1) * edge, :] for q in range(parts)])

    ready()

    def pair(turn, carry):
        for k, (left, left_to, right, right_to) in enumerate(
            ((left_a, left_b, right_a, right_b), (left_b, left_a, right_b, right_a))
        ):
            now = 2 * turn + k
            for side, ref, line, other in ((0, left, halo, halo + 1), (1, right, 1, 0)):
                fill(ref, line * levels, [strips_ref[now, side, q] for q in range(parts)])
                for q in range(parts):
                    ref[q, other * levels : (other + 1) * levels, :] = strips_ref[now, side, parts + q]
            column_steps(left, left_to, lon_ref, lat_ref, levels, 1, halo + 1, -1, now)
            column_steps(right, right_to, lon_ref, lat_ref, levels, 1, halo + 1, 1, halo + cols - 2 - now)
        return carry

    lax.fori_loop(0, PASSES // 2, pair, 0)
    for q in range(parts):
        rows_ref[q, 0:edge, :] = left_a[q, 0:edge, :]
        rows_ref[q, edge : cols * levels - edge, :] = inner_ref[q]
        rows_ref[q, cols * levels - edge :, :] = right_a[q, 2 * levels : 2 * levels + edge, :]


def second_kernel(
    v_ref, control_ref, own_ref, left_ref, right_ref, all_ref,
    out_ref, a_ref, b_ref, lon_ref, lat_ref,
):
    halo = PASSES
    levels, cols, lat = control_ref.shape
    parts = lat // STEN
    edge = halo * levels
    total = own_ref.shape[0] // STEN * STEN
    hold_faces(all_ref, lon_ref, lat_ref, cols + 2 * halo)
    place = spread_block(lat)

    def scatter(source, first, count, step, target):
        pieces = []
        keys = []
        for j in range(total // STEN):
            index = source[total + j : total + j + 1, :].astype(jnp.int32)
            level, column, seg = block_place(index, cols, parts)
            keys.append((column - first) * levels + level)
            keep = lane_segment(STEN, lat) == to_column(seg.astype(F32)).astype(jnp.int32)
            held = [dot(piece, place) for piece in split(source[j * STEN : (j + 1) * STEN, :])]
            held = [jnp.where(keep, piece, F32(0.0)).astype(BF16) for piece in held]
            pieces.append(jnp.concatenate(held, axis=1))
        for c in range(0, count, step):
            rows = step * levels
            sums = jnp.zeros((rows, 2 * lat), F32)
            for key, piece in zip(keys, pieces):
                sums = sums + dot(onehot(iota((rows, STEN), 0) + c * levels == key), piece)
            sums = sums[:, :lat] + sums[:, lat:]
            fill(a_ref, (target + c) * levels, [sums[:, q * STEN : (q + 1) * STEN] for q in range(parts)])

    scatter(own_ref, 0, cols, 8, halo)
    scatter(left_ref, cols - halo, halo, halo // 2, 0)
    scatter(right_ref, 0, halo, halo // 2, halo + cols)
    diffuse(a_ref, b_ref, lon_ref, lat_ref, levels)
    matrix = mixing_matrix_back(v_ref[...])
    back = interleave(lat)
    group = WIDE // levels
    for g in range(cols // group):
        part = slice(g * group, (g + 1) * group)
        rows = slice(edge + g * WIDE, edge + (g + 1) * WIDE)
        x = jnp.concatenate([a_ref[q, rows, :] for q in range(parts)], axis=1)
        y = product(matrix, move(split(x), back)).reshape(levels, group, lat)
        out_ref[:, part, :] = control_ref[:, part, :] + y


def call(kernel, out_shape, specs, scratch, flops, moved, limit=VMEM_LIMIT):
    return pl.pallas_call(
        kernel,
        out_shape=out_shape,
        in_specs=specs,
        out_specs=jax.tree.map(lambda _: VMEM_SPEC, out_shape),
        scratch_shapes=list(scratch),
        cost_estimate=pl.CostEstimate(flops=flops, bytes_accessed=moved, transcendentals=0),
        compiler_params=pltpu.CompilerParams(vmem_limit_bytes=limit),
    )


def call_loading(kernel, out_shape, smem, arrays, scratch, flops, moved):
    count = len(arrays)
    copies_of = [pltpu.VMEM(array.shape, array.dtype) for array in arrays]
    outs = len(jax.tree.leaves(out_shape))

    def body(*refs):
        smem_refs, refs = refs[: len(smem)], refs[len(smem) :]
        sources, refs = refs[:count], refs[count:]
        out_refs, refs = refs[:outs], refs[outs:]
        targets, sems, rest = refs[:count], refs[count], refs[count + 1 :]
        copies = [pltpu.make_async_copy(a, b, sems.at[k]) for k, (a, b) in enumerate(zip(sources, targets))]
        for copy in copies:
            copy.start()
        waited = [0]

        def ready(n=count):
            for copy in copies[waited[0] : n]:
                copy.wait()
            waited[0] = max(n, waited[0])

        kernel(ready, *smem_refs, *targets, *out_refs, *rest)
        ready()

    return call(
        body,
        out_shape,
        [SMEM_SPEC] * len(smem) + [pl.BlockSpec(memory_space=pltpu.HBM)] * count,
        [*copies_of, pltpu.SemaphoreType.DMA((count,)), *scratch],
        flops,
        moved,
        WHOLE_VMEM,
    )(*smem, *arrays)


def shape(*dims):
    return jax.ShapeDtypeStruct(dims, F32)


def local(
    control, std_field, kappa_lon, kappa_lat, sea_mask, vertical,
    block_index, weights, obs_value, obs_rinv, obs_count,
):
    levels, cols, lat = control.shape
    parts = lat // STEN
    owners, slots = block_index.shape[1:]
    total = owners * slots
    halo = PASSES
    width = cols + 2 * halo
    cells = width * levels * lat
    count = lax.axis_size("lon")
    to_right = [(i, (i + 1) % count) for i in range(count)]
    to_left = [((i + 1) % count, i) for i in range(count)]

    message = parts * halo * (levels + 2) + parts
    message = -(-message // 8) * 8
    plane = pltpu.VMEM((cols, lat), F32)
    hbm = pl.BlockSpec(memory_space=pltpu.HBM)
    mixed, faces, edge_left, edge_right = call(
        head_kernel,
        (
            shape(parts, cols * levels, STEN), shape(3 * parts, cols, STEN),
            shape(message, STEN), shape(message, STEN),
        ),
        [hbm] * 5,
        [
            pltpu.VMEM((cols, lat), jnp.int32), plane, plane, pltpu.VMEM((levels, levels), F32),
            pltpu.VMEM((levels, cols, lat), F32), pltpu.SemaphoreType.DMA((5,)),
        ],
        12 * cells * lat, 8 * 4 * cells, WHOLE_VMEM,
    )(sea_mask, kappa_lon, kappa_lat, vertical, control)
    from_left = lax.ppermute(edge_right, "lon", to_right)
    from_right = lax.ppermute(edge_left, "lon", to_left)

    inside = pltpu.VMEM((parts + 2, cols * levels, STEN), F32)
    wedge = pltpu.VMEM((parts + 2, (halo + 2) * levels, STEN), F32)
    inner, strips, sent = call_loading(
        inner_kernel,
        (
            shape(parts, (cols - 2 * halo) * levels, STEN), shape(PASSES, 2, 2 * parts, levels, STEN),
            shape(owners, 2 * slots, STEN),
        ),
        [],
        [faces, mixed, block_index[0].T, obs_value[0].T, obs_rinv[0].T, obs_count, weights[0]],
        [
            inside, inside,
            pltpu.VMEM((parts, cols * 8, STEN), F32), pltpu.VMEM((parts + 1, cols * 8, STEN), F32),
        ],
        5 * PASSES * cells, PASSES * 4 * cells,
    )
    recv = lax.all_to_all(sent, "lon", split_axis=0, concat_axis=0, tiled=True)
    field = pltpu.VMEM((parts + 2, width * levels, STEN), F32)
    faces_held = [pltpu.VMEM((parts, width * 8, STEN), F32), pltpu.VMEM((parts + 1, width * 8, STEN), F32)]
    rows, all_faces = call_loading(
        edge_kernel,
        (shape(parts, cols * levels, STEN), shape(2 * parts, -(-width // 8) * 8, STEN)),
        [],
        [faces, from_left, from_right, strips, inner],
        [wedge, wedge, wedge, wedge, *faces_held],
        5 * PASSES * cells, PASSES * 4 * cells,
    )
    recv, rows = lax.optimization_barrier((recv, rows))
    index = recv[:, slots, 2 * slots : 3 * slots].reshape(total).astype(jnp.int32)
    level, column, _ = block_place(index, cols, parts)
    places = jnp.stack([index, column * levels + level])
    extra = -(-total // (8 * STEN)) * 8
    spread, departure = call_loading(
        departure_kernel,
        (shape(total + extra, STEN), shape(owners, STEN)),
        [places],
        [sea_mask, std_field, recv, rows],
        [
            pltpu.VMEM((total, STEN), F32), pltpu.VMEM((parts, total, STEN), F32), pltpu.VMEM((total, STEN), F32),
            pltpu.VMEM((parts, total, STEN), F32), pltpu.VMEM((levels * cols * parts, STEN), F32),
            pltpu.VMEM((cols * parts, STEN), F32),
        ],
        8 * total * lat, 4 * 4 * total * lat,
    )

    spread_left = lax.ppermute(spread, "lon", to_right)
    spread_right = lax.ppermute(spread, "lon", to_left)
    mine = lax.all_to_all(departure[:, None, :], "lon", split_axis=0, concat_axis=0, tiled=True)

    gradient = call(
        second_kernel, shape(levels, cols, lat), [VMEM_SPEC] * 6, [field, field, *faces_held],
        10 * PASSES * cells, 2 * PASSES * 4 * cells,
    )(vertical, control, spread, spread_left, spread_right, all_faces)
    gradient, mine = lax.optimization_barrier((gradient, mine))
    return gradient, mine[:, 0, :slots][None]


def solution(mesh):
    in_specs = (
        P("grp", "lon", None),
        P(None, "lon", None),
        P("lon", None),
        P("lon", None),
        P("lon", None),
        P(),
        P(("grp", "lon"), None, None),
        P(("grp", "lon"), None, None, None),
        P(("grp", "lon"), None, None),
        P(("grp", "lon"), None, None),
        P(("grp", "lon"), None),
    )
    out_specs = (P("grp", "lon", None), P(("grp", "lon"), None, None))
    return jax.shard_map(local, mesh=mesh, in_specs=in_specs, out_specs=out_specs, check_vma=False)
```

```python
import jax
import jax.numpy as jnp
from jax import lax
from jax.experimental import pallas as pl
from jax.experimental.pallas import tpu as pltpu
from jax.sharding import PartitionSpec as P

STEN = 128
PASSES = 10
WIDE = 256
F32 = jnp.float32
BF16 = jnp.bfloat16
HEAD_VMEM = 52 * 1024 * 1024
TIERS = ((0, 4), (4, PASSES))
VMEM_LIMIT = 24 * 1024 * 1024

VMEM_SPEC = pl.BlockSpec(memory_space=pltpu.VMEM)
SMEM_SPEC = pl.BlockSpec(memory_space=pltpu.SMEM)


def split(x):
    high = x.astype(BF16)
    return high, (x - high.astype(F32)).astype(BF16)


def split3(x):
    high = x.astype(BF16)
    rest = x - high.astype(F32)
    middle = rest.astype(BF16)
    return high, middle, (rest - middle.astype(F32)).astype(BF16)


def dot(a, b):
    return jnp.dot(a, b, preferred_element_type=F32)


def log2(n):
    assert n & (n - 1) == 0
    return n.bit_length() - 1


def iota(shape, dim):
    return lax.broadcasted_iota(jnp.int32, shape, dim)


def onehot(condition):
    return jnp.where(condition, F32(1.0), F32(0.0)).astype(BF16)


def product(left, right):
    (lh, ll), (rh, rl) = left, right
    return dot(lh, rh) + (dot(lh, rl) + dot(ll, rh))


def mixing_matrix(vertical):
    levels = vertical.shape[0]
    group = WIDE // levels
    expand = onehot(iota((levels, WIDE), 1) // group == iota((levels, WIDE), 0))
    keep = iota((WIDE, WIDE), 0) // levels == iota((WIDE, WIDE), 1) % group
    out = []
    for part in split(vertical):
        rows = dot(part, expand)
        tiled = jnp.concatenate([rows] * group, axis=0)
        out.append(jnp.where(keep, tiled, F32(0.0)).astype(BF16))
    return tuple(out)


def mixing_matrix_back(vertical):
    levels = vertical.shape[0]
    group = WIDE // levels
    spread = onehot(iota((levels, WIDE), 1) % levels == iota((levels, WIDE), 0))
    repeat = onehot(iota((WIDE, levels), 0) // group == iota((WIDE, levels), 1))
    keep = iota((WIDE, WIDE), 0) % group == iota((WIDE, WIDE), 1) // levels
    out = []
    for part in split(vertical):
        rows = lax.dot_general(part, spread, (((0,), (0,)), ((), ())), preferred_element_type=F32)
        rows = rows.astype(BF16)
        out.append(jnp.where(keep, dot(repeat, rows), F32(0.0)).astype(BF16))
    return tuple(out)


def deinterleave(lat):
    parts = lat // STEN
    target = iota((lat, lat), 1)
    return onehot(iota((lat, lat), 0) == (target % STEN) * parts + target // STEN)


def interleave(lat):
    parts = lat // STEN
    source = iota((lat, lat), 0)
    return onehot(iota((lat, lat), 1) == (source % STEN) * parts + source // STEN)


def spread_block(lat):
    parts = lat // STEN
    target = iota((STEN, lat), 1)
    return onehot(iota((STEN, lat), 0) == (target % (STEN // parts)) * parts + target // STEN)


def lane_segment(rows, lat):
    parts = lat // STEN
    return (iota((rows, lat), 1) % STEN) // (STEN // parts)


def move(x, matrix):
    return tuple(dot(part, matrix).astype(BF16) for part in x)


def unpack_meta(recv_ref, slots, field):
    owners = recv_ref.shape[0]
    total = owners * slots
    rows = jnp.broadcast_to(recv_ref[:, slots : slots + 1, :], (owners, slots, STEN)).reshape(total, STEN)
    wanted = (iota((total, STEN), 0) & (slots - 1)) + field * slots
    return jnp.sum(jnp.where(iota((total, STEN), 1) == wanted, rows, F32(0.0)), axis=1, keepdims=True)


def head_kernel(
    stack_ref, control_hbm, mixed_ref, faces_ref, left_ref, right_ref, control_ref, sem,
):
    copy = pltpu.make_async_copy(control_hbm, control_ref, sem)
    copy.start()
    levels, cols, lat = control_ref.shape
    parts = lat // STEN
    group = WIDE // levels
    halo = PASSES
    edge = halo * levels
    place = deinterleave(lat)
    matrix = mixing_matrix(stack_ref[3 * cols : 3 * cols + levels, 0:levels])
    wet = stack_ref[2 * cols : 3 * cols, :]
    east = jnp.where(iota((cols, lat), 0) == cols - 1, F32(1.0), pltpu.roll(wet, cols - 1, 0))
    north = jnp.where(iota((cols, lat), 1) == lat - 1, F32(0.0), pltpu.roll(wet, lat - 1, 1))
    for k, face in enumerate(
        (stack_ref[0:cols, :] * wet * east, stack_ref[cols : 2 * cols, :] * wet * north, wet)
    ):
        held = sum(dot(piece, place) for piece in (split3(face) if k < 2 else (face.astype(BF16),)))
        for q in range(parts):
            faces_ref[k * parts + q] = held[:, q * STEN : (q + 1) * STEN]
    copy.wait()
    for g in range(cols // group):
        x = control_ref[:, g * group : (g + 1) * group, :].reshape(WIDE, lat)
        y = product(matrix, move(split(x), place))
        for q in range(parts):
            mixed_ref[q, g * WIDE : (g + 1) * WIDE, :] = y[:, q * STEN : (q + 1) * STEN]
    for out, start in ((left_ref, 0), (right_ref, cols - halo)):
        for q in range(parts):
            out[q * edge : (q + 1) * edge, :] = mixed_ref[q, start * levels : start * levels + edge, :]
        for k in range(2 * parts):
            first = parts * edge + k * halo
            out[first : first + halo, :] = faces_ref[k, start : start + halo, :]
        first = parts * edge + 2 * parts * halo
        for q in range(parts):
            out[first + q : first + q + 1, :] = faces_ref[2 * parts + q, 0:1, :]
        out[first + parts :, :] = jnp.zeros((out.shape[0] - first - parts, STEN), F32)


def build_faces(faces_ref, from_left, from_right, lon_ref, lat_ref, levels):
    halo = PASSES
    cols = faces_ref.shape[1]
    parts = faces_ref.shape[0] // 3
    first = parts * halo * levels
    shape = (8, STEN)

    def far(source, k, c):
        at = first + k * halo + c
        return source[at : at + 1, :]

    for c in range(cols + 2 * halo):
        rows = slice(8 * c, 8 * c + 8)
        for q in range(parts):
            if c < halo:
                lon_row, lat_row = far(from_left, q, c), far(from_left, parts + q, c)
                if c == halo - 1:
                    lon_row = lon_row * faces_ref[2 * parts + q, 0:1, :]
            elif c < halo + cols:
                own = c - halo
                lon_row = faces_ref[q, own : own + 1, :]
                lat_row = faces_ref[parts + q, own : own + 1, :]
                if own == cols - 1:
                    at = first + 2 * parts * halo + q
                    lon_row = lon_row * from_right[at : at + 1, :]
            else:
                own = c - halo - cols
                lon_row, lat_row = far(from_right, q, own), far(from_right, parts + q, own)
            lon_ref[q, rows, :] = jnp.broadcast_to(lon_row, shape)
            lat_ref[q, rows, :] = jnp.broadcast_to(lat_row, shape)
            if q == parts - 1:
                lat_ref[parts, rows, :] = jnp.broadcast_to(pltpu.roll(lat_row, 1, 1), shape)


def add_ghosts(ref, first, values):
    count = values[0].shape[0]
    parts = len(values)
    ref[parts, first : first + count, :] = pltpu.roll(values[0], STEN - 1, 1)
    ref[parts + 1, first : first + count, :] = pltpu.roll(values[-1], 1, 1)


def fill(ref, first, values):
    for q, value in enumerate(values):
        ref[q, first : first + value.shape[0], :] = value
    add_ghosts(ref, first, values)


def column_steps(src, dst, lon_ref, lat_ref, levels, low, high, step=0, face=0):
    parts = lon_ref.shape[0]
    halves = range(levels // 8)

    def load(k, c, h):
        return src[k, c * levels + 8 * h : c * levels + 8 * h + 8, :]

    def rate(ref, k, c):
        return ref[k, pl.ds(pl.multiple_of(8 * (c + face), 8), 8), :]

    here = [[load(q, low, h) for q in range(parts)] for h in halves]
    west = [[rate(lon_ref, q, low - 1) * (here[h][q] - load(q, low - 1, h)) for q in range(parts)] for h in halves]
    for c in range(low, high):
        lon = [rate(lon_ref, q, c) for q in range(parts)]
        lat = [rate(lat_ref, q, c) for q in range(parts + 1)]
        for h in halves:
            line = here[h]
            east = [load(q, c + 1, h) for q in range(parts)]
            flux_east = [lon[q] * (east[q] - line[q]) for q in range(parts)]
            ahead = line[1:] + [load(parts, c, h)]
            flux_north = [lat[parts] * (line[0] - load(parts + 1, c, h))]
            flux_north += [lat[q] * (ahead[q] - line[q]) for q in range(parts)]
            out = [
                line[q] + (flux_east[q] - west[h][q]) + (flux_north[q + 1] - flux_north[q])
                for q in range(parts)
            ]
            first = (c + step) * levels + 8 * h
            for q in range(parts):
                dst[q, first : first + 8, :] = out[q]
            add_ghosts(dst, first, out)
            here[h], west[h] = east, flux_east


def diffuse(a_ref, b_ref, lon_ref, lat_ref, levels, before_pass=None):
    width = a_ref.shape[1] // levels

    for first, last in TIERS:

        def pair(turn, carry):
            for k, (src, dst) in enumerate(((a_ref, b_ref), (b_ref, a_ref))):
                if before_pass is not None:
                    before_pass(2 * turn + k, src)
                column_steps(src, dst, lon_ref, lat_ref, levels, first + 1 + k, width - first - 1 - k)
            return carry

        lax.fori_loop(first // 2, last // 2, pair, 0)


def inner_kernel(mixed_ref, faces_ref, inner_ref, strips_ref, a_ref, b_ref, lon_ref, lat_ref):
    parts, own_rows, _ = mixed_ref.shape
    cols = faces_ref.shape[1]
    levels = own_rows // cols
    shape = (8, STEN)
    for c in range(cols):
        rows = slice(8 * c, 8 * c + 8)
        for q in range(parts):
            lat_row = faces_ref[parts + q, c : c + 1, :]
            lon_ref[q, rows, :] = jnp.broadcast_to(faces_ref[q, c : c + 1, :], shape)
            lat_ref[q, rows, :] = jnp.broadcast_to(lat_row, shape)
            if q == parts - 1:
                lat_ref[parts, rows, :] = jnp.broadcast_to(pltpu.roll(lat_row, 1, 1), shape)
    fill(a_ref, 0, [mixed_ref[q] for q in range(parts)])

    def save(turn, src):
        for side, (line, other) in enumerate(((turn, turn + 1), (cols - 1 - turn, cols - 2 - turn))):
            line = pl.ds(pl.multiple_of(line * levels, levels), levels)
            other = pl.ds(pl.multiple_of(other * levels, levels), levels)
            for q in range(parts):
                strips_ref[turn, side, q] = src[q, line, :]
                strips_ref[turn, side, parts + q] = src[q, other, :]

    diffuse(a_ref, b_ref, lon_ref, lat_ref, levels, save)
    for q in range(parts):
        inner_ref[q] = a_ref[q, PASSES * levels : (cols - PASSES) * levels, :]


def block_place(index, cols, parts):
    return (
        lax.shift_right_logical(index, log2(cols * parts)),
        lax.shift_right_logical(index, log2(parts)) & (cols - 1),
        index & (parts - 1),
    )


def weights_kernel(place_ref, recv_ref, std_ref, mask_ref, out_ref, held_ref, pick_ref, std_rows, wet_rows):
    owners, rows, _ = recv_ref.shape
    slots = rows // 2
    total = owners * slots
    levels, cols, lat = std_ref.shape
    parts = lat // STEN
    for s in range(parts):
        part = slice(s * STEN, (s + 1) * STEN)
        wet_rows[s * cols : (s + 1) * cols, :] = mask_ref[:, part].astype(F32)
        for a in range(levels):
            first = (a * parts + s) * cols
            std_rows[first : first + cols, :] = std_ref[a, :, part]

    def pick(o, carry):
        for k in range(slots):
            slot = o * slots + k
            level, column, seg = block_place(place_ref[0, slot], cols, parts)
            value = std_rows[pl.ds((level * parts + seg) * cols + column, 1), :]
            wet = wet_rows[pl.ds(seg * cols + column, 1), :]
            pick_ref[pl.ds(slot, 1), :] = value * wet
        return carry

    lax.fori_loop(0, owners, pick, 0)
    ws = recv_ref[:, 0:slots, :].reshape(total, STEN) * pick_ref[...]
    out_ref[...] = ws
    place = spread_block(lat)
    segs = unpack_meta(recv_ref, slots, 2).astype(jnp.int32) & (parts - 1)
    for j in range(total // STEN):
        part = slice(j * STEN, (j + 1) * STEN)
        seg = segs[part]
        held = sum(dot(piece, place) for piece in split3(ws[part]))
        held = jnp.where(lane_segment(STEN, lat) == seg, held, F32(0.0))
        for q in range(parts):
            held_ref[q, part, :] = held[:, q * STEN : (q + 1) * STEN]


def to_row(column):
    eye = iota((STEN, STEN), 0) == iota((STEN, STEN), 1)
    return jnp.sum(jnp.where(eye, column, F32(0.0)), axis=0, keepdims=True)


def to_column(row):
    eye = iota((STEN, STEN), 0) == iota((STEN, STEN), 1)
    return jnp.sum(jnp.where(eye, row, F32(0.0)), axis=1, keepdims=True)


def edge_kernel(
    place_ref, inner_ref, strips_ref, from_left, from_right, faces_ref, recv_ref, ws_ref, held_ref,
    spread_ref, departure_ref, rows_ref, left_a, left_b, right_a, right_b, lon_ref, lat_ref, pick_ref,
):
    halo = PASSES
    levels = strips_ref.shape[3]
    parts = inner_ref.shape[0]
    owners, rows, _ = recv_ref.shape
    cols = faces_ref.shape[1]
    slots = rows // 2
    total = owners * slots
    edge = halo * levels
    build_faces(faces_ref, from_left, from_right, lon_ref, lat_ref, levels)
    fill(left_a, 0, [from_left[q * edge : (q + 1) * edge, :] for q in range(parts)])
    fill(right_a, 2 * levels, [from_right[q * edge : (q + 1) * edge, :] for q in range(parts)])

    def pair(turn, carry):
        for k, (left, left_to, right, right_to) in enumerate(
            ((left_a, left_b, right_a, right_b), (left_b, left_a, right_b, right_a))
        ):
            now = 2 * turn + k
            for side, ref, line, other in ((0, left, halo, halo + 1), (1, right, 1, 0)):
                fill(ref, line * levels, [strips_ref[now, side, q] for q in range(parts)])
                for q in range(parts):
                    ref[q, other * levels : (other + 1) * levels, :] = strips_ref[now, side, parts + q]
            column_steps(left, left_to, lon_ref, lat_ref, levels, 1, halo + 1, -1, now)
            column_steps(right, right_to, lon_ref, lat_ref, levels, 1, halo + 1, 1, halo + cols - 2 - now)
        return carry

    lax.fori_loop(0, PASSES // 2, pair, 0)
    for q in range(parts):
        rows_ref[q, 0:edge, :] = left_a[q, 0:edge, :]
        rows_ref[q, edge : cols * levels - edge, :] = inner_ref[q]
        rows_ref[q, cols * levels - edge :, :] = right_a[q, 2 * levels : 2 * levels + edge, :]

    def pick(o, carry):
        for k in range(slots):
            slot = o * slots + k
            row = place_ref[1, slot]
            for q in range(parts):
                pick_ref[q, pl.ds(slot, 1), :] = rows_ref[q, pl.ds(row, 1), :]
        return carry

    lax.fori_loop(0, owners, pick, 0)
    value, rinv, index, valid = (unpack_meta(recv_ref, slots, field) for field in range(4))
    evolved = sum(pick_ref[q] * held_ref[q] for q in range(parts))
    evolved = jnp.sum(evolved, axis=1, keepdims=True)
    departure = jnp.where(valid > 0.5, evolved - value, F32(0.0))
    scaled = rinv * departure
    spread_ref[0:total, :] = scaled * ws_ref[...]
    spread_ref[total:, :] = jnp.zeros((spread_ref.shape[0] - total, STEN), F32)
    for j in range(total // STEN):
        part = slice(j * STEN, (j + 1) * STEN)
        spread_ref[total + j : total + j + 1, :] = to_row(index[part])
    lanes = jnp.where(iota((total, STEN), 1) == (iota((total, STEN), 0) & (slots - 1)), departure, F32(0.0))
    departure_ref[...] = jnp.sum(lanes.reshape(owners, slots, STEN), axis=1)


def second_kernel(
    v_ref, control_ref, own_ref, left_ref, right_ref, faces_ref, from_left, from_right,
    out_ref, a_ref, b_ref, lon_ref, lat_ref,
):
    halo = PASSES
    levels, cols, lat = control_ref.shape
    parts = lat // STEN
    edge = halo * levels
    total = own_ref.shape[0] // STEN * STEN
    build_faces(faces_ref, from_left, from_right, lon_ref, lat_ref, levels)
    place = spread_block(lat)

    def scatter(source, first, count, step, target):
        pieces = []
        keys = []
        for j in range(total // STEN):
            index = source[total + j : total + j + 1, :].astype(jnp.int32)
            level, column, seg = block_place(index, cols, parts)
            keys.append((column - first) * levels + level)
            keep = lane_segment(STEN, lat) == to_column(seg.astype(F32)).astype(jnp.int32)
            held = [dot(piece, place) for piece in split(source[j * STEN : (j + 1) * STEN, :])]
            held = [jnp.where(keep, piece, F32(0.0)).astype(BF16) for piece in held]
            pieces.append(jnp.concatenate(held, axis=1))
        for c in range(0, count, step):
            rows = step * levels
            sums = jnp.zeros((rows, 2 * lat), F32)
            for key, piece in zip(keys, pieces):
                sums = sums + dot(onehot(iota((rows, STEN), 0) + c * levels == key), piece)
            sums = sums[:, :lat] + sums[:, lat:]
            fill(a_ref, (target + c) * levels, [sums[:, q * STEN : (q + 1) * STEN] for q in range(parts)])

    scatter(own_ref, 0, cols, 8, halo)
    scatter(left_ref, cols - halo, halo, halo // 2, 0)
    scatter(right_ref, 0, halo, halo // 2, halo + cols)
    diffuse(a_ref, b_ref, lon_ref, lat_ref, levels)
    matrix = mixing_matrix_back(v_ref[...])
    back = interleave(lat)
    group = WIDE // levels
    for g in range(cols // group):
        part = slice(g * group, (g + 1) * group)
        rows = slice(edge + g * WIDE, edge + (g + 1) * WIDE)
        x = jnp.concatenate([a_ref[q, rows, :] for q in range(parts)], axis=1)
        y = product(matrix, move(split(x), back)).reshape(levels, group, lat)
        out_ref[:, part, :] = control_ref[:, part, :] + y


def call(kernel, out_shape, specs, scratch, flops, moved, limit=VMEM_LIMIT):
    return pl.pallas_call(
        kernel,
        out_shape=out_shape,
        in_specs=specs,
        out_specs=jax.tree.map(lambda _: VMEM_SPEC, out_shape),
        scratch_shapes=list(scratch),
        cost_estimate=pl.CostEstimate(flops=flops, bytes_accessed=moved, transcendentals=0),
        compiler_params=pltpu.CompilerParams(vmem_limit_bytes=limit),
    )


def shape(*dims):
    return jax.ShapeDtypeStruct(dims, F32)


def local(
    control, std_field, kappa_lon, kappa_lat, sea_mask, vertical,
    block_index, weights, obs_value, obs_rinv, obs_count,
):
    levels, cols, lat = control.shape
    parts = lat // STEN
    owners, slots = block_index.shape[1:]
    total = owners * slots
    halo = PASSES
    width = cols + 2 * halo
    cells = width * levels * lat
    count = lax.axis_size("lon")
    to_right = [(i, (i + 1) % count) for i in range(count)]
    to_left = [((i + 1) % count, i) for i in range(count)]

    message = parts * halo * (levels + 2) + parts
    message = -(-message // 8) * 8
    valid = jnp.arange(slots, dtype=jnp.int32)[None, :] < obs_count[0][:, None]
    meta = jnp.concatenate([obs_value[0], obs_rinv[0], block_index[0].astype(F32), valid.astype(F32)], axis=1)
    meta = jnp.pad(meta, ((0, 0), (0, STEN - 4 * slots)))
    meta = jnp.broadcast_to(meta[:, None, :], (owners, slots, STEN))
    sent = jnp.concatenate([weights[0], meta], axis=1)
    stack = jnp.concatenate(
        [kappa_lon, kappa_lat, sea_mask.astype(F32), jnp.pad(vertical, ((0, 0), (0, lat - levels)))]
    )
    sent, stack = lax.optimization_barrier((sent, stack))
    mixed, faces, edge_left, edge_right = call(
        head_kernel,
        (
            shape(parts, cols * levels, STEN), shape(3 * parts, cols, STEN),
            shape(message, STEN), shape(message, STEN),
        ),
        [VMEM_SPEC, pl.BlockSpec(memory_space=pltpu.HBM)],
        [pltpu.VMEM((levels, cols, lat), F32), pltpu.SemaphoreType.DMA(())],
        12 * cells * lat, 8 * 4 * cells, HEAD_VMEM,
    )(stack, control)
    from_left = lax.ppermute(edge_right, "lon", to_right)
    from_right = lax.ppermute(edge_left, "lon", to_left)

    recv = lax.all_to_all(sent, "lon", split_axis=0, concat_axis=0, tiled=True)
    index = recv[:, slots, 2 * slots : 3 * slots].reshape(total).astype(jnp.int32)
    level, column, _ = block_place(index, cols, parts)
    places = jnp.stack([index, column * levels + level])
    ws, held = call(
        weights_kernel,
        (shape(total, STEN), shape(parts, total, STEN)),
        [SMEM_SPEC] + [VMEM_SPEC] * 3,
        [
            pltpu.VMEM((total, STEN), F32), pltpu.VMEM((levels * cols * parts, STEN), F32),
            pltpu.VMEM((cols * parts, STEN), F32),
        ],
        6 * total * STEN * lat, 4 * 4 * cells,
    )(places, recv, std_field, sea_mask)

    field = pltpu.VMEM((parts + 2, width * levels, STEN), F32)
    faces_held = [pltpu.VMEM((parts, width * 8, STEN), F32), pltpu.VMEM((parts + 1, width * 8, STEN), F32)]
    extra = -(-total // (8 * STEN)) * 8
    inside = pltpu.VMEM((parts + 2, cols * levels, STEN), F32)
    wedge = pltpu.VMEM((parts + 2, (halo + 2) * levels, STEN), F32)
    inner, strips = call(
        inner_kernel,
        (shape(parts, (cols - 2 * halo) * levels, STEN), shape(PASSES, 2, 2 * parts, levels, STEN)),
        [VMEM_SPEC] * 2,
        [
            inside, inside,
            pltpu.VMEM((parts, cols * 8, STEN), F32), pltpu.VMEM((parts + 1, cols * 8, STEN), F32),
        ],
        5 * PASSES * cells, PASSES * 4 * cells,
    )(mixed, faces)
    spread, departure = call(
        edge_kernel,
        (shape(total + extra, STEN), shape(owners, STEN)),
        [SMEM_SPEC] + [VMEM_SPEC] * 8,
        [
            pltpu.VMEM((parts, cols * levels, STEN), F32), wedge, wedge, wedge, wedge, *faces_held,
            pltpu.VMEM((parts, total, STEN), F32),
        ],
        5 * PASSES * cells, PASSES * 4 * cells,
    )(places, inner, strips, from_left, from_right, faces, recv, ws, held)

    spread_left = lax.ppermute(spread, "lon", to_right)
    spread_right = lax.ppermute(spread, "lon", to_left)
    mine = lax.all_to_all(departure[:, None, :], "lon", split_axis=0, concat_axis=0, tiled=True)

    gradient = call(
        second_kernel, shape(levels, cols, lat), [VMEM_SPEC] * 8, [field, field, *faces_held],
        10 * PASSES * cells, 2 * PASSES * 4 * cells,
    )(vertical, control, spread, spread_left, spread_right, faces, from_left, from_right)
    gradient, mine = lax.optimization_barrier((gradient, mine))
    return gradient, mine[:, 0, :slots][None]


def solution(mesh):
    in_specs = (
        P("grp", "lon", None),
        P(None, "lon", None),
        P("lon", None),
        P("lon", None),
        P("lon", None),
        P(),
        P(("grp", "lon"), None, None),
        P(("grp", "lon"), None, None, None),
        P(("grp", "lon"), None, None),
        P(("grp", "lon"), None, None),
        P(("grp", "lon"), None),
    )
    out_specs = (P("grp", "lon", None), P(("grp", "lon"), None, None))
    return jax.shard_map(local, mesh=mesh, in_specs=in_specs, out_specs=out_specs, check_vma=False)
```

```python
import jax
import jax.numpy as jnp
from jax import lax
from jax.experimental import pallas as pl
from jax.experimental.pallas import tpu as pltpu
from jax.sharding import PartitionSpec as P

STEN = 128
PASSES = 10
WIDE = 256
F32 = jnp.float32
BF16 = jnp.bfloat16
WHOLE_VMEM = 60 * 1024 * 1024
TIERS = ((0, 4), (4, PASSES))
VMEM_LIMIT = 24 * 1024 * 1024

VMEM_SPEC = pl.BlockSpec(memory_space=pltpu.VMEM)
SMEM_SPEC = pl.BlockSpec(memory_space=pltpu.SMEM)


def split(x):
    high = x.astype(BF16)
    return high, (x - high.astype(F32)).astype(BF16)


def split3(x):
    high = x.astype(BF16)
    rest = x - high.astype(F32)
    middle = rest.astype(BF16)
    return high, middle, (rest - middle.astype(F32)).astype(BF16)


def dot(a, b):
    return jnp.dot(a, b, preferred_element_type=F32)


def log2(n):
    assert n & (n - 1) == 0
    return n.bit_length() - 1


def iota(shape, dim):
    return lax.broadcasted_iota(jnp.int32, shape, dim)


def onehot(condition):
    return jnp.where(condition, F32(1.0), F32(0.0)).astype(BF16)


def product(left, right):
    (lh, ll), (rh, rl) = left, right
    return dot(lh, rh) + (dot(lh, rl) + dot(ll, rh))


def mixing_matrix(vertical):
    levels = vertical.shape[0]
    group = WIDE // levels
    expand = onehot(iota((levels, WIDE), 1) // group == iota((levels, WIDE), 0))
    keep = iota((WIDE, WIDE), 0) // levels == iota((WIDE, WIDE), 1) % group
    out = []
    for part in split(vertical):
        rows = dot(part, expand)
        tiled = jnp.concatenate([rows] * group, axis=0)
        out.append(jnp.where(keep, tiled, F32(0.0)).astype(BF16))
    return tuple(out)


def mixing_matrix_back(vertical):
    levels = vertical.shape[0]
    group = WIDE // levels
    spread = onehot(iota((levels, WIDE), 1) % levels == iota((levels, WIDE), 0))
    repeat = onehot(iota((WIDE, levels), 0) // group == iota((WIDE, levels), 1))
    keep = iota((WIDE, WIDE), 0) % group == iota((WIDE, WIDE), 1) // levels
    out = []
    for part in split(vertical):
        rows = lax.dot_general(part, spread, (((0,), (0,)), ((), ())), preferred_element_type=F32)
        rows = rows.astype(BF16)
        out.append(jnp.where(keep, dot(repeat, rows), F32(0.0)).astype(BF16))
    return tuple(out)


def deinterleave(lat):
    parts = lat // STEN
    target = iota((lat, lat), 1)
    return onehot(iota((lat, lat), 0) == (target % STEN) * parts + target // STEN)


def interleave(lat):
    parts = lat // STEN
    source = iota((lat, lat), 0)
    return onehot(iota((lat, lat), 1) == (source % STEN) * parts + source // STEN)


def spread_block(lat):
    parts = lat // STEN
    target = iota((STEN, lat), 1)
    return onehot(iota((STEN, lat), 0) == (target % (STEN // parts)) * parts + target // STEN)


def lane_segment(rows, lat):
    parts = lat // STEN
    return (iota((rows, lat), 1) % STEN) // (STEN // parts)


def move(x, matrix):
    return tuple(dot(part, matrix).astype(BF16) for part in x)


def pack_meta(slots, values):
    stacked = jnp.concatenate(values, axis=0)
    eye = onehot(iota((stacked.shape[0], STEN), 0) == iota((stacked.shape[0], STEN), 1))
    return sum(
        lax.dot_general(part, eye, (((0,), (0,)), ((), ())), preferred_element_type=F32)
        for part in split3(stacked)
    )


def unpack_meta(recv_ref, slots, field):
    owners = recv_ref.shape[0]
    total = owners * slots
    rows = jnp.broadcast_to(recv_ref[:, slots : slots + 1, :], (owners, slots, STEN)).reshape(total, STEN)
    wanted = (iota((total, STEN), 0) & (slots - 1)) + field * slots
    return jnp.sum(jnp.where(iota((total, STEN), 1) == wanted, rows, F32(0.0)), axis=1, keepdims=True)


def head_kernel(
    mask_hbm, klon_hbm, klat_hbm, v_hbm, control_hbm, mixed_ref, faces_ref, left_ref, right_ref,
    mask_ref, klon_ref, klat_ref, v_ref, control_ref, sems,
):
    pairs = (
        (mask_hbm, mask_ref), (klon_hbm, klon_ref), (klat_hbm, klat_ref), (v_hbm, v_ref), (control_hbm, control_ref),
    )
    copies = [pltpu.make_async_copy(source, target, sems.at[k]) for k, (source, target) in enumerate(pairs)]
    for copy in copies:
        copy.start()
    levels, cols, lat = control_ref.shape
    parts = lat // STEN
    group = WIDE // levels
    halo = PASSES
    edge = halo * levels
    place = deinterleave(lat)
    for copy in copies[:4]:
        copy.wait()
    matrix = mixing_matrix(v_ref[...])
    wet = mask_ref[...].astype(F32)
    east = jnp.where(iota((cols, lat), 0) == cols - 1, F32(1.0), pltpu.roll(wet, cols - 1, 0))
    north = jnp.where(iota((cols, lat), 1) == lat - 1, F32(0.0), pltpu.roll(wet, lat - 1, 1))
    for k, face in enumerate((klon_ref[...] * wet * east, klat_ref[...] * wet * north, wet)):
        held = sum(dot(piece, place) for piece in (split3(face) if k < 2 else (face.astype(BF16),)))
        for q in range(parts):
            faces_ref[k * parts + q] = held[:, q * STEN : (q + 1) * STEN]
    copies[4].wait()
    for g in range(cols // group):
        x = control_ref[:, g * group : (g + 1) * group, :].reshape(WIDE, lat)
        y = product(matrix, move(split(x), place))
        for q in range(parts):
            mixed_ref[q, g * WIDE : (g + 1) * WIDE, :] = y[:, q * STEN : (q + 1) * STEN]
    for out, start in ((left_ref, 0), (right_ref, cols - halo)):
        for q in range(parts):
            out[q * edge : (q + 1) * edge, :] = mixed_ref[q, start * levels : start * levels + edge, :]
        for k in range(2 * parts):
            first = parts * edge + k * halo
            out[first : first + halo, :] = faces_ref[k, start : start + halo, :]
        first = parts * edge + 2 * parts * halo
        for q in range(parts):
            out[first + q : first + q + 1, :] = faces_ref[2 * parts + q, 0:1, :]
        out[first + parts :, :] = jnp.zeros((out.shape[0] - first - parts, STEN), F32)


def pack_kernel(
    index_hbm, value_hbm, rinv_hbm, count_hbm, weights_hbm, sent_ref,
    index_ref, value_ref, rinv_ref, count_ref, sems,
):
    owners, slots, _ = weights_hbm.shape
    pairs = (
        (index_hbm, index_ref), (value_hbm, value_ref), (rinv_hbm, rinv_ref), (count_hbm, count_ref),
        (weights_hbm, sent_ref.at[:, 0:slots, :]),
    )
    copies = [pltpu.make_async_copy(source, target, sems.at[k]) for k, (source, target) in enumerate(pairs)]
    for copy in copies:
        copy.start()
    for copy in copies:
        copy.wait()
    valid = jnp.where(iota((slots, owners), 0) < count_ref[...], F32(1.0), F32(0.0))
    meta = pack_meta(slots, [value_ref[...], rinv_ref[...], index_ref[...].astype(F32), valid])
    sent_ref[:, slots:, :] = jnp.broadcast_to(meta[:, None, :], (owners, slots, STEN))


def build_faces(faces_ref, from_left, from_right, lon_ref, lat_ref, levels):
    halo = PASSES
    cols = faces_ref.shape[1]
    parts = faces_ref.shape[0] // 3
    first = parts * halo * levels
    shape = (8, STEN)

    def far(source, k, c):
        at = first + k * halo + c
        return source[at : at + 1, :]

    for c in range(cols + 2 * halo):
        rows = slice(8 * c, 8 * c + 8)
        for q in range(parts):
            if c < halo:
                lon_row, lat_row = far(from_left, q, c), far(from_left, parts + q, c)
                if c == halo - 1:
                    lon_row = lon_row * faces_ref[2 * parts + q, 0:1, :]
            elif c < halo + cols:
                own = c - halo
                lon_row = faces_ref[q, own : own + 1, :]
                lat_row = faces_ref[parts + q, own : own + 1, :]
                if own == cols - 1:
                    at = first + 2 * parts * halo + q
                    lon_row = lon_row * from_right[at : at + 1, :]
            else:
                own = c - halo - cols
                lon_row, lat_row = far(from_right, q, own), far(from_right, parts + q, own)
            lon_ref[q, rows, :] = jnp.broadcast_to(lon_row, shape)
            lat_ref[q, rows, :] = jnp.broadcast_to(lat_row, shape)
            if q == parts - 1:
                lat_ref[parts, rows, :] = jnp.broadcast_to(pltpu.roll(lat_row, 1, 1), shape)


def add_ghosts(ref, first, values):
    count = values[0].shape[0]
    parts = len(values)
    ref[parts, first : first + count, :] = pltpu.roll(values[0], STEN - 1, 1)
    ref[parts + 1, first : first + count, :] = pltpu.roll(values[-1], 1, 1)


def fill(ref, first, values):
    for q, value in enumerate(values):
        ref[q, first : first + value.shape[0], :] = value
    add_ghosts(ref, first, values)


def column_steps(src, dst, lon_ref, lat_ref, levels, low, high, step=0, face=0):
    parts = lon_ref.shape[0]
    halves = range(levels // 8)

    def load(k, c, h):
        return src[k, c * levels + 8 * h : c * levels + 8 * h + 8, :]

    def rate(ref, k, c):
        return ref[k, pl.ds(pl.multiple_of(8 * (c + face), 8), 8), :]

    here = [[load(q, low, h) for q in range(parts)] for h in halves]
    west = [[rate(lon_ref, q, low - 1) * (here[h][q] - load(q, low - 1, h)) for q in range(parts)] for h in halves]
    for c in range(low, high):
        lon = [rate(lon_ref, q, c) for q in range(parts)]
        lat = [rate(lat_ref, q, c) for q in range(parts + 1)]
        for h in halves:
            line = here[h]
            east = [load(q, c + 1, h) for q in range(parts)]
            flux_east = [lon[q] * (east[q] - line[q]) for q in range(parts)]
            ahead = line[1:] + [load(parts, c, h)]
            flux_north = [lat[parts] * (line[0] - load(parts + 1, c, h))]
            flux_north += [lat[q] * (ahead[q] - line[q]) for q in range(parts)]
            out = [
                line[q] + (flux_east[q] - west[h][q]) + (flux_north[q + 1] - flux_north[q])
                for q in range(parts)
            ]
            first = (c + step) * levels + 8 * h
            for q in range(parts):
                dst[q, first : first + 8, :] = out[q]
            add_ghosts(dst, first, out)
            here[h], west[h] = east, flux_east


def diffuse(a_ref, b_ref, lon_ref, lat_ref, levels, before_pass=None):
    width = a_ref.shape[1] // levels

    for first, last in TIERS:

        def pair(turn, carry):
            for k, (src, dst) in enumerate(((a_ref, b_ref), (b_ref, a_ref))):
                if before_pass is not None:
                    before_pass(2 * turn + k, src)
                column_steps(src, dst, lon_ref, lat_ref, levels, first + 1 + k, width - first - 1 - k)
            return carry

        lax.fori_loop(first // 2, last // 2, pair, 0)


def inner_kernel(mixed_ref, faces_ref, inner_ref, strips_ref, a_ref, b_ref, lon_ref, lat_ref):
    parts, own_rows, _ = mixed_ref.shape
    cols = faces_ref.shape[1]
    levels = own_rows // cols
    shape = (8, STEN)
    for c in range(cols):
        rows = slice(8 * c, 8 * c + 8)
        for q in range(parts):
            lat_row = faces_ref[parts + q, c : c + 1, :]
            lon_ref[q, rows, :] = jnp.broadcast_to(faces_ref[q, c : c + 1, :], shape)
            lat_ref[q, rows, :] = jnp.broadcast_to(lat_row, shape)
            if q == parts - 1:
                lat_ref[parts, rows, :] = jnp.broadcast_to(pltpu.roll(lat_row, 1, 1), shape)
    fill(a_ref, 0, [mixed_ref[q] for q in range(parts)])

    def save(turn, src):
        for side, (line, other) in enumerate(((turn, turn + 1), (cols - 1 - turn, cols - 2 - turn))):
            line = pl.ds(pl.multiple_of(line * levels, levels), levels)
            other = pl.ds(pl.multiple_of(other * levels, levels), levels)
            for q in range(parts):
                strips_ref[turn, side, q] = src[q, line, :]
                strips_ref[turn, side, parts + q] = src[q, other, :]

    diffuse(a_ref, b_ref, lon_ref, lat_ref, levels, save)
    for q in range(parts):
        inner_ref[q] = a_ref[q, PASSES * levels : (cols - PASSES) * levels, :]


def block_place(index, cols, parts):
    return (
        lax.shift_right_logical(index, log2(cols * parts)),
        lax.shift_right_logical(index, log2(parts)) & (cols - 1),
        index & (parts - 1),
    )


def weights_kernel(place_ref, recv_ref, std_ref, mask_ref, out_ref, held_ref, pick_ref, std_rows, wet_rows):
    owners, rows, _ = recv_ref.shape
    slots = rows // 2
    total = owners * slots
    levels, cols, lat = std_ref.shape
    parts = lat // STEN
    for s in range(parts):
        part = slice(s * STEN, (s + 1) * STEN)
        wet_rows[s * cols : (s + 1) * cols, :] = mask_ref[:, part].astype(F32)
        for a in range(levels):
            first = (a * parts + s) * cols
            std_rows[first : first + cols, :] = std_ref[a, :, part]

    def pick(o, carry):
        for k in range(slots):
            slot = o * slots + k
            level, column, seg = block_place(place_ref[0, slot], cols, parts)
            value = std_rows[pl.ds((level * parts + seg) * cols + column, 1), :]
            wet = wet_rows[pl.ds(seg * cols + column, 1), :]
            pick_ref[pl.ds(slot, 1), :] = value * wet
        return carry

    lax.fori_loop(0, owners, pick, 0)
    ws = recv_ref[:, 0:slots, :].reshape(total, STEN) * pick_ref[...]
    out_ref[...] = ws
    place = spread_block(lat)
    segs = unpack_meta(recv_ref, slots, 2).astype(jnp.int32) & (parts - 1)
    for j in range(total // STEN):
        part = slice(j * STEN, (j + 1) * STEN)
        seg = segs[part]
        held = sum(dot(piece, place) for piece in split3(ws[part]))
        held = jnp.where(lane_segment(STEN, lat) == seg, held, F32(0.0))
        for q in range(parts):
            held_ref[q, part, :] = held[:, q * STEN : (q + 1) * STEN]


def to_row(column):
    eye = iota((STEN, STEN), 0) == iota((STEN, STEN), 1)
    return jnp.sum(jnp.where(eye, column, F32(0.0)), axis=0, keepdims=True)


def to_column(row):
    eye = iota((STEN, STEN), 0) == iota((STEN, STEN), 1)
    return jnp.sum(jnp.where(eye, row, F32(0.0)), axis=1, keepdims=True)


def edge_kernel(
    place_ref, inner_ref, strips_ref, from_left, from_right, faces_ref, recv_ref, ws_ref, held_ref,
    spread_ref, departure_ref, rows_ref, left_a, left_b, right_a, right_b, lon_ref, lat_ref, pick_ref,
):
    halo = PASSES
    levels = strips_ref.shape[3]
    parts = inner_ref.shape[0]
    owners, rows, _ = recv_ref.shape
    cols = faces_ref.shape[1]
    slots = rows // 2
    total = owners * slots
    edge = halo * levels
    build_faces(faces_ref, from_left, from_right, lon_ref, lat_ref, levels)
    fill(left_a, 0, [from_left[q * edge : (q + 1) * edge, :] for q in range(parts)])
    fill(right_a, 2 * levels, [from_right[q * edge : (q + 1) * edge, :] for q in range(parts)])

    def pair(turn, carry):
        for k, (left, left_to, right, right_to) in enumerate(
            ((left_a, left_b, right_a, right_b), (left_b, left_a, right_b, right_a))
        ):
            now = 2 * turn + k
            for side, ref, line, other in ((0, left, halo, halo + 1), (1, right, 1, 0)):
                fill(ref, line * levels, [strips_ref[now, side, q] for q in range(parts)])
                for q in range(parts):
                    ref[q, other * levels : (other + 1) * levels, :] = strips_ref[now, side, parts + q]
            column_steps(left, left_to, lon_ref, lat_ref, levels, 1, halo + 1, -1, now)
            column_steps(right, right_to, lon_ref, lat_ref, levels, 1, halo + 1, 1, halo + cols - 2 - now)
        return carry

    lax.fori_loop(0, PASSES // 2, pair, 0)
    for q in range(parts):
        rows_ref[q, 0:edge, :] = left_a[q, 0:edge, :]
        rows_ref[q, edge : cols * levels - edge, :] = inner_ref[q]
        rows_ref[q, cols * levels - edge :, :] = right_a[q, 2 * levels : 2 * levels + edge, :]

    def pick(o, carry):
        for k in range(slots):
            slot = o * slots + k
            row = place_ref[1, slot]
            for q in range(parts):
                pick_ref[q, pl.ds(slot, 1), :] = rows_ref[q, pl.ds(row, 1), :]
        return carry

    lax.fori_loop(0, owners, pick, 0)
    value, rinv, index, valid = (unpack_meta(recv_ref, slots, field) for field in range(4))
    evolved = sum(pick_ref[q] * held_ref[q] for q in range(parts))
    evolved = jnp.sum(evolved, axis=1, keepdims=True)
    departure = jnp.where(valid > 0.5, evolved - value, F32(0.0))
    scaled = rinv * departure
    spread_ref[0:total, :] = scaled * ws_ref[...]
    spread_ref[total:, :] = jnp.zeros((spread_ref.shape[0] - total, STEN), F32)
    for j in range(total // STEN):
        part = slice(j * STEN, (j + 1) * STEN)
        spread_ref[total + j : total + j + 1, :] = to_row(index[part])
    lanes = jnp.where(iota((total, STEN), 1) == (iota((total, STEN), 0) & (slots - 1)), departure, F32(0.0))
    departure_ref[...] = jnp.sum(lanes.reshape(owners, slots, STEN), axis=1)


def second_kernel(
    v_ref, control_ref, own_ref, left_ref, right_ref, faces_ref, from_left, from_right,
    out_ref, a_ref, b_ref, lon_ref, lat_ref,
):
    halo = PASSES
    levels, cols, lat = control_ref.shape
    parts = lat // STEN
    edge = halo * levels
    total = own_ref.shape[0] // STEN * STEN
    build_faces(faces_ref, from_left, from_right, lon_ref, lat_ref, levels)
    place = spread_block(lat)

    def scatter(source, first, count, step, target):
        pieces = []
        keys = []
        for j in range(total // STEN):
            index = source[total + j : total + j + 1, :].astype(jnp.int32)
            level, column, seg = block_place(index, cols, parts)
            keys.append((column - first) * levels + level)
            keep = lane_segment(STEN, lat) == to_column(seg.astype(F32)).astype(jnp.int32)
            held = [dot(piece, place) for piece in split(source[j * STEN : (j + 1) * STEN, :])]
            held = [jnp.where(keep, piece, F32(0.0)).astype(BF16) for piece in held]
            pieces.append(jnp.concatenate(held, axis=1))
        for c in range(0, count, step):
            rows = step * levels
            sums = jnp.zeros((rows, 2 * lat), F32)
            for key, piece in zip(keys, pieces):
                sums = sums + dot(onehot(iota((rows, STEN), 0) + c * levels == key), piece)
            sums = sums[:, :lat] + sums[:, lat:]
            fill(a_ref, (target + c) * levels, [sums[:, q * STEN : (q + 1) * STEN] for q in range(parts)])

    scatter(own_ref, 0, cols, 8, halo)
    scatter(left_ref, cols - halo, halo, halo // 2, 0)
    scatter(right_ref, 0, halo, halo // 2, halo + cols)
    diffuse(a_ref, b_ref, lon_ref, lat_ref, levels)
    matrix = mixing_matrix_back(v_ref[...])
    back = interleave(lat)
    group = WIDE // levels
    for g in range(cols // group):
        part = slice(g * group, (g + 1) * group)
        rows = slice(edge + g * WIDE, edge + (g + 1) * WIDE)
        x = jnp.concatenate([a_ref[q, rows, :] for q in range(parts)], axis=1)
        y = product(matrix, move(split(x), back)).reshape(levels, group, lat)
        out_ref[:, part, :] = control_ref[:, part, :] + y


def call(kernel, out_shape, specs, scratch, flops, moved, limit=VMEM_LIMIT):
    return pl.pallas_call(
        kernel,
        out_shape=out_shape,
        in_specs=specs,
        out_specs=jax.tree.map(lambda _: VMEM_SPEC, out_shape),
        scratch_shapes=list(scratch),
        cost_estimate=pl.CostEstimate(flops=flops, bytes_accessed=moved, transcendentals=0),
        compiler_params=pltpu.CompilerParams(vmem_limit_bytes=limit),
    )


def shape(*dims):
    return jax.ShapeDtypeStruct(dims, F32)


def local(
    control, std_field, kappa_lon, kappa_lat, sea_mask, vertical,
    block_index, weights, obs_value, obs_rinv, obs_count,
):
    levels, cols, lat = control.shape
    parts = lat // STEN
    owners, slots = block_index.shape[1:]
    total = owners * slots
    halo = PASSES
    width = cols + 2 * halo
    cells = width * levels * lat
    count = lax.axis_size("lon")
    to_right = [(i, (i + 1) % count) for i in range(count)]
    to_left = [((i + 1) % count, i) for i in range(count)]

    message = parts * halo * (levels + 2) + parts
    message = -(-message // 8) * 8
    hbm = pl.BlockSpec(memory_space=pltpu.HBM)
    small = pltpu.VMEM((slots, owners), F32)
    sent = call(
        pack_kernel,
        shape(owners, 2 * slots, STEN),
        [hbm] * 5,
        [
            pltpu.VMEM((slots, owners), jnp.int32), small, small, pltpu.VMEM((1, owners), jnp.int32),
            pltpu.SemaphoreType.DMA((5,)),
        ],
        6 * STEN * owners * STEN, 4 * 4 * total * STEN, WHOLE_VMEM,
    )(block_index[0].T, obs_value[0].T, obs_rinv[0].T, obs_count, weights[0])
    sent, matrix = lax.optimization_barrier((sent, vertical))
    plane = pltpu.VMEM((cols, lat), F32)
    mixed, faces, edge_left, edge_right = call(
        head_kernel,
        (
            shape(parts, cols * levels, STEN), shape(3 * parts, cols, STEN),
            shape(message, STEN), shape(message, STEN),
        ),
        [hbm] * 5,
        [
            pltpu.VMEM((cols, lat), jnp.int32), plane, plane, pltpu.VMEM((levels, levels), F32),
            pltpu.VMEM((levels, cols, lat), F32), pltpu.SemaphoreType.DMA((5,)),
        ],
        12 * cells * lat, 8 * 4 * cells, WHOLE_VMEM,
    )(sea_mask, kappa_lon, kappa_lat, matrix, control)
    from_left = lax.ppermute(edge_right, "lon", to_right)
    from_right = lax.ppermute(edge_left, "lon", to_left)

    recv = lax.all_to_all(sent, "lon", split_axis=0, concat_axis=0, tiled=True)
    index = recv[:, slots, 2 * slots : 3 * slots].reshape(total).astype(jnp.int32)
    level, column, _ = block_place(index, cols, parts)
    places = jnp.stack([index, column * levels + level])
    ws, held = call(
        weights_kernel,
        (shape(total, STEN), shape(parts, total, STEN)),
        [SMEM_SPEC] + [VMEM_SPEC] * 3,
        [
            pltpu.VMEM((total, STEN), F32), pltpu.VMEM((levels * cols * parts, STEN), F32),
            pltpu.VMEM((cols * parts, STEN), F32),
        ],
        6 * total * STEN * lat, 4 * 4 * cells,
    )(places, recv, std_field, sea_mask)

    field = pltpu.VMEM((parts + 2, width * levels, STEN), F32)
    faces_held = [pltpu.VMEM((parts, width * 8, STEN), F32), pltpu.VMEM((parts + 1, width * 8, STEN), F32)]
    extra = -(-total // (8 * STEN)) * 8
    inside = pltpu.VMEM((parts + 2, cols * levels, STEN), F32)
    wedge = pltpu.VMEM((parts + 2, (halo + 2) * levels, STEN), F32)
    inner, strips = call(
        inner_kernel,
        (shape(parts, (cols - 2 * halo) * levels, STEN), shape(PASSES, 2, 2 * parts, levels, STEN)),
        [VMEM_SPEC] * 2,
        [
            inside, inside,
            pltpu.VMEM((parts, cols * 8, STEN), F32), pltpu.VMEM((parts + 1, cols * 8, STEN), F32),
        ],
        5 * PASSES * cells, PASSES * 4 * cells,
    )(mixed, faces)
    spread, departure = call(
        edge_kernel,
        (shape(total + extra, STEN), shape(owners, STEN)),
        [SMEM_SPEC] + [VMEM_SPEC] * 8,
        [
            pltpu.VMEM((parts, cols * levels, STEN), F32), wedge, wedge, wedge, wedge, *faces_held,
            pltpu.VMEM((parts, total, STEN), F32),
        ],
        5 * PASSES * cells, PASSES * 4 * cells,
    )(places, inner, strips, from_left, from_right, faces, recv, ws, held)

    spread_left = lax.ppermute(spread, "lon", to_right)
    spread_right = lax.ppermute(spread, "lon", to_left)
    mine = lax.all_to_all(departure[:, None, :], "lon", split_axis=0, concat_axis=0, tiled=True)

    gradient = call(
        second_kernel, shape(levels, cols, lat), [VMEM_SPEC] * 8, [field, field, *faces_held],
        10 * PASSES * cells, 2 * PASSES * 4 * cells,
    )(vertical, control, spread, spread_left, spread_right, faces, from_left, from_right)
    gradient, mine = lax.optimization_barrier((gradient, mine))
    return gradient, mine[:, 0, :slots][None]


def solution(mesh):
    in_specs = (
        P("grp", "lon", None),
        P(None, "lon", None),
        P("lon", None),
        P("lon", None),
        P("lon", None),
        P(),
        P(("grp", "lon"), None, None),
        P(("grp", "lon"), None, None, None),
        P(("grp", "lon"), None, None),
        P(("grp", "lon"), None, None),
        P(("grp", "lon"), None),
    )
    out_specs = (P("grp", "lon", None), P(("grp", "lon"), None, None))
    return jax.shard_map(local, mesh=mesh, in_specs=in_specs, out_specs=out_specs, check_vma=False)
```

```python
import jax
import jax.numpy as jnp
from jax import lax
from jax.experimental import pallas as pl
from jax.experimental.pallas import tpu as pltpu
from jax.sharding import PartitionSpec as P

STEN = 128
PASSES = 10
WIDE = 256
F32 = jnp.float32
BF16 = jnp.bfloat16
WHOLE_VMEM = 60 * 1024 * 1024
TIERS = ((0, 2), (2, 6), (6, PASSES))
VMEM_LIMIT = 24 * 1024 * 1024

VMEM_SPEC = pl.BlockSpec(memory_space=pltpu.VMEM)
SMEM_SPEC = pl.BlockSpec(memory_space=pltpu.SMEM)


def split(x):
    high = x.astype(BF16)
    return high, (x - high.astype(F32)).astype(BF16)


def split3(x):
    high = x.astype(BF16)
    rest = x - high.astype(F32)
    middle = rest.astype(BF16)
    return high, middle, (rest - middle.astype(F32)).astype(BF16)


def dot(a, b):
    return jnp.dot(a, b, preferred_element_type=F32)


def log2(n):
    assert n & (n - 1) == 0
    return n.bit_length() - 1


def iota(shape, dim):
    return lax.broadcasted_iota(jnp.int32, shape, dim)


def onehot(condition):
    return jnp.where(condition, F32(1.0), F32(0.0)).astype(BF16)


def product(left, right):
    (lh, ll), (rh, rl) = left, right
    return dot(lh, rh) + (dot(lh, rl) + dot(ll, rh))


def mixing_matrix(vertical):
    levels = vertical.shape[0]
    group = WIDE // levels
    expand = onehot(iota((levels, WIDE), 1) // group == iota((levels, WIDE), 0))
    keep = iota((WIDE, WIDE), 0) // levels == iota((WIDE, WIDE), 1) % group
    out = []
    for part in split(vertical):
        rows = dot(part, expand)
        tiled = jnp.concatenate([rows] * group, axis=0)
        out.append(jnp.where(keep, tiled, F32(0.0)).astype(BF16))
    return tuple(out)


def mixing_matrix_back(vertical):
    levels = vertical.shape[0]
    group = WIDE // levels
    spread = onehot(iota((levels, WIDE), 1) % levels == iota((levels, WIDE), 0))
    repeat = onehot(iota((WIDE, levels), 0) // group == iota((WIDE, levels), 1))
    keep = iota((WIDE, WIDE), 0) % group == iota((WIDE, WIDE), 1) // levels
    out = []
    for part in split(vertical):
        rows = lax.dot_general(part, spread, (((0,), (0,)), ((), ())), preferred_element_type=F32)
        rows = rows.astype(BF16)
        out.append(jnp.where(keep, dot(repeat, rows), F32(0.0)).astype(BF16))
    return tuple(out)


def deinterleave(lat):
    parts = lat // STEN
    target = iota((lat, lat), 1)
    return onehot(iota((lat, lat), 0) == (target % STEN) * parts + target // STEN)


def interleave(lat):
    parts = lat // STEN
    source = iota((lat, lat), 0)
    return onehot(iota((lat, lat), 1) == (source % STEN) * parts + source // STEN)


def spread_block(lat):
    parts = lat // STEN
    target = iota((STEN, lat), 1)
    return onehot(iota((STEN, lat), 0) == (target % (STEN // parts)) * parts + target // STEN)


def lane_segment(rows, lat):
    parts = lat // STEN
    return (iota((rows, lat), 1) % STEN) // (STEN // parts)


def move(x, matrix):
    return tuple(dot(part, matrix).astype(BF16) for part in x)


def pack_meta(slots, values):
    stacked = jnp.concatenate(values, axis=0)
    eye = onehot(iota((stacked.shape[0], STEN), 0) == iota((stacked.shape[0], STEN), 1))
    return sum(
        lax.dot_general(part, eye, (((0,), (0,)), ((), ())), preferred_element_type=F32)
        for part in split3(stacked)
    )


def unpack_meta(recv_ref, slots, field):
    owners = recv_ref.shape[0]
    total = owners * slots
    rows = jnp.broadcast_to(recv_ref[:, slots : slots + 1, :], (owners, slots, STEN)).reshape(total, STEN)
    wanted = (iota((total, STEN), 0) & (slots - 1)) + field * slots
    return jnp.sum(jnp.where(iota((total, STEN), 1) == wanted, rows, F32(0.0)), axis=1, keepdims=True)


def head_kernel(
    mask_hbm, klon_hbm, klat_hbm, v_hbm, control_hbm, index_hbm, value_hbm, rinv_hbm, count_hbm, weights_hbm,
    mixed_ref, faces_ref, left_ref, right_ref, sent_ref,
    mask_ref, klon_ref, klat_ref, v_ref, control_ref, index_ref, value_ref, rinv_ref, count_ref, sems,
):
    owners, rows, _ = sent_ref.shape
    slots = rows // 2
    pairs = (
        (mask_hbm, mask_ref), (klon_hbm, klon_ref), (klat_hbm, klat_ref), (v_hbm, v_ref),
        (control_hbm, control_ref), (index_hbm, index_ref), (value_hbm, value_ref), (rinv_hbm, rinv_ref),
        (count_hbm, count_ref), (weights_hbm, sent_ref.at[:, 0:slots, :]),
    )
    copies = [pltpu.make_async_copy(source, target, sems.at[k]) for k, (source, target) in enumerate(pairs)]
    for copy in copies:
        copy.start()
    levels, cols, lat = control_ref.shape
    parts = lat // STEN
    group = WIDE // levels
    halo = PASSES
    edge = halo * levels
    place = deinterleave(lat)
    for copy in copies[:4]:
        copy.wait()
    matrix = mixing_matrix(v_ref[...])
    wet = mask_ref[...].astype(F32)
    east = jnp.where(iota((cols, lat), 0) == cols - 1, F32(1.0), pltpu.roll(wet, cols - 1, 0))
    north = jnp.where(iota((cols, lat), 1) == lat - 1, F32(0.0), pltpu.roll(wet, lat - 1, 1))
    for k, face in enumerate((klon_ref[...] * wet * east, klat_ref[...] * wet * north, wet)):
        held = sum(dot(piece, place) for piece in (split3(face) if k < 2 else (face.astype(BF16),)))
        for q in range(parts):
            faces_ref[k * parts + q] = held[:, q * STEN : (q + 1) * STEN]
    copies[4].wait()
    for g in range(cols // group):
        x = control_ref[:, g * group : (g + 1) * group, :].reshape(WIDE, lat)
        y = product(matrix, move(split(x), place))
        for q in range(parts):
            mixed_ref[q, g * WIDE : (g + 1) * WIDE, :] = y[:, q * STEN : (q + 1) * STEN]
    for out, start in ((left_ref, 0), (right_ref, cols - halo)):
        for q in range(parts):
            out[q * edge : (q + 1) * edge, :] = mixed_ref[q, start * levels : start * levels + edge, :]
        for k in range(2 * parts):
            first = parts * edge + k * halo
            out[first : first + halo, :] = faces_ref[k, start : start + halo, :]
        first = parts * edge + 2 * parts * halo
        for q in range(parts):
            out[first + q : first + q + 1, :] = faces_ref[2 * parts + q, 0:1, :]
        out[first + parts :, :] = jnp.zeros((out.shape[0] - first - parts, STEN), F32)
    for copy in copies[5:]:
        copy.wait()
    valid = jnp.where(iota((slots, owners), 0) < count_ref[...], F32(1.0), F32(0.0))
    meta = pack_meta(slots, [value_ref[...], rinv_ref[...], index_ref[...].astype(F32), valid])
    sent_ref[:, slots:, :] = jnp.broadcast_to(meta[:, None, :], (owners, slots, STEN))


def build_faces(faces_ref, from_left, from_right, lon_ref, lat_ref, levels):
    halo = PASSES
    cols = faces_ref.shape[1]
    parts = faces_ref.shape[0] // 3
    first = parts * halo * levels
    shape = (8, STEN)

    def far(source, k, c):
        at = first + k * halo + c
        return source[at : at + 1, :]

    for c in range(cols + 2 * halo):
        rows = slice(8 * c, 8 * c + 8)
        for q in range(parts):
            if c < halo:
                lon_row, lat_row = far(from_left, q, c), far(from_left, parts + q, c)
                if c == halo - 1:
                    lon_row = lon_row * faces_ref[2 * parts + q, 0:1, :]
            elif c < halo + cols:
                own = c - halo
                lon_row = faces_ref[q, own : own + 1, :]
                lat_row = faces_ref[parts + q, own : own + 1, :]
                if own == cols - 1:
                    at = first + 2 * parts * halo + q
                    lon_row = lon_row * from_right[at : at + 1, :]
            else:
                own = c - halo - cols
                lon_row, lat_row = far(from_right, q, own), far(from_right, parts + q, own)
            lon_ref[q, rows, :] = jnp.broadcast_to(lon_row, shape)
            lat_ref[q, rows, :] = jnp.broadcast_to(lat_row, shape)
            if q == parts - 1:
                lat_ref[parts, rows, :] = jnp.broadcast_to(pltpu.roll(lat_row, 1, 1), shape)


def add_ghosts(ref, first, values):
    count = values[0].shape[0]
    parts = len(values)
    ref[parts, first : first + count, :] = pltpu.roll(values[0], STEN - 1, 1)
    ref[parts + 1, first : first + count, :] = pltpu.roll(values[-1], 1, 1)


def fill(ref, first, values):
    for q, value in enumerate(values):
        ref[q, first : first + value.shape[0], :] = value
    add_ghosts(ref, first, values)


def column_steps(src, dst, lon_ref, lat_ref, levels, low, high, step=0, face=0):
    parts = lon_ref.shape[0]
    halves = range(levels // 8)

    def load(k, c, h):
        return src[k, c * levels + 8 * h : c * levels + 8 * h + 8, :]

    def rate(ref, k, c):
        return ref[k, pl.ds(pl.multiple_of(8 * (c + face), 8), 8), :]

    here = [[load(q, low, h) for q in range(parts)] for h in halves]
    west = [[rate(lon_ref, q, low - 1) * (here[h][q] - load(q, low - 1, h)) for q in range(parts)] for h in halves]
    for c in range(low, high):
        lon = [rate(lon_ref, q, c) for q in range(parts)]
        lat = [rate(lat_ref, q, c) for q in range(parts + 1)]
        for h in halves:
            line = here[h]
            east = [load(q, c + 1, h) for q in range(parts)]
            flux_east = [lon[q] * (east[q] - line[q]) for q in range(parts)]
            ahead = line[1:] + [load(parts, c, h)]
            flux_north = [lat[parts] * (line[0] - load(parts + 1, c, h))]
            flux_north += [lat[q] * (ahead[q] - line[q]) for q in range(parts)]
            out = [
                line[q] + (flux_east[q] - west[h][q]) + (flux_north[q + 1] - flux_north[q])
                for q in range(parts)
            ]
            first = (c + step) * levels + 8 * h
            for q in range(parts):
                dst[q, first : first + 8, :] = out[q]
            add_ghosts(dst, first, out)
            here[h], west[h] = east, flux_east


def diffuse(a_ref, b_ref, lon_ref, lat_ref, levels, before_pass=None):
    width = a_ref.shape[1] // levels

    for first, last in TIERS:

        def pair(turn, carry):
            for k, (src, dst) in enumerate(((a_ref, b_ref), (b_ref, a_ref))):
                if before_pass is not None:
                    before_pass(2 * turn + k, src)
                column_steps(src, dst, lon_ref, lat_ref, levels, first + 1 + k, width - first - 1 - k)
            return carry

        lax.fori_loop(first // 2, last // 2, pair, 0)


def inner_kernel(mixed_ref, faces_ref, inner_ref, strips_ref, a_ref, b_ref, lon_ref, lat_ref):
    parts, own_rows, _ = mixed_ref.shape
    cols = faces_ref.shape[1]
    levels = own_rows // cols
    shape = (8, STEN)
    for c in range(cols):
        rows = slice(8 * c, 8 * c + 8)
        for q in range(parts):
            lat_row = faces_ref[parts + q, c : c + 1, :]
            lon_ref[q, rows, :] = jnp.broadcast_to(faces_ref[q, c : c + 1, :], shape)
            lat_ref[q, rows, :] = jnp.broadcast_to(lat_row, shape)
            if q == parts - 1:
                lat_ref[parts, rows, :] = jnp.broadcast_to(pltpu.roll(lat_row, 1, 1), shape)
    fill(a_ref, 0, [mixed_ref[q] for q in range(parts)])

    def save(turn, src):
        for side, (line, other) in enumerate(((turn, turn + 1), (cols - 1 - turn, cols - 2 - turn))):
            line = pl.ds(pl.multiple_of(line * levels, levels), levels)
            other = pl.ds(pl.multiple_of(other * levels, levels), levels)
            for q in range(parts):
                strips_ref[turn, side, q] = src[q, line, :]
                strips_ref[turn, side, parts + q] = src[q, other, :]

    diffuse(a_ref, b_ref, lon_ref, lat_ref, levels, save)
    for q in range(parts):
        inner_ref[q] = a_ref[q, PASSES * levels : (cols - PASSES) * levels, :]


def block_place(index, cols, parts):
    return (
        lax.shift_right_logical(index, log2(cols * parts)),
        lax.shift_right_logical(index, log2(parts)) & (cols - 1),
        index & (parts - 1),
    )


def weights_kernel(place_ref, recv_ref, std_ref, mask_ref, out_ref, held_ref, pick_ref, std_rows, wet_rows):
    owners, rows, _ = recv_ref.shape
    slots = rows // 2
    total = owners * slots
    levels, cols, lat = std_ref.shape
    parts = lat // STEN
    for s in range(parts):
        part = slice(s * STEN, (s + 1) * STEN)
        wet_rows[s * cols : (s + 1) * cols, :] = mask_ref[:, part].astype(F32)
        for a in range(levels):
            first = (a * parts + s) * cols
            std_rows[first : first + cols, :] = std_ref[a, :, part]

    def pick(o, carry):
        for k in range(slots):
            slot = o * slots + k
            level, column, seg = block_place(place_ref[0, slot], cols, parts)
            value = std_rows[pl.ds((level * parts + seg) * cols + column, 1), :]
            wet = wet_rows[pl.ds(seg * cols + column, 1), :]
            pick_ref[pl.ds(slot, 1), :] = value * wet
        return carry

    lax.fori_loop(0, owners, pick, 0)
    ws = recv_ref[:, 0:slots, :].reshape(total, STEN) * pick_ref[...]
    out_ref[...] = ws
    place = spread_block(lat)
    segs = unpack_meta(recv_ref, slots, 2).astype(jnp.int32) & (parts - 1)
    for j in range(total // STEN):
        part = slice(j * STEN, (j + 1) * STEN)
        seg = segs[part]
        held = sum(dot(piece, place) for piece in split3(ws[part]))
        held = jnp.where(lane_segment(STEN, lat) == seg, held, F32(0.0))
        for q in range(parts):
            held_ref[q, part, :] = held[:, q * STEN : (q + 1) * STEN]


def to_row(column):
    eye = iota((STEN, STEN), 0) == iota((STEN, STEN), 1)
    return jnp.sum(jnp.where(eye, column, F32(0.0)), axis=0, keepdims=True)


def to_column(row):
    eye = iota((STEN, STEN), 0) == iota((STEN, STEN), 1)
    return jnp.sum(jnp.where(eye, row, F32(0.0)), axis=1, keepdims=True)


def edge_kernel(
    place_ref, inner_ref, strips_ref, from_left, from_right, faces_ref, recv_ref, ws_ref, held_ref,
    spread_ref, departure_ref, rows_ref, left_a, left_b, right_a, right_b, lon_ref, lat_ref, pick_ref,
):
    halo = PASSES
    levels = strips_ref.shape[3]
    parts = inner_ref.shape[0]
    owners, rows, _ = recv_ref.shape
    cols = faces_ref.shape[1]
    slots = rows // 2
    total = owners * slots
    edge = halo * levels
    build_faces(faces_ref, from_left, from_right, lon_ref, lat_ref, levels)
    fill(left_a, 0, [from_left[q * edge : (q + 1) * edge, :] for q in range(parts)])
    fill(right_a, 2 * levels, [from_right[q * edge : (q + 1) * edge, :] for q in range(parts)])

    def pair(turn, carry):
        for k, (left, left_to, right, right_to) in enumerate(
            ((left_a, left_b, right_a, right_b), (left_b, left_a, right_b, right_a))
        ):
            now = 2 * turn + k
            for side, ref, line, other in ((0, left, halo, halo + 1), (1, right, 1, 0)):
                fill(ref, line * levels, [strips_ref[now, side, q] for q in range(parts)])
                for q in range(parts):
                    ref[q, other * levels : (other + 1) * levels, :] = strips_ref[now, side, parts + q]
            column_steps(left, left_to, lon_ref, lat_ref, levels, 1, halo + 1, -1, now)
            column_steps(right, right_to, lon_ref, lat_ref, levels, 1, halo + 1, 1, halo + cols - 2 - now)
        return carry

    lax.fori_loop(0, PASSES // 2, pair, 0)
    for q in range(parts):
        rows_ref[q, 0:edge, :] = left_a[q, 0:edge, :]
        rows_ref[q, edge : cols * levels - edge, :] = inner_ref[q]
        rows_ref[q, cols * levels - edge :, :] = right_a[q, 2 * levels : 2 * levels + edge, :]

    def pick(o, carry):
        for k in range(slots):
            slot = o * slots + k
            row = place_ref[1, slot]
            for q in range(parts):
                pick_ref[q, pl.ds(slot, 1), :] = rows_ref[q, pl.ds(row, 1), :]
        return carry

    lax.fori_loop(0, owners, pick, 0)
    value, rinv, index, valid = (unpack_meta(recv_ref, slots, field) for field in range(4))
    evolved = sum(pick_ref[q] * held_ref[q] for q in range(parts))
    evolved = jnp.sum(evolved, axis=1, keepdims=True)
    departure = jnp.where(valid > 0.5, evolved - value, F32(0.0))
    scaled = rinv * departure
    spread_ref[0:total, :] = scaled * ws_ref[...]
    spread_ref[total:, :] = jnp.zeros((spread_ref.shape[0] - total, STEN), F32)
    for j in range(total // STEN):
        part = slice(j * STEN, (j + 1) * STEN)
        spread_ref[total + j : total + j + 1, :] = to_row(index[part])
    lanes = jnp.where(iota((total, STEN), 1) == (iota((total, STEN), 0) & (slots - 1)), departure, F32(0.0))
    departure_ref[...] = jnp.sum(lanes.reshape(owners, slots, STEN), axis=1)


def second_kernel(
    v_ref, control_ref, own_ref, left_ref, right_ref, faces_ref, from_left, from_right,
    out_ref, a_ref, b_ref, lon_ref, lat_ref,
):
    halo = PASSES
    levels, cols, lat = control_ref.shape
    parts = lat // STEN
    edge = halo * levels
    total = own_ref.shape[0] // STEN * STEN
    build_faces(faces_ref, from_left, from_right, lon_ref, lat_ref, levels)
    place = spread_block(lat)

    def scatter(source, first, count, step, target):
        pieces = []
        keys = []
        for j in range(total // STEN):
            index = source[total + j : total + j + 1, :].astype(jnp.int32)
            level, column, seg = block_place(index, cols, parts)
            keys.append((column - first) * levels + level)
            keep = lane_segment(STEN, lat) == to_column(seg.astype(F32)).astype(jnp.int32)
            held = [dot(piece, place) for piece in split(source[j * STEN : (j + 1) * STEN, :])]
            held = [jnp.where(keep, piece, F32(0.0)).astype(BF16) for piece in held]
            pieces.append(jnp.concatenate(held, axis=1))
        for c in range(0, count, step):
            rows = step * levels
            sums = jnp.zeros((rows, 2 * lat), F32)
            for key, piece in zip(keys, pieces):
                sums = sums + dot(onehot(iota((rows, STEN), 0) + c * levels == key), piece)
            sums = sums[:, :lat] + sums[:, lat:]
            fill(a_ref, (target + c) * levels, [sums[:, q * STEN : (q + 1) * STEN] for q in range(parts)])

    scatter(own_ref, 0, cols, 8, halo)
    scatter(left_ref, cols - halo, halo, halo // 2, 0)
    scatter(right_ref, 0, halo, halo // 2, halo + cols)
    diffuse(a_ref, b_ref, lon_ref, lat_ref, levels)
    matrix = mixing_matrix_back(v_ref[...])
    back = interleave(lat)
    group = WIDE // levels
    for g in range(cols // group):
        part = slice(g * group, (g + 1) * group)
        rows = slice(edge + g * WIDE, edge + (g + 1) * WIDE)
        x = jnp.concatenate([a_ref[q, rows, :] for q in range(parts)], axis=1)
        y = product(matrix, move(split(x), back)).reshape(levels, group, lat)
        out_ref[:, part, :] = control_ref[:, part, :] + y


def call(kernel, out_shape, specs, scratch, flops, moved, limit=VMEM_LIMIT):
    return pl.pallas_call(
        kernel,
        out_shape=out_shape,
        in_specs=specs,
        out_specs=jax.tree.map(lambda _: VMEM_SPEC, out_shape),
        scratch_shapes=list(scratch),
        cost_estimate=pl.CostEstimate(flops=flops, bytes_accessed=moved, transcendentals=0),
        compiler_params=pltpu.CompilerParams(vmem_limit_bytes=limit),
    )


def shape(*dims):
    return jax.ShapeDtypeStruct(dims, F32)


def local(
    control, std_field, kappa_lon, kappa_lat, sea_mask, vertical,
    block_index, weights, obs_value, obs_rinv, obs_count,
):
    levels, cols, lat = control.shape
    parts = lat // STEN
    owners, slots = block_index.shape[1:]
    total = owners * slots
    halo = PASSES
    width = cols + 2 * halo
    cells = width * levels * lat
    count = lax.axis_size("lon")
    to_right = [(i, (i + 1) % count) for i in range(count)]
    to_left = [((i + 1) % count, i) for i in range(count)]

    message = parts * halo * (levels + 2) + parts
    message = -(-message // 8) * 8
    small = pltpu.VMEM((slots, owners), F32)
    plane = pltpu.VMEM((cols, lat), F32)
    mixed, faces, edge_left, edge_right, sent = call(
        head_kernel,
        (
            shape(parts, cols * levels, STEN), shape(3 * parts, cols, STEN),
            shape(message, STEN), shape(message, STEN), shape(owners, 2 * slots, STEN),
        ),
        [pl.BlockSpec(memory_space=pltpu.HBM)] * 10,
        [
            pltpu.VMEM((cols, lat), jnp.int32), plane, plane, pltpu.VMEM((levels, levels), F32),
            pltpu.VMEM((levels, cols, lat), F32), pltpu.VMEM((slots, owners), jnp.int32), small, small,
            pltpu.VMEM((1, owners), jnp.int32), pltpu.SemaphoreType.DMA((10,)),
        ],
        12 * cells * lat, 8 * 4 * cells, WHOLE_VMEM,
    )(
        sea_mask, kappa_lon, kappa_lat, vertical, control,
        block_index[0].T, obs_value[0].T, obs_rinv[0].T, obs_count, weights[0],
    )
    from_left = lax.ppermute(edge_right, "lon", to_right)
    from_right = lax.ppermute(edge_left, "lon", to_left)

    recv = lax.all_to_all(sent, "lon", split_axis=0, concat_axis=0, tiled=True)
    index = recv[:, slots, 2 * slots : 3 * slots].reshape(total).astype(jnp.int32)
    level, column, _ = block_place(index, cols, parts)
    places = jnp.stack([index, column * levels + level])
    ws, held = call(
        weights_kernel,
        (shape(total, STEN), shape(parts, total, STEN)),
        [SMEM_SPEC] + [VMEM_SPEC] * 3,
        [
            pltpu.VMEM((total, STEN), F32), pltpu.VMEM((levels * cols * parts, STEN), F32),
            pltpu.VMEM((cols * parts, STEN), F32),
        ],
        6 * total * STEN * lat, 4 * 4 * cells,
    )(places, recv, std_field, sea_mask)

    field = pltpu.VMEM((parts + 2, width * levels, STEN), F32)
    faces_held = [pltpu.VMEM((parts, width * 8, STEN), F32), pltpu.VMEM((parts + 1, width * 8, STEN), F32)]
    extra = -(-total // (8 * STEN)) * 8
    inside = pltpu.VMEM((parts + 2, cols * levels, STEN), F32)
    wedge = pltpu.VMEM((parts + 2, (halo + 2) * levels, STEN), F32)
    inner, strips = call(
        inner_kernel,
        (shape(parts, (cols - 2 * halo) * levels, STEN), shape(PASSES, 2, 2 * parts, levels, STEN)),
        [VMEM_SPEC] * 2,
        [
            inside, inside,
            pltpu.VMEM((parts, cols * 8, STEN), F32), pltpu.VMEM((parts + 1, cols * 8, STEN), F32),
        ],
        5 * PASSES * cells, PASSES * 4 * cells,
    )(mixed, faces)
    spread, departure = call(
        edge_kernel,
        (shape(total + extra, STEN), shape(owners, STEN)),
        [SMEM_SPEC] + [VMEM_SPEC] * 8,
        [
            pltpu.VMEM((parts, cols * levels, STEN), F32), wedge, wedge, wedge, wedge, *faces_held,
            pltpu.VMEM((parts, total, STEN), F32),
        ],
        5 * PASSES * cells, PASSES * 4 * cells,
    )(places, inner, strips, from_left, from_right, faces, recv, ws, held)

    spread_left = lax.ppermute(spread, "lon", to_right)
    spread_right = lax.ppermute(spread, "lon", to_left)
    mine = lax.all_to_all(departure[:, None, :], "lon", split_axis=0, concat_axis=0, tiled=True)

    gradient = call(
        second_kernel, shape(levels, cols, lat), [VMEM_SPEC] * 8, [field, field, *faces_held],
        10 * PASSES * cells, 2 * PASSES * 4 * cells,
    )(vertical, control, spread, spread_left, spread_right, faces, from_left, from_right)
    gradient, mine = lax.optimization_barrier((gradient, mine))
    return gradient, mine[:, 0, :slots][None]


def solution(mesh):
    in_specs = (
        P("grp", "lon", None),
        P(None, "lon", None),
        P("lon", None),
        P("lon", None),
        P("lon", None),
        P(),
        P(("grp", "lon"), None, None),
        P(("grp", "lon"), None, None, None),
        P(("grp", "lon"), None, None),
        P(("grp", "lon"), None, None),
        P(("grp", "lon"), None),
    )
    out_specs = (P("grp", "lon", None), P(("grp", "lon"), None, None))
    return jax.shard_map(local, mesh=mesh, in_specs=in_specs, out_specs=out_specs, check_vma=False)
```

```python
import jax
import jax.numpy as jnp
from jax import lax
from jax.experimental import pallas as pl
from jax.experimental.pallas import tpu as pltpu
from jax.sharding import PartitionSpec as P

STEN = 128
PASSES = 10
WIDE = 256
F32 = jnp.float32
BF16 = jnp.bfloat16
WHOLE_VMEM = 60 * 1024 * 1024
TIERS = tuple((k, k + 2) for k in range(0, PASSES, 2))
VMEM_LIMIT = 24 * 1024 * 1024

VMEM_SPEC = pl.BlockSpec(memory_space=pltpu.VMEM)
SMEM_SPEC = pl.BlockSpec(memory_space=pltpu.SMEM)


def split(x):
    high = x.astype(BF16)
    return high, (x - high.astype(F32)).astype(BF16)


def split3(x):
    high = x.astype(BF16)
    rest = x - high.astype(F32)
    middle = rest.astype(BF16)
    return high, middle, (rest - middle.astype(F32)).astype(BF16)


def dot(a, b):
    return jnp.dot(a, b, preferred_element_type=F32)


def log2(n):
    assert n & (n - 1) == 0
    return n.bit_length() - 1


def iota(shape, dim):
    return lax.broadcasted_iota(jnp.int32, shape, dim)


def onehot(condition):
    return jnp.where(condition, F32(1.0), F32(0.0)).astype(BF16)


def product(left, right):
    (lh, ll), (rh, rl) = left, right
    return dot(lh, rh) + (dot(lh, rl) + dot(ll, rh))


def mixing_matrix(vertical):
    levels = vertical.shape[0]
    group = WIDE // levels
    expand = onehot(iota((levels, WIDE), 1) // group == iota((levels, WIDE), 0))
    keep = iota((WIDE, WIDE), 0) // levels == iota((WIDE, WIDE), 1) % group
    out = []
    for part in split(vertical):
        rows = dot(part, expand)
        tiled = jnp.concatenate([rows] * group, axis=0)
        out.append(jnp.where(keep, tiled, F32(0.0)).astype(BF16))
    return tuple(out)


def mixing_matrix_back(vertical):
    levels = vertical.shape[0]
    group = WIDE // levels
    spread = onehot(iota((levels, WIDE), 1) % levels == iota((levels, WIDE), 0))
    repeat = onehot(iota((WIDE, levels), 0) // group == iota((WIDE, levels), 1))
    keep = iota((WIDE, WIDE), 0) % group == iota((WIDE, WIDE), 1) // levels
    out = []
    for part in split(vertical):
        rows = lax.dot_general(part, spread, (((0,), (0,)), ((), ())), preferred_element_type=F32)
        rows = rows.astype(BF16)
        out.append(jnp.where(keep, dot(repeat, rows), F32(0.0)).astype(BF16))
    return tuple(out)


def deinterleave(lat):
    parts = lat // STEN
    target = iota((lat, lat), 1)
    return onehot(iota((lat, lat), 0) == (target % STEN) * parts + target // STEN)


def interleave(lat):
    parts = lat // STEN
    source = iota((lat, lat), 0)
    return onehot(iota((lat, lat), 1) == (source % STEN) * parts + source // STEN)


def spread_block(lat):
    parts = lat // STEN
    target = iota((STEN, lat), 1)
    return onehot(iota((STEN, lat), 0) == (target % (STEN // parts)) * parts + target // STEN)


def lane_segment(rows, lat):
    parts = lat // STEN
    return (iota((rows, lat), 1) % STEN) // (STEN // parts)


def move(x, matrix):
    return tuple(dot(part, matrix).astype(BF16) for part in x)


def pack_meta(slots, values):
    stacked = jnp.concatenate(values, axis=0)
    eye = onehot(iota((stacked.shape[0], STEN), 0) == iota((stacked.shape[0], STEN), 1))
    return sum(
        lax.dot_general(part, eye, (((0,), (0,)), ((), ())), preferred_element_type=F32)
        for part in split3(stacked)
    )


def unpack_meta(recv_ref, slots, field):
    owners = recv_ref.shape[0]
    total = owners * slots
    rows = jnp.broadcast_to(recv_ref[:, slots : slots + 1, :], (owners, slots, STEN)).reshape(total, STEN)
    wanted = (iota((total, STEN), 0) & (slots - 1)) + field * slots
    return jnp.sum(jnp.where(iota((total, STEN), 1) == wanted, rows, F32(0.0)), axis=1, keepdims=True)


def head_kernel(
    mask_hbm, klon_hbm, klat_hbm, v_hbm, control_hbm, index_hbm, value_hbm, rinv_hbm, count_hbm, weights_hbm,
    mixed_ref, faces_ref, left_ref, right_ref, sent_ref,
    mask_ref, klon_ref, klat_ref, v_ref, control_ref, index_ref, value_ref, rinv_ref, count_ref, sems,
):
    owners, rows, _ = sent_ref.shape
    slots = rows // 2
    pairs = (
        (mask_hbm, mask_ref), (klon_hbm, klon_ref), (klat_hbm, klat_ref), (v_hbm, v_ref),
        (control_hbm, control_ref), (index_hbm, index_ref), (value_hbm, value_ref), (rinv_hbm, rinv_ref),
        (count_hbm, count_ref), (weights_hbm, sent_ref.at[:, 0:slots, :]),
    )
    copies = [pltpu.make_async_copy(source, target, sems.at[k]) for k, (source, target) in enumerate(pairs)]
    for copy in copies:
        copy.start()
    levels, cols, lat = control_ref.shape
    parts = lat // STEN
    group = WIDE // levels
    halo = PASSES
    edge = halo * levels
    place = deinterleave(lat)
    for copy in copies[:4]:
        copy.wait()
    matrix = mixing_matrix(v_ref[...])
    wet = mask_ref[...].astype(F32)
    east = jnp.where(iota((cols, lat), 0) == cols - 1, F32(1.0), pltpu.roll(wet, cols - 1, 0))
    north = jnp.where(iota((cols, lat), 1) == lat - 1, F32(0.0), pltpu.roll(wet, lat - 1, 1))
    for k, face in enumerate((klon_ref[...] * wet * east, klat_ref[...] * wet * north, wet)):
        held = sum(dot(piece, place) for piece in (split3(face) if k < 2 else (face.astype(BF16),)))
        for q in range(parts):
            faces_ref[k * parts + q] = held[:, q * STEN : (q + 1) * STEN]
    copies[4].wait()
    for g in range(cols // group):
        x = control_ref[:, g * group : (g + 1) * group, :].reshape(WIDE, lat)
        y = product(matrix, move(split(x), place))
        for q in range(parts):
            mixed_ref[q, g * WIDE : (g + 1) * WIDE, :] = y[:, q * STEN : (q + 1) * STEN]
    for out, start in ((left_ref, 0), (right_ref, cols - halo)):
        for q in range(parts):
            out[q * edge : (q + 1) * edge, :] = mixed_ref[q, start * levels : start * levels + edge, :]
        for k in range(2 * parts):
            first = parts * edge + k * halo
            out[first : first + halo, :] = faces_ref[k, start : start + halo, :]
        first = parts * edge + 2 * parts * halo
        for q in range(parts):
            out[first + q : first + q + 1, :] = faces_ref[2 * parts + q, 0:1, :]
        out[first + parts :, :] = jnp.zeros((out.shape[0] - first - parts, STEN), F32)
    for copy in copies[5:]:
        copy.wait()
    valid = jnp.where(iota((slots, owners), 0) < count_ref[...], F32(1.0), F32(0.0))
    meta = pack_meta(slots, [value_ref[...], rinv_ref[...], index_ref[...].astype(F32), valid])
    sent_ref[:, slots:, :] = jnp.broadcast_to(meta[:, None, :], (owners, slots, STEN))


def build_faces(faces_ref, from_left, from_right, lon_ref, lat_ref, levels):
    halo = PASSES
    cols = faces_ref.shape[1]
    parts = faces_ref.shape[0] // 3
    first = parts * halo * levels
    shape = (8, STEN)

    def far(source, k, c):
        at = first + k * halo + c
        return source[at : at + 1, :]

    for c in range(cols + 2 * halo):
        rows = slice(8 * c, 8 * c + 8)
        for q in range(parts):
            if c < halo:
                lon_row, lat_row = far(from_left, q, c), far(from_left, parts + q, c)
                if c == halo - 1:
                    lon_row = lon_row * faces_ref[2 * parts + q, 0:1, :]
            elif c < halo + cols:
                own = c - halo
                lon_row = faces_ref[q, own : own + 1, :]
                lat_row = faces_ref[parts + q, own : own + 1, :]
                if own == cols - 1:
                    at = first + 2 * parts * halo + q
                    lon_row = lon_row * from_right[at : at + 1, :]
            else:
                own = c - halo - cols
                lon_row, lat_row = far(from_right, q, own), far(from_right, parts + q, own)
            lon_ref[q, rows, :] = jnp.broadcast_to(lon_row, shape)
            lat_ref[q, rows, :] = jnp.broadcast_to(lat_row, shape)
            if q == parts - 1:
                lat_ref[parts, rows, :] = jnp.broadcast_to(pltpu.roll(lat_row, 1, 1), shape)


def add_ghosts(ref, first, values):
    count = values[0].shape[0]
    parts = len(values)
    ref[parts, first : first + count, :] = pltpu.roll(values[0], STEN - 1, 1)
    ref[parts + 1, first : first + count, :] = pltpu.roll(values[-1], 1, 1)


def fill(ref, first, values):
    for q, value in enumerate(values):
        ref[q, first : first + value.shape[0], :] = value
    add_ghosts(ref, first, values)


def column_steps(src, dst, lon_ref, lat_ref, levels, low, high, step=0, face=0):
    parts = lon_ref.shape[0]
    halves = range(levels // 8)

    def load(k, c, h):
        return src[k, c * levels + 8 * h : c * levels + 8 * h + 8, :]

    def rate(ref, k, c):
        return ref[k, pl.ds(pl.multiple_of(8 * (c + face), 8), 8), :]

    here = [[load(q, low, h) for q in range(parts)] for h in halves]
    west = [[rate(lon_ref, q, low - 1) * (here[h][q] - load(q, low - 1, h)) for q in range(parts)] for h in halves]
    for c in range(low, high):
        lon = [rate(lon_ref, q, c) for q in range(parts)]
        lat = [rate(lat_ref, q, c) for q in range(parts + 1)]
        for h in halves:
            line = here[h]
            east = [load(q, c + 1, h) for q in range(parts)]
            flux_east = [lon[q] * (east[q] - line[q]) for q in range(parts)]
            ahead = line[1:] + [load(parts, c, h)]
            flux_north = [lat[parts] * (line[0] - load(parts + 1, c, h))]
            flux_north += [lat[q] * (ahead[q] - line[q]) for q in range(parts)]
            out = [
                line[q] + (flux_east[q] - west[h][q]) + (flux_north[q + 1] - flux_north[q])
                for q in range(parts)
            ]
            first = (c + step) * levels + 8 * h
            for q in range(parts):
                dst[q, first : first + 8, :] = out[q]
            add_ghosts(dst, first, out)
            here[h], west[h] = east, flux_east


def diffuse(a_ref, b_ref, lon_ref, lat_ref, levels, before_pass=None):
    width = a_ref.shape[1] // levels

    for first, last in TIERS:

        def pair(turn, carry):
            for k, (src, dst) in enumerate(((a_ref, b_ref), (b_ref, a_ref))):
                if before_pass is not None:
                    before_pass(2 * turn + k, src)
                column_steps(src, dst, lon_ref, lat_ref, levels, first + 1 + k, width - first - 1 - k)
            return carry

        lax.fori_loop(first // 2, last // 2, pair, 0)


def inner_kernel(mixed_ref, faces_ref, inner_ref, strips_ref, a_ref, b_ref, lon_ref, lat_ref):
    parts, own_rows, _ = mixed_ref.shape
    cols = faces_ref.shape[1]
    levels = own_rows // cols
    shape = (8, STEN)
    for c in range(cols):
        rows = slice(8 * c, 8 * c + 8)
        for q in range(parts):
            lat_row = faces_ref[parts + q, c : c + 1, :]
            lon_ref[q, rows, :] = jnp.broadcast_to(faces_ref[q, c : c + 1, :], shape)
            lat_ref[q, rows, :] = jnp.broadcast_to(lat_row, shape)
            if q == parts - 1:
                lat_ref[parts, rows, :] = jnp.broadcast_to(pltpu.roll(lat_row, 1, 1), shape)
    fill(a_ref, 0, [mixed_ref[q] for q in range(parts)])

    def save(turn, src):
        for side, (line, other) in enumerate(((turn, turn + 1), (cols - 1 - turn, cols - 2 - turn))):
            line = pl.ds(pl.multiple_of(line * levels, levels), levels)
            other = pl.ds(pl.multiple_of(other * levels, levels), levels)
            for q in range(parts):
                strips_ref[turn, side, q] = src[q, line, :]
                strips_ref[turn, side, parts + q] = src[q, other, :]

    diffuse(a_ref, b_ref, lon_ref, lat_ref, levels, save)
    for q in range(parts):
        inner_ref[q] = a_ref[q, PASSES * levels : (cols - PASSES) * levels, :]


def block_place(index, cols, parts):
    return (
        lax.shift_right_logical(index, log2(cols * parts)),
        lax.shift_right_logical(index, log2(parts)) & (cols - 1),
        index & (parts - 1),
    )


def weights_kernel(place_ref, recv_ref, std_ref, mask_ref, out_ref, held_ref, pick_ref, std_rows, wet_rows):
    owners, rows, _ = recv_ref.shape
    slots = rows // 2
    total = owners * slots
    levels, cols, lat = std_ref.shape
    parts = lat // STEN
    for s in range(parts):
        part = slice(s * STEN, (s + 1) * STEN)
        wet_rows[s * cols : (s + 1) * cols, :] = mask_ref[:, part].astype(F32)
        for a in range(levels):
            first = (a * parts + s) * cols
            std_rows[first : first + cols, :] = std_ref[a, :, part]

    def pick(o, carry):
        for k in range(slots):
            slot = o * slots + k
            level, column, seg = block_place(place_ref[0, slot], cols, parts)
            value = std_rows[pl.ds((level * parts + seg) * cols + column, 1), :]
            wet = wet_rows[pl.ds(seg * cols + column, 1), :]
            pick_ref[pl.ds(slot, 1), :] = value * wet
        return carry

    lax.fori_loop(0, owners, pick, 0)
    ws = recv_ref[:, 0:slots, :].reshape(total, STEN) * pick_ref[...]
    out_ref[...] = ws
    place = spread_block(lat)
    segs = unpack_meta(recv_ref, slots, 2).astype(jnp.int32) & (parts - 1)
    for j in range(total // STEN):
        part = slice(j * STEN, (j + 1) * STEN)
        seg = segs[part]
        held = sum(dot(piece, place) for piece in split3(ws[part]))
        held = jnp.where(lane_segment(STEN, lat) == seg, held, F32(0.0))
        for q in range(parts):
            held_ref[q, part, :] = held[:, q * STEN : (q + 1) * STEN]


def to_row(column):
    eye = iota((STEN, STEN), 0) == iota((STEN, STEN), 1)
    return jnp.sum(jnp.where(eye, column, F32(0.0)), axis=0, keepdims=True)


def to_column(row):
    eye = iota((STEN, STEN), 0) == iota((STEN, STEN), 1)
    return jnp.sum(jnp.where(eye, row, F32(0.0)), axis=1, keepdims=True)


def edge_kernel(
    place_ref, inner_ref, strips_ref, from_left, from_right, faces_ref, recv_ref, ws_ref, held_ref,
    spread_ref, departure_ref, rows_ref, left_a, left_b, right_a, right_b, lon_ref, lat_ref, pick_ref,
):
    halo = PASSES
    levels = strips_ref.shape[3]
    parts = inner_ref.shape[0]
    owners, rows, _ = recv_ref.shape
    cols = faces_ref.shape[1]
    slots = rows // 2
    total = owners * slots
    edge = halo * levels
    build_faces(faces_ref, from_left, from_right, lon_ref, lat_ref, levels)
    fill(left_a, 0, [from_left[q * edge : (q + 1) * edge, :] for q in range(parts)])
    fill(right_a, 2 * levels, [from_right[q * edge : (q + 1) * edge, :] for q in range(parts)])

    def pair(turn, carry):
        for k, (left, left_to, right, right_to) in enumerate(
            ((left_a, left_b, right_a, right_b), (left_b, left_a, right_b, right_a))
        ):
            now = 2 * turn + k
            for side, ref, line, other in ((0, left, halo, halo + 1), (1, right, 1, 0)):
                fill(ref, line * levels, [strips_ref[now, side, q] for q in range(parts)])
                for q in range(parts):
                    ref[q, other * levels : (other + 1) * levels, :] = strips_ref[now, side, parts + q]
            column_steps(left, left_to, lon_ref, lat_ref, levels, 1, halo + 1, -1, now)
            column_steps(right, right_to, lon_ref, lat_ref, levels, 1, halo + 1, 1, halo + cols - 2 - now)
        return carry

    lax.fori_loop(0, PASSES // 2, pair, 0)
    for q in range(parts):
        rows_ref[q, 0:edge, :] = left_a[q, 0:edge, :]
        rows_ref[q, edge : cols * levels - edge, :] = inner_ref[q]
        rows_ref[q, cols * levels - edge :, :] = right_a[q, 2 * levels : 2 * levels + edge, :]

    def pick(o, carry):
        for k in range(slots):
            slot = o * slots + k
            row = place_ref[1, slot]
            for q in range(parts):
                pick_ref[q, pl.ds(slot, 1), :] = rows_ref[q, pl.ds(row, 1), :]
        return carry

    lax.fori_loop(0, owners, pick, 0)
    value, rinv, index, valid = (unpack_meta(recv_ref, slots, field) for field in range(4))
    evolved = sum(pick_ref[q] * held_ref[q] for q in range(parts))
    evolved = jnp.sum(evolved, axis=1, keepdims=True)
    departure = jnp.where(valid > 0.5, evolved - value, F32(0.0))
    scaled = rinv * departure
    spread_ref[0:total, :] = scaled * ws_ref[...]
    spread_ref[total:, :] = jnp.zeros((spread_ref.shape[0] - total, STEN), F32)
    for j in range(total // STEN):
        part = slice(j * STEN, (j + 1) * STEN)
        spread_ref[total + j : total + j + 1, :] = to_row(index[part])
    lanes = jnp.where(iota((total, STEN), 1) == (iota((total, STEN), 0) & (slots - 1)), departure, F32(0.0))
    departure_ref[...] = jnp.sum(lanes.reshape(owners, slots, STEN), axis=1)


def second_kernel(
    v_ref, control_ref, own_ref, left_ref, right_ref, faces_ref, from_left, from_right,
    out_ref, a_ref, b_ref, lon_ref, lat_ref,
):
    halo = PASSES
    levels, cols, lat = control_ref.shape
    parts = lat // STEN
    edge = halo * levels
    total = own_ref.shape[0] // STEN * STEN
    build_faces(faces_ref, from_left, from_right, lon_ref, lat_ref, levels)
    place = spread_block(lat)

    def scatter(source, first, count, step, target):
        pieces = []
        keys = []
        for j in range(total // STEN):
            index = source[total + j : total + j + 1, :].astype(jnp.int32)
            level, column, seg = block_place(index, cols, parts)
            keys.append((column - first) * levels + level)
            keep = lane_segment(STEN, lat) == to_column(seg.astype(F32)).astype(jnp.int32)
            held = [dot(piece, place) for piece in split(source[j * STEN : (j + 1) * STEN, :])]
            held = [jnp.where(keep, piece, F32(0.0)).astype(BF16) for piece in held]
            pieces.append(jnp.concatenate(held, axis=1))
        for c in range(0, count, step):
            rows = step * levels
            sums = jnp.zeros((rows, 2 * lat), F32)
            for key, piece in zip(keys, pieces):
                sums = sums + dot(onehot(iota((rows, STEN), 0) + c * levels == key), piece)
            sums = sums[:, :lat] + sums[:, lat:]
            fill(a_ref, (target + c) * levels, [sums[:, q * STEN : (q + 1) * STEN] for q in range(parts)])

    scatter(own_ref, 0, cols, 8, halo)
    scatter(left_ref, cols - halo, halo, halo // 2, 0)
    scatter(right_ref, 0, halo, halo // 2, halo + cols)
    diffuse(a_ref, b_ref, lon_ref, lat_ref, levels)
    matrix = mixing_matrix_back(v_ref[...])
    back = interleave(lat)
    group = WIDE // levels
    for g in range(cols // group):
        part = slice(g * group, (g + 1) * group)
        rows = slice(edge + g * WIDE, edge + (g + 1) * WIDE)
        x = jnp.concatenate([a_ref[q, rows, :] for q in range(parts)], axis=1)
        y = product(matrix, move(split(x), back)).reshape(levels, group, lat)
        out_ref[:, part, :] = control_ref[:, part, :] + y


def call(kernel, out_shape, specs, scratch, flops, moved, limit=VMEM_LIMIT):
    return pl.pallas_call(
        kernel,
        out_shape=out_shape,
        in_specs=specs,
        out_specs=jax.tree.map(lambda _: VMEM_SPEC, out_shape),
        scratch_shapes=list(scratch),
        cost_estimate=pl.CostEstimate(flops=flops, bytes_accessed=moved, transcendentals=0),
        compiler_params=pltpu.CompilerParams(vmem_limit_bytes=limit),
    )


def shape(*dims):
    return jax.ShapeDtypeStruct(dims, F32)


def local(
    control, std_field, kappa_lon, kappa_lat, sea_mask, vertical,
    block_index, weights, obs_value, obs_rinv, obs_count,
):
    levels, cols, lat = control.shape
    parts = lat // STEN
    owners, slots = block_index.shape[1:]
    total = owners * slots
    halo = PASSES
    width = cols + 2 * halo
    cells = width * levels * lat
    count = lax.axis_size("lon")
    to_right = [(i, (i + 1) % count) for i in range(count)]
    to_left = [((i + 1) % count, i) for i in range(count)]

    message = parts * halo * (levels + 2) + parts
    message = -(-message // 8) * 8
    small = pltpu.VMEM((slots, owners), F32)
    plane = pltpu.VMEM((cols, lat), F32)
    mixed, faces, edge_left, edge_right, sent = call(
        head_kernel,
        (
            shape(parts, cols * levels, STEN), shape(3 * parts, cols, STEN),
            shape(message, STEN), shape(message, STEN), shape(owners, 2 * slots, STEN),
        ),
        [pl.BlockSpec(memory_space=pltpu.HBM)] * 10,
        [
            pltpu.VMEM((cols, lat), jnp.int32), plane, plane, pltpu.VMEM((levels, levels), F32),
            pltpu.VMEM((levels, cols, lat), F32), pltpu.VMEM((slots, owners), jnp.int32), small, small,
            pltpu.VMEM((1, owners), jnp.int32), pltpu.SemaphoreType.DMA((10,)),
        ],
        12 * cells * lat, 8 * 4 * cells, WHOLE_VMEM,
    )(
        sea_mask, kappa_lon, kappa_lat, vertical, control,
        block_index[0].T, obs_value[0].T, obs_rinv[0].T, obs_count, weights[0],
    )
    from_left = lax.ppermute(edge_right, "lon", to_right)
    from_right = lax.ppermute(edge_left, "lon", to_left)

    recv = lax.all_to_all(sent, "lon", split_axis=0, concat_axis=0, tiled=True)
    index = recv[:, slots, 2 * slots : 3 * slots].reshape(total).astype(jnp.int32)
    level, column, _ = block_place(index, cols, parts)
    places = jnp.stack([index, column * levels + level])
    ws, held = call(
        weights_kernel,
        (shape(total, STEN), shape(parts, total, STEN)),
        [SMEM_SPEC] + [VMEM_SPEC] * 3,
        [
            pltpu.VMEM((total, STEN), F32), pltpu.VMEM((levels * cols * parts, STEN), F32),
            pltpu.VMEM((cols * parts, STEN), F32),
        ],
        6 * total * STEN * lat, 4 * 4 * cells,
    )(places, recv, std_field, sea_mask)

    field = pltpu.VMEM((parts + 2, width * levels, STEN), F32)
    faces_held = [pltpu.VMEM((parts, width * 8, STEN), F32), pltpu.VMEM((parts + 1, width * 8, STEN), F32)]
    extra = -(-total // (8 * STEN)) * 8
    inside = pltpu.VMEM((parts + 2, cols * levels, STEN), F32)
    wedge = pltpu.VMEM((parts + 2, (halo + 2) * levels, STEN), F32)
    inner, strips = call(
        inner_kernel,
        (shape(parts, (cols - 2 * halo) * levels, STEN), shape(PASSES, 2, 2 * parts, levels, STEN)),
        [VMEM_SPEC] * 2,
        [
            inside, inside,
            pltpu.VMEM((parts, cols * 8, STEN), F32), pltpu.VMEM((parts + 1, cols * 8, STEN), F32),
        ],
        5 * PASSES * cells, PASSES * 4 * cells,
    )(mixed, faces)
    spread, departure = call(
        edge_kernel,
        (shape(total + extra, STEN), shape(owners, STEN)),
        [SMEM_SPEC] + [VMEM_SPEC] * 8,
        [
            pltpu.VMEM((parts, cols * levels, STEN), F32), wedge, wedge, wedge, wedge, *faces_held,
            pltpu.VMEM((parts, total, STEN), F32),
        ],
        5 * PASSES * cells, PASSES * 4 * cells,
    )(places, inner, strips, from_left, from_right, faces, recv, ws, held)

    spread_left = lax.ppermute(spread, "lon", to_right)
    spread_right = lax.ppermute(spread, "lon", to_left)
    mine = lax.all_to_all(departure[:, None, :], "lon", split_axis=0, concat_axis=0, tiled=True)

    gradient = call(
        second_kernel, shape(levels, cols, lat), [VMEM_SPEC] * 8, [field, field, *faces_held],
        10 * PASSES * cells, 2 * PASSES * 4 * cells,
    )(vertical, control, spread, spread_left, spread_right, faces, from_left, from_right)
    gradient, mine = lax.optimization_barrier((gradient, mine))
    return gradient, mine[:, 0, :slots][None]


def solution(mesh):
    in_specs = (
        P("grp", "lon", None),
        P(None, "lon", None),
        P("lon", None),
        P("lon", None),
        P("lon", None),
        P(),
        P(("grp", "lon"), None, None),
        P(("grp", "lon"), None, None, None),
        P(("grp", "lon"), None, None),
        P(("grp", "lon"), None, None),
        P(("grp", "lon"), None),
    )
    out_specs = (P("grp", "lon", None), P(("grp", "lon"), None, None))
    return jax.shard_map(local, mesh=mesh, in_specs=in_specs, out_specs=out_specs, check_vma=False)
```
